128 devices in a mesh: traj: 8 (over x, core), tm: 16 (over y, z).
Axes of the slice: x: 4, y: 4, z: 4, core: 2. Of those that a mesh axis runs over, the one named last changes fastest.
Arguments:
- frames: bfloat16 [8, 4096, 4096], P('traj', 'tm'), may hold values from -60 to 60
- w_in: bfloat16 [4096, 512], replicated, may hold values from -0.0625 to 0.0625
- b_in: float32 [512], replicated, may hold values from -3 to 3
- w_conv: bfloat16 [3, 1024, 512], replicated, may hold values from -0.5 to 0.5
- b_conv: float32 [3, 512], replicated, may hold values from -3 to 3
Outputs:
- score: float32 [], replicated
- grad_w_in: float32 [4096, 512], replicated
- grad_b_in: float32 [512], replicated
- grad_w_conv: float32 [3, 1024, 512], replicated
- grad_b_conv: float32 [3, 512], replicated
The draws below stay inside these ranges and needn't reach their ends.
All inputs are finite; a program needn't handle non-finite values.
Results may differ from the reference program's by a relative error of at most 0.012.
Values may be sent and summed in bfloat16 or wider, within the bound.
No kernel may reach another device: no remote copies, remote signals or barrier semaphores. Data moves between devices by JAX's collectives and lax.ppermute only.
A program may use at most 128 MiB of HBM per device.

```python
import math
import jax
import jax.numpy as jnp
from jax import lax

F = 4096
C = 512
NL = 3
NS_IT = 2
LAG = 16
TRAJS = 8
LENGTH = 4096


def draw_frames(key, part):
    key = jax.random.fold_in(key, 7)
    key_base, key_rows, key_cols = jax.random.split(key, 3)
    time_pos = jnp.arange(LENGTH, dtype=jnp.float32) / (LENGTH - 1)
    row_gain = (1.0 + 2.0 * time_pos)[None, :, None] * jnp.exp(jax.random.uniform(key_rows, (TRAJS, LENGTH, 1), jnp.float32, -0.35, 0.35))
    col_gain = jnp.exp(jax.random.uniform(key_cols, (F,), jnp.float32, math.log(0.5), math.log(2.0)))
    base_vals = jnp.clip(jax.random.normal(key_base, (TRAJS, LENGTH, F), jnp.float32), -5.0, 5.0)
    return (base_vals * row_gain * col_gain).astype(jnp.bfloat16)


def centred(stream_key, extent, deviation, limit, held_as=jnp.bfloat16):
    return jnp.clip(deviation * jax.random.normal(stream_key, extent, jnp.float32), -limit, limit).astype(held_as)


def setup_inputs(seed: int = 0) -> dict:
    key_of = jax.random.split(jax.random.key(seed), 6)
    frames = draw_frames(jax.random.fold_in(key_of[5], 71), 0)
    w_in = centred(key_of[1], (F, C), (0.3 * F ** -0.5), 0.0625)
    b_in = centred(key_of[2], (C,), 0.5, 3.0, jnp.float32)
    w_conv = centred(key_of[3], (NL, 2 * C, C), ((2 * C) ** -0.5), 0.5)
    b_conv = centred(key_of[4], (NL, C), 0.5, 3.0, jnp.float32)
    return {"frames": frames, "w_in": w_in, "b_in": b_in, "w_conv": w_conv, "b_conv": b_conv}


RIDGE = 0.0001

def matmul_hi(first_mat, second_mat):
    return jnp.dot(first_mat, second_mat, precision=lax.Precision.HIGHEST, preferred_element_type=jnp.float32)

def gram_hi(first_mat, second_mat):
    return lax.dot_general(first_mat, second_mat, (((0,), (0,)), ((), ())), precision=lax.Precision.HIGHEST, preferred_element_type=jnp.float32)

def inv_sqrt(matrix):
    unit = jnp.eye(matrix.shape[0], dtype=jnp.float32)
    shifted = matrix + RIDGE * unit
    norm_scale = jnp.sqrt(jnp.sum(shifted * shifted))
    approx = shifted / norm_scale
    inverse = unit
    for sweep in range(NS_IT):
        mixing = 1.5 * unit - 0.5 * matmul_hi(inverse, approx)
        approx = matmul_hi(approx, mixing)
        inverse = matmul_hi(mixing, inverse)
    return inverse / jnp.sqrt(norm_scale)

def vamp_score(cov_early, cov_cross, cov_later):
    koopman = matmul_hi(matmul_hi(inv_sqrt(cov_early), cov_cross), inv_sqrt(cov_later))
    return 1.0 + jnp.sum(koopman * koopman)

def reference(frames, w_in, b_in, w_conv, b_conv):
    traj_count, length, feature_dim = frames.shape
    channels = w_in.shape[1]
    flat_frames = frames.reshape(traj_count * length, feature_dim)
    squash0 = jnp.tanh(jnp.dot(flat_frames, w_in, preferred_element_type=jnp.float32) + b_in)
    hidden = squash0.astype(jnp.bfloat16).reshape(traj_count, length, channels)
    stored = []
    for layer_idx in range(NL):
        dilation = 2 ** layer_idx
        history = jnp.concatenate([jnp.zeros((traj_count, dilation, channels), jnp.bfloat16), hidden[:, :length - dilation]], axis=1)
        joined = jnp.concatenate([hidden, history], axis=2).reshape(traj_count * length, 2 * channels)
        squashed = jnp.tanh(jnp.dot(joined, w_conv[layer_idx], preferred_element_type=jnp.float32) + b_conv[layer_idx])
        stored.append((joined, squashed))
        hidden = (hidden.astype(jnp.float32) + squashed.reshape(traj_count, length, channels)).astype(jnp.bfloat16)
    outputs = hidden.astype(jnp.float32)
    early_rows = outputs[:, :length - LAG].reshape(-1, channels)
    later_rows = outputs[:, LAG:].reshape(-1, channels)
    pair_count = traj_count * (length - LAG)
    centred_early = early_rows - lax.optimization_barrier(jnp.sum(early_rows, axis=0)) / pair_count
    centred_later = later_rows - lax.optimization_barrier(jnp.sum(later_rows, axis=0)) / pair_count
    cov_early = gram_hi(centred_early, centred_early) / pair_count
    cov_cross = gram_hi(centred_early, centred_later) / pair_count
    cov_later = gram_hi(centred_later, centred_later) / pair_count
    score, pullback = jax.vjp(vamp_score, cov_early, cov_cross, cov_later)
    grad_early, grad_cross, grad_later = pullback(jnp.ones_like(score))
    dearly = (matmul_hi(centred_early, grad_early + grad_early.T) + matmul_hi(centred_later, grad_cross.T)) / pair_count
    dlater = (matmul_hi(centred_early, grad_cross) + matmul_hi(centred_later, grad_later + grad_later.T)) / pair_count
    hidden_grad = jnp.zeros((traj_count, length, channels), jnp.float32)
    hidden_grad = hidden_grad.at[:, :length - LAG].add(dearly.reshape(traj_count, length - LAG, channels))
    hidden_grad = hidden_grad.at[:, LAG:].add(dlater.reshape(traj_count, length - LAG, channels))
    weight_grads = []
    bias_grads = []
    for layer_idx in reversed(range(NL)):
        dilation = 2 ** layer_idx
        joined, squashed = stored[layer_idx]
        pre_grad = (hidden_grad.reshape(-1, channels) * (1.0 - squashed * squashed)).astype(jnp.bfloat16)
        weight_grads.insert(0, lax.dot_general(joined, pre_grad, (((0,), (0,)), ((), ())), preferred_element_type=jnp.float32))
        bias_grads.insert(0, lax.optimization_barrier(jnp.sum(pre_grad.astype(jnp.float32), axis=0)))
        input_grad = lax.dot_general(pre_grad, w_conv[layer_idx], (((1,), (1,)), ((), ())), preferred_element_type=jnp.float32)
        input_grad = input_grad.reshape(traj_count, length, 2 * channels)
        delayed = jnp.concatenate([input_grad[:, dilation:, channels:], jnp.zeros((traj_count, dilation, channels), jnp.float32)], axis=1)
        hidden_grad = hidden_grad + input_grad[:, :, :channels] + delayed
    pre_grad0 = (hidden_grad.reshape(-1, channels) * (1.0 - squash0 * squash0)).astype(jnp.bfloat16)
    grad_w_in = lax.dot_general(flat_frames, pre_grad0, (((0,), (0,)), ((), ())), preferred_element_type=jnp.float32)
    grad_b_in = lax.optimization_barrier(jnp.sum(pre_grad0.astype(jnp.float32), axis=0))
    return (score, grad_w_in, grad_b_in, jnp.stack(weight_grads), jnp.stack(bias_grads))
```

```python
import jax
import jax.numpy as jnp
from jax import lax
from jax.sharding import Mesh, PartitionSpec as P

NL = 3
LAG = 16
RIDGE = 0.0001
HALO = 24
BF = jnp.bfloat16
F32 = jnp.float32
PEERS = ("x", "tm")
HI = lax.Precision.HIGHEST


def mm(a, b, precision=HI):
    return jnp.dot(a, b, precision=precision, preferred_element_type=F32)


def tdot(a, b, precision=None):
    return lax.dot_general(
        a, b, (((0,), (0,)), ((), ())), precision=precision, preferred_element_type=F32
    )


def dott(a, b):
    return lax.dot_general(a, b, (((1,), (1,)), ((), ())), preferred_element_type=F32)


def swap_core(value):
    return lax.ppermute(value, "c", [(0, 1), (1, 0)])


def shift_segment(value, steps):
    count = lax.axis_size("tm")
    first, last = max(0, -steps), min(count, count - steps)
    return lax.ppermute(value, "tm", [(i, i + steps) for i in range(first, last)])


def exchange(value):
    return lax.all_to_all(value, PEERS, 0, 0, tiled=True)


def spread(chunk, peers):
    full = jnp.broadcast_to(chunk[None], (peers,) + chunk.shape)
    return exchange(full)


C0, C1, C2, C3, C4 = 2.25, -2.4375, 1.6875, -0.5625, 0.0625


def inv_sqrt(cov, unit):
    shifted = cov + RIDGE * unit
    scale = jnp.sqrt(jnp.sum(shifted * shifted))
    a = shifted / scale
    a2 = mm(a, a)
    poly = C0 * unit + C1 * a + C2 * a2 + mm(a2, C3 * a + C4 * a2)
    root = lax.rsqrt(scale)
    return a, a2, poly, scale, poly * root


def inv_sqrt_grad(a, a2, poly, scale, grad):
    root = lax.rsqrt(scale)
    dscale = -0.5 * jnp.sum(grad * poly) * root / scale
    g = grad * root
    y = mm(g, a)
    x = mm(a2, g)
    xs = x + x.T
    h = C2 * g + (0.5 * C3) * (y + y.T) + C4 * xs
    z = mm(a, h)
    da = C1 * g + (0.5 * C3) * xs + z + z.T
    dscale = dscale - jnp.sum(da * a) / scale
    return da / scale + dscale * a


def score_and_grads(cov_e, cov_c, cov_l):
    unit = jnp.eye(cov_e.shape[0], dtype=F32)
    se = inv_sqrt(cov_e, unit)
    sl = inv_sqrt(cov_l, unit)
    re, rl = se[4], sl[4]
    u = mm(re, cov_c)
    v = mm(cov_c, rl)
    k = mm(u, rl)
    score = 1.0 + jnp.sum(k * k)
    k2 = 2.0 * k
    gc = mm(mm(re, k2), rl)
    gre = dott_hi(k2, v)
    grl = tdot(u, k2, HI)
    ge = inv_sqrt_grad(*se[:4], gre + gre.T)
    gl = inv_sqrt_grad(*sl[:4], grl + grl.T)
    return score, ge, gc, gl


def dott_hi(a, b):
    return lax.dot_general(
        a, b, (((1,), (1,)), ((), ())), precision=HI, preferred_element_type=F32
    )


def per_device(frames, w_in, b_in, w_conv, b_conv):
    frames = frames[0]
    rows, features = frames.shape
    ch = w_in.shape[1]
    core = lax.axis_index("c")
    segment = lax.axis_index("tm")
    segments = lax.axis_size("tm")
    peers = lax.axis_size("x") * segments
    length = rows * segments
    pair_count = 2 * lax.axis_size("x") * (length - LAG)

    squash0 = jnp.tanh(jnp.dot(frames, w_in, preferred_element_type=F32) + b_in)
    own = squash0.astype(BF)
    before = shift_segment(own[rows - HALO :], 1)
    after = shift_segment(own[:HALO], -1)
    hidden = jnp.concatenate([before, own, after], axis=0)
    ext = rows + 2 * HALO
    time = segment * rows - HALO + jnp.arange(ext)[:, None]
    started = time >= 0
    joined_all, squash_all = [], []
    for layer in range(NL):
        step = 2**layer
        hist = jnp.concatenate([jnp.zeros((step, ch), BF), hidden[: ext - step]], axis=0)
        joined = jnp.concatenate([hidden, hist], axis=1)
        squash = jnp.tanh(jnp.dot(joined, w_conv[layer], preferred_element_type=F32) + b_conv[layer])
        joined_all.append(joined)
        squash_all.append(squash)
        hidden = jnp.where(started, (hidden.astype(F32) + squash).astype(BF), 0)
    out = hidden.astype(F32)

    ids = jnp.arange(rows)[:, None]
    is_last = segment == segments - 1
    pair = jnp.where(jnp.logical_and(is_last, ids >= rows - LAG), 0.0, 1.0).astype(F32)
    count = jnp.where(is_last, rows - LAG, rows).astype(F32)
    early = out[HALO : HALO + rows] * pair
    later = out[HALO + LAG : HALO + LAG + rows] * pair
    mean_e = jnp.sum(early, axis=0) / count
    mean_l = jnp.sum(later, axis=0) / count
    ce = (early - mean_e) * pair
    cl = (later - mean_l) * pair
    local = jnp.stack([tdot(ce, ce, HI), tdot(ce, cl, HI), tdot(cl, cl, HI)])
    means = jnp.stack([mean_e, mean_l])
    half = ch // 2
    per = half // peers
    mine = lax.dynamic_slice_in_dim(local, core * half, half, 1)
    other = lax.dynamic_slice_in_dim(local, (1 - core) * half, half, 1)
    got = swap_core(other.astype(BF)).astype(F32)
    means_hi = means.astype(BF)
    means_lo = (means - means_hi.astype(F32)).astype(BF)
    means_both = jnp.concatenate([means_hi, means_lo], axis=0)
    sib = swap_core(means_both).astype(F32)
    sib = sib[:2] + sib[2:]
    sent = means_hi.astype(F32) + means_lo.astype(F32)
    gap = sent - sib
    mid = 0.5 * (sent + sib)
    gap_mine = lax.dynamic_slice_in_dim(gap, core * half, half, 1)
    outer = jnp.stack(
        [
            gap_mine[0][:, None] * gap[0][None],
            gap_mine[0][:, None] * gap[1][None],
            gap_mine[1][:, None] * gap[1][None],
        ]
    )
    pairsum = mine + got + (0.5 * count) * outer
    mid_hi = mid.astype(BF)
    mid_lo = (mid - mid_hi.astype(F32)).astype(BF)
    mid_rows = jnp.concatenate([mid_hi, mid_lo], axis=0)
    packed = jnp.concatenate(
        [
            pairsum.astype(BF).reshape(3, peers, per, ch).transpose(1, 0, 2, 3).reshape(peers, 3 * per, ch),
            jnp.broadcast_to(mid_rows[None], (peers, 4, ch)),
        ],
        axis=1,
    )
    arrived = exchange(packed).astype(F32)
    within = jnp.sum(arrived[:, : 3 * per], axis=0).reshape(3, per, ch)
    all_means = arrived[:, 3 * per : 3 * per + 2] + arrived[:, 3 * per + 2 :]
    seg_of = jnp.arange(peers) % segments
    counts = jnp.where(seg_of == segments - 1, rows - LAG, rows).astype(F32) * 2.0
    mean_all = jnp.sum(all_means * counts[:, None, None], axis=0) / pair_count
    dev = all_means - mean_all[None]
    peer = lax.axis_index("x") * segments + segment
    start = core * half + peer * per
    dev_rows = lax.dynamic_slice_in_dim(dev, start, per, 2) * counts[:, None, None]
    between = jnp.stack(
        [
            tdot(dev_rows[:, 0], dev[:, 0], HI),
            tdot(dev_rows[:, 0], dev[:, 1], HI),
            tdot(dev_rows[:, 1], dev[:, 1], HI),
        ]
    )
    cov_rows = ((within + between) / pair_count).reshape(3 * per, ch)
    pad = jnp.zeros((4, ch), BF)
    cov_half = spread(jnp.concatenate([cov_rows.astype(BF), pad], axis=0), peers)
    cov_other = swap_core(cov_half)
    low = jnp.where(core == 0, cov_half, cov_other)
    high = jnp.where(core == 0, cov_other, cov_half)
    cov = jnp.stack([low, high])[:, :, : 3 * per].astype(F32)
    cov = cov.reshape(2, peers, 3, per, ch).transpose(2, 0, 1, 3, 4).reshape(3, ch, ch)

    score, ge, gc, gl = score_and_grads(cov[0], cov[1], cov[2])

    grows = rows + 8
    base = lax.slice_in_dim(out, HALO, HALO + grows, axis=0)
    t = time[HALO : HALO + grows]
    has_early = t < length - LAG
    has_later = jnp.logical_and(t >= LAG, t < length)
    ce = jnp.where(has_early, base - mean_all[0], 0.0)
    cl_next = jnp.where(has_early, out[HALO + LAG : HALO + LAG + grows] - mean_all[1], 0.0)
    ce_prev = jnp.where(has_later, out[HALO - LAG : HALO - LAG + grows] - mean_all[0], 0.0)
    cl = jnp.where(has_later, base - mean_all[1], 0.0)
    lhs = jnp.concatenate([ce, cl_next, ce_prev, cl], axis=1)
    rhs = jnp.concatenate([ge, gc.T, gc, gl], axis=0)
    grad = mm(lhs, rhs) / pair_count
    weight_grads, bias_grads = [None] * NL, [None] * NL
    for layer in reversed(range(NL)):
        step = 2**layer
        joined = joined_all[layer]
        squash = squash_all[layer][HALO : HALO + grows]
        pre = jnp.where(t < length, grad * (1.0 - squash * squash), 0.0).astype(BF)
        weight_grads[layer] = tdot(joined[HALO : HALO + rows], pre[:rows])
        bias_grads[layer] = jnp.sum(pre[:rows].astype(F32), axis=0)
        back = dott(pre, w_conv[layer])
        delayed = jnp.concatenate([back[step:, ch:], jnp.zeros((step, ch), F32)], axis=0)
        grad = grad + back[:, :ch] + delayed
    pre0 = (grad[:rows] * (1.0 - squash0 * squash0)).astype(BF)
    g_in = tdot(frames, pre0)
    gb = jnp.stack([jnp.sum(pre0.astype(F32), axis=0)] + bias_grads)

    big = jnp.concatenate([g_in] + weight_grads, axis=0)
    total = big.shape[0]
    half = total // 2
    per = half // peers
    mine = lax.dynamic_slice_in_dim(big, core * half, half, 0)
    other = lax.dynamic_slice_in_dim(big, (1 - core) * half, half, 0)
    mine = mine + swap_core(other.astype(BF)).astype(F32)
    gb_hi = gb.astype(BF)
    gb_lo = (gb - gb_hi.astype(F32)).astype(BF)
    gb_rows = jnp.concatenate([gb_hi, gb_lo], axis=0)
    packed = jnp.concatenate(
        [mine.astype(BF).reshape(peers, per, ch), jnp.broadcast_to(gb_rows[None], (peers, 8, ch))],
        axis=1,
    )
    summed = jnp.sum(exchange(packed).astype(F32), axis=0)
    gb_half = summed[per : per + 4] + summed[per + 4 :]
    gb_hi = gb_half.astype(BF)
    gb_lo = (gb_half - gb_hi.astype(F32)).astype(BF)
    gb_sib = swap_core(jnp.concatenate([gb_hi, gb_lo], axis=0)).astype(F32)
    gb_sum = gb_hi.astype(F32) + gb_lo.astype(F32) + gb_sib[:4] + gb_sib[4:]
    half_sum = spread(summed[:per].astype(BF), peers).reshape(half, ch)
    other_sum = swap_core(half_sum)
    low = jnp.where(core == 0, half_sum, other_sum)
    high = jnp.where(core == 0, other_sum, half_sum)
    full = jnp.concatenate([low, high], axis=0).astype(F32)
    return (
        score,
        full[:features],
        gb_sum[0],
        full[features:].reshape(NL, 2 * ch, ch),
        gb_sum[1:],
    )


def solution(mesh):
    devices = mesh.devices
    trajs, segments = devices.shape
    inner = Mesh(devices.reshape(trajs // 2, 2, segments), ("x", "c", "tm"))
    return jax.shard_map(
        per_device,
        mesh=inner,
        in_specs=(P(("x", "c"), "tm", None), P(), P(), P(), P()),
        out_specs=(P(), P(), P(), P(), P()),
        check_vma=False,
    )
```

```python
import functools

import jax
import jax.numpy as jnp
from jax import lax
from jax.experimental import pallas as pl
from jax.experimental.pallas import tpu as pltpu
from jax.sharding import Mesh, PartitionSpec as P

NL = 3
LAG = 16
RIDGE = 0.0001
HALO = 32
LANES = 128
BF = jnp.bfloat16
F32 = jnp.float32
PEERS = ("x", "tm")
HI = lax.Precision.HIGHEST
C0, C1, C2, C3, C4 = 2.25, -2.4375, 1.6875, -0.5625, 0.0625

NN = (((1,), (0,)), ((), ()))
NT = (((1,), (1,)), ((), ()))
TN = (((0,), (0,)), ((), ()))


def dot(a, b, dims=NN, precision=None):
    return lax.dot_general(a, b, dims, precision=precision, preferred_element_type=F32)


def split(a):
    hi = a.astype(BF)
    return hi, (a - hi.astype(F32)).astype(BF)


def dot3(a, b, dims=NN):
    return dot(a[0], b[0], dims) + (dot(a[0], b[1], dims) + dot(a[1], b[0], dims))


def swap_core(value):
    return lax.ppermute(value, "c", [(0, 1), (1, 0)])


def shift_segment(value, steps):
    count = lax.axis_size("tm")
    first, last = max(0, -steps), min(count, count - steps)
    return lax.ppermute(value, "tm", [(i, i + steps) for i in range(first, last)])


def exchange(value):
    return lax.all_to_all(value, PEERS, 0, 0, tiled=True)


def call(kernel, outs, *args, scratch=(), flops=0, moved=0):
    specs = [
        pl.BlockSpec(memory_space=pltpu.SMEM if a.dtype == jnp.int32 else pltpu.VMEM) for a in args
    ]
    return pl.pallas_call(
        kernel,
        out_shape=outs,
        in_specs=specs,
        out_specs=[pl.BlockSpec(memory_space=pltpu.VMEM) for _ in outs],
        scratch_shapes=list(scratch),
        compiler_params=pltpu.CompilerParams(vmem_limit_bytes=50 * 2**20),
        cost_estimate=pl.CostEstimate(flops=flops, bytes_accessed=moved, transcendentals=0),
    )(*args)


def sds(shape, dtype):
    return jax.ShapeDtypeStruct(shape, dtype)


def forward_kernel(dims, info, before, own, after, w, b, hid, sq, mine, other, means, mom):
    rows, ch, length, peers, piece = dims
    core, segment = info[0], info[1]
    ext = rows + 2 * HALO
    nb = ch // LANES
    t = segment * rows - HALO + lax.broadcasted_iota(jnp.int32, (ext, 1), 0)
    h = jnp.concatenate(
        [before[...].astype(F32), own[...].astype(F32), after[...].astype(F32)], axis=0
    )
    for layer in range(NL):
        hb = h.astype(BF)
        hid[layer] = hb
        hist = pltpu.roll(h, 2**layer, 0).astype(BF)
        s = jnp.tanh(dot(hb, w[layer, :ch]) + dot(hist, w[layer, ch:]) + b[layer : layer + 1])
        sq[layer] = s
        h = jnp.where(t >= 0, (h + s).astype(BF).astype(F32), 0.0)
    hid[NL] = h.astype(BF)
    tp = segment * rows + lax.broadcasted_iota(jnp.int32, (rows, 1), 0)
    pair = jnp.where(tp < length - LAG, 1.0, 0.0).astype(F32)
    last = segment == length // rows - 1
    count = jnp.where(last, rows - LAG, rows).astype(F32)
    early = h[HALO : HALO + rows] * pair
    later = h[HALO + LAG : HALO + LAG + rows] * pair
    mean_e = jnp.sum(early, axis=0, keepdims=True) / count
    mean_l = jnp.sum(later, axis=0, keepdims=True) / count
    means[...] = jnp.concatenate([mean_e, mean_l, jnp.zeros((6, ch), F32)], axis=0)
    ce = split((early - mean_e) * pair)
    cl = split((later - mean_l) * pair)
    left_e = jnp.concatenate([ce[0], ce[0], ce[1]], axis=0)
    left_l = jnp.concatenate([cl[0], cl[0], cl[1]], axis=0)
    right_e = jnp.concatenate([ce[0], ce[1], ce[0]], axis=0)
    right_l = jnp.concatenate([cl[0], cl[1], cl[0]], axis=0)
    mom[0] = dot(left_e, right_e, TN)
    mom[1] = dot(left_e, right_l, TN)
    mom[2] = dot(left_l, right_l, TN)
    half = ch // 2

    def pack(i, carry):
        at = pl.multiple_of(core * half + i * piece, piece)
        to = pl.multiple_of((1 - core) * half + i * piece, piece)
        for m in range(3):
            for j in range(nb):
                cols = slice(j * LANES, (j + 1) * LANES)
                put = slice(m * piece, (m + 1) * piece)
                mine[i * nb + j, put, :] = mom[m, pl.ds(at, piece), cols]
                other[i * nb + j, put, :] = mom[m, pl.ds(to, piece), cols].astype(BF)
        return carry

    lax.fori_loop(0, peers // nb, pack, 0)


def pair_kernel(dims, info, mine, got, means, sib, packed, turned):
    rows, ch, length, peers, piece = dims
    core, segment = info[0], info[1]
    nb = ch // LANES
    half = ch // 2
    last = segment == length // rows - 1
    weight = 0.5 * jnp.where(last, rows - LAG, rows).astype(F32)
    gap = means[...] - sib[...]
    mid = 0.5 * (means[...] + sib[...])
    turned[...] = gap.T * weight
    hi, lo = split(mid)
    tail = []
    for part in (hi.astype(F32), lo.astype(F32)):
        for k in range(2):
            for j in range(nb):
                tail.append(part[k : k + 1, j * LANES : (j + 1) * LANES])
    tail = jnp.concatenate(tail, axis=0).astype(BF)

    def pack(i, carry):
        at = pl.multiple_of(core * half + i * piece, piece)
        col = turned[pl.ds(at, piece), :]
        for j in range(nb):
            cols = slice(j * LANES, (j + 1) * LANES)
            p = i * nb + j
            for m, (a, c) in enumerate(((0, 0), (0, 1), (1, 1))):
                put = slice(m * piece, (m + 1) * piece)
                value = mine[p, put, :] + got[p, put, :].astype(F32)
                value = value + col[:, a : a + 1] * gap[c : c + 1, cols]
                packed[p, put, :] = value.astype(BF)
            packed[p, 3 * piece :, :] = tail
        return carry

    lax.fori_loop(0, peers // nb, pack, 0)


def merge_kernel(dims, info, arrived, cov, mean_all, flat, dev, square):
    rows, ch, length, peers, piece = dims
    core, peer = info[0], info[2]
    nb = ch // LANES
    segments = length // rows
    total = 2 * (peers // segments) * (length - LAG)
    body = 3 * piece

    def add(p, acc):
        z = arrived[p, body:, :].astype(F32)
        flat[pl.ds(pl.multiple_of(p * 2 * nb, 2 * nb), 2 * nb), :] = z[: 2 * nb] + z[2 * nb :]
        return acc + arrived[p, :body, :].astype(F32)

    within = lax.fori_loop(0, peers, add, jnp.zeros((body, LANES), F32))
    seg = lax.rem(lax.broadcasted_iota(jnp.int32, (peers, 1), 0), segments)
    counts = 2.0 * jnp.where(seg == segments - 1, rows - LAG, rows).astype(F32)
    mean_all[...] = jnp.zeros_like(mean_all)
    for k in range(2):
        for j in range(nb):
            cols = slice(j * LANES, (j + 1) * LANES)
            v = flat[pl.ds(k * nb + j, peers, stride=2 * nb), :]
            mean = jnp.sum(v * counts, axis=0, keepdims=True) / total
            mean_all[k : k + 1, cols] = mean
            dev[k, :, cols] = v - mean
    start = core * (ch // 2) + (peer // nb) * piece
    block = pl.multiple_of((start // LANES) * LANES, LANES)
    inside = pl.multiple_of(lax.rem(start, LANES), piece)
    here = pl.multiple_of(lax.rem(peer, nb) * LANES, LANES)
    for m, (a, c) in enumerate(((0, 0), (0, 1), (1, 1))):
        left = dev[a, :, pl.ds(block, LANES)] * counts
        square[m] = dot(left, dev[c, :, pl.ds(here, LANES)], TN, HI)
    between = jnp.concatenate([square[m, pl.ds(inside, piece), :] for m in range(3)], axis=0)
    value = ((within + between) / total).astype(BF)
    cov[...] = jnp.broadcast_to(value[None], cov.shape)


def score_kernel(dims, info, half_cov, other_cov, grads, score, cov):
    rows, ch, length, peers, piece = dims
    core = info[0]
    nb = ch // LANES
    half = ch // 2

    def place(i, carry):
        at = pl.multiple_of(core * half + i * piece, piece)
        to = pl.multiple_of((1 - core) * half + i * piece, piece)
        for m in range(3):
            for j in range(nb):
                cols = slice(j * LANES, (j + 1) * LANES)
                put = slice(m * piece, (m + 1) * piece)
                cov[m, pl.ds(at, piece), cols] = half_cov[i * nb + j, put, :].astype(F32)
                cov[m, pl.ds(to, piece), cols] = other_cov[i * nb + j, put, :].astype(F32)
        return carry

    lax.fori_loop(0, peers // nb, place, 0)
    row = lax.broadcasted_iota(jnp.int32, (ch, ch), 0)
    col = lax.broadcasted_iota(jnp.int32, (ch, ch), 1)
    unit = jnp.where(row == col, 1.0, 0.0).astype(F32)

    def forward(matrix):
        shifted = matrix + RIDGE * unit
        square = jnp.sum(shifted * shifted, keepdims=True)
        inv_scale = lax.rsqrt(square)
        a = shifted * inv_scale
        ab = a.astype(BF)
        a2 = dot(ab, ab)
        a2b = a2.astype(BF)
        poly = C0 * unit + C1 * a + C2 * a2 + dot(a2b, (C3 * a + C4 * a2).astype(BF))
        root = jnp.sqrt(inv_scale)
        return a, ab, a2b, poly, inv_scale, root, split(poly * root)

    def backward(a, ab, a2b, poly, inv_scale, root, grad):
        dscale = -0.5 * jnp.sum(grad * poly, keepdims=True) * root * inv_scale
        g = grad * root
        gb = g.astype(BF)
        y = dot(gb, ab)
        x = dot(a2b, gb)
        xs = x + x.T
        h = C2 * g + (0.5 * C3) * (y + y.T) + C4 * xs
        z = dot(ab, h.astype(BF))
        da = C1 * g + (0.5 * C3) * xs + z + z.T
        dscale = dscale - jnp.sum(da * a, keepdims=True) * inv_scale
        return da * inv_scale + dscale * a

    fe = forward(cov[0])
    fl = forward(cov[2])
    re, rl = fe[6], fl[6]
    c = split(cov[1])
    u = split(dot3(re, c))
    v = split(dot3(c, rl))
    k = dot3(u, rl)
    score[...] = jnp.broadcast_to(1.0 + jnp.sum(k * k, keepdims=True), score.shape)
    k2 = split(2.0 * k)
    gc = dot3(split(dot3(re, k2)), rl)
    grads[ch : 2 * ch] = gc.T.astype(BF)
    grads[2 * ch : 3 * ch] = gc.astype(BF)
    gre = dot3(k2, v, NT)
    grads[:ch] = backward(*fe[:6], gre + gre.T).astype(BF)
    grl = dot3(u, k2, TN)
    grads[3 * ch :] = backward(*fl[:6], grl + grl.T).astype(BF)


def backward_kernel(dims, info, hid, sq, sq0, frames, w, grads, mean_all, mine, other):
    rows, ch, length, peers, piece = dims
    core, segment = info[0], info[1]
    segments = length // rows
    features = frames.shape[1]
    half = ch // 2
    nh = half // LANES
    total = 2 * (peers // segments) * (length - LAG)
    grows = rows + 16
    t = segment * rows + lax.broadcasted_iota(jnp.int32, (grows, 1), 0)
    has_early = t < length - LAG
    has_later = jnp.logical_and(t >= LAG, t < length)
    out = hid[NL].astype(F32)
    base = out[HALO : HALO + grows]
    mean_e, mean_l = mean_all[0:1], mean_all[1:2]
    zero = jnp.zeros((1, ch), F32)
    consts = []
    for early_on in (True, False):
        left_e, left_l = mean_e, mean_l
        for _ in range(3):
            top_e, top_l = left_e.astype(BF).astype(F32), left_l.astype(BF).astype(F32)
            parts = [top_e, top_l, zero, zero] if early_on else [zero, zero, top_e, top_l]
            consts.append(jnp.concatenate(parts, axis=1))
            left_e, left_l = left_e - top_e, left_l - top_l
    consts = jnp.concatenate(consts + [jnp.zeros((10, 4 * ch), F32)], axis=0)
    lhs = jnp.concatenate(
        [
            jnp.where(has_early, base, 0.0),
            jnp.where(has_early, out[HALO + LAG : HALO + LAG + grows], 0.0),
            jnp.where(has_later, out[HALO - LAG : HALO - LAG + grows], 0.0),
            jnp.where(has_later, base, 0.0),
        ],
        axis=1,
    )
    lhs = jnp.concatenate([lhs, consts], axis=0).astype(BF)
    grad = dot(lhs, grads[...])
    off_early = grad[grows : grows + 1] + grad[grows + 1 : grows + 2] + grad[grows + 2 : grows + 3]
    off_later = grad[grows + 3 : grows + 4] + grad[grows + 4 : grows + 5] + grad[grows + 5 : grows + 6]
    grad = grad[:grows] - jnp.where(has_early, off_early, 0.0) - jnp.where(has_later, off_later, 0.0)
    grad = grad / total
    biases = [None] * (NL + 1)
    first = core == 0

    def halves(value):
        lo, hi = value[:, :half], value[:, half:]
        return jnp.where(first, lo, hi), jnp.where(first, hi, lo)

    def store(left, value, p0, count, size, at):
        for part, ref in zip(halves(value), (mine, other)):
            res = dot(left, part.astype(BF), TN).astype(BF)
            for j in range(nh):
                piece_j = res[:, j * LANES : (j + 1) * LANES].reshape(count, size, LANES)
                ref[p0 : p0 + count, at + j * size : at + (j + 1) * size, :] = piece_j

    in_size = features // peers
    conv_size = 2 * ch // peers
    for layer in reversed(range(NL)):
        step = 2**layer
        s = sq[layer, HALO : HALO + grows, :]
        pre = jnp.where(t < length, grad * (1.0 - s * s), 0.0).astype(BF)
        own = pre[:rows].astype(F32)
        biases[layer + 1] = jnp.sum(own, axis=0, keepdims=True)
        h = hid[layer].astype(F32)
        hist = pltpu.roll(h, step, 0)[HALO : HALO + rows].astype(BF)
        at = nh * in_size + layer * nh * conv_size
        count = ch // conv_size
        store(hid[layer, HALO : HALO + rows, :], own, 0, count, conv_size, at)
        store(hist, own, count, count, conv_size, at)
        back = dot(pre, w[layer, ch:], NT)
        grad = grad + dot(pre, w[layer, :ch], NT) + pltpu.roll(back, grows - step, 0)
    s = sq0[...]
    own = (grad[:rows] * (1.0 - s * s)).astype(BF).astype(F32)
    biases[0] = jnp.sum(own, axis=0, keepdims=True)
    tile = min(features, 512)
    for k in range(features // tile):
        count = tile // in_size
        store(frames[:, k * tile : (k + 1) * tile], own, k * count, count, in_size, 0)
    bias = jnp.concatenate(biases, axis=0)
    for part, ref in zip(halves(bias), (mine, other)):
        hi, lo = split(part)
        tail = []
        for value in (hi.astype(F32), lo.astype(F32)):
            for j in range(nh):
                tail.append(value[:, j * LANES : (j + 1) * LANES])
        tail = jnp.concatenate(tail, axis=0).astype(BF)
        at = ref.shape[1] - tail.shape[0]
        ref[:, at:, :] = jnp.broadcast_to(tail[None], (peers,) + tail.shape)


def add_kernel(nbias, mine, got, packed):
    body = packed.shape[1] - 2 * nbias
    a, b = mine[...].astype(F32), got[...].astype(F32)
    value = a + b
    packed[:, :body, :] = value[:, :body].astype(BF)
    bias = value[0, body : body + nbias] + value[0, body + nbias :]
    hi = bias.astype(BF).astype(F32)
    tail = jnp.concatenate([hi, bias - hi], axis=0).astype(BF)
    packed[:, body:, :] = jnp.broadcast_to(tail[None], (packed.shape[0],) + tail.shape)


def sum_kernel(arrived, tails, full, bias):
    peers = arrived.shape[0]

    def add(p, acc):
        return acc + arrived[p].astype(F32)

    value = lax.fori_loop(0, peers, add, jnp.zeros(arrived.shape[1:], F32), unroll=4)
    full[...] = jnp.broadcast_to(value.astype(BF)[None], full.shape)

    @pl.when(pl.program_id(0) == 0)
    def _():
        def add_tail(p, acc):
            return acc + tails[p].astype(F32)

        t = lax.fori_loop(0, peers, add_tail, jnp.zeros(tails.shape[1:], F32))
        n = t.shape[0] // 2
        bias[...] = t[:n] + t[n:]


def unpack_kernel(sizes, info, mine, got, bias, bias_got, w_in, w_conv, b_all):
    in_size, conv_size, nh = sizes
    first = info[0] == 0
    count = mine.shape[0]
    lo = jnp.where(first, mine[...].astype(F32), got[...].astype(F32))
    hi = jnp.where(first, got[...].astype(F32), mine[...].astype(F32))
    for side, value in enumerate((lo, hi)):
        for j in range(nh):
            cols = slice((side * nh + j) * LANES, (side * nh + j + 1) * LANES)
            part = value[:, j * in_size : (j + 1) * in_size]
            w_in[:, cols] = part.reshape(count * in_size, LANES)
            for layer in range(NL):
                at = nh * in_size + (layer * nh + j) * conv_size
                part = value[:, at : at + conv_size]
                w_conv[layer, :, cols] = part.reshape(count * conv_size, LANES)

    @pl.when(pl.program_id(0) == 0)
    def _():
        lo = jnp.where(first, bias[...], bias_got[...])
        hi = jnp.where(first, bias_got[...], bias[...])
        n = NL + 1
        for side, value in enumerate((lo, hi)):
            for j in range(nh):
                cols = slice((side * nh + j) * LANES, (side * nh + j + 1) * LANES)
                b_all[:, cols] = value[j * n : (j + 1) * n]


def per_device(frames, w_in, b_in, w_conv, b_conv):
    frames = frames[0]
    rows, features = frames.shape
    ch = w_in.shape[1]
    core = lax.axis_index("c")
    segment = lax.axis_index("tm")
    segments = lax.axis_size("tm")
    peers = lax.axis_size("x") * segments
    length = rows * segments
    nb = ch // LANES
    nh = nb // 2
    piece = (ch // 2) * nb // peers
    dims = (rows, ch, length, peers, piece)
    info = jnp.stack([core, segment, lax.axis_index("x") * segments + segment]).astype(jnp.int32)
    ext = rows + 2 * HALO

    squash0 = jnp.tanh(jnp.dot(frames, w_in, preferred_element_type=F32) + b_in)
    own = squash0.astype(BF)
    before = shift_segment(own[rows - HALO :], 1)
    after = shift_segment(own[:HALO], -1)
    hid, sq, mine, other, means = call(
        functools.partial(forward_kernel, dims),
        [
            sds((NL + 1, ext, ch), BF),
            sds((NL, ext, ch), F32),
            sds((peers, 3 * piece, LANES), F32),
            sds((peers, 3 * piece, LANES), BF),
            sds((8, ch), F32),
        ],
        info, before, own, after, w_conv, b_conv,
        scratch=[pltpu.VMEM((3, ch, ch), F32)],
    )
    (packed,) = call(
        functools.partial(pair_kernel, dims),
        [sds((peers, 3 * piece + 4 * nb, LANES), BF)],
        info, mine, swap_core(other), means, swap_core(means),
        scratch=[pltpu.VMEM((ch, 8), F32)],
    )
    cov, mean_all = call(
        functools.partial(merge_kernel, dims),
        [sds((peers, 3 * piece, LANES), BF), sds((8, ch), F32)],
        info, exchange(packed),
        scratch=[
            pltpu.VMEM((peers * 2 * nb, LANES), F32),
            pltpu.VMEM((2, peers, ch), F32),
            pltpu.VMEM((3, LANES, LANES), F32),
        ],
    )
    cov = exchange(cov)
    grads, score = call(
        functools.partial(score_kernel, dims),
        [sds((4 * ch, ch), BF), sds((8, LANES), F32)],
        info, cov, swap_core(cov),
        scratch=[pltpu.VMEM((3, ch, ch), F32)],
    )
    in_size = features // peers
    conv_size = 2 * ch // peers
    body = nh * (in_size + NL * conv_size)
    nbias = (NL + 1) * nh
    wide = body + 2 * nbias
    mine, other = call(
        functools.partial(backward_kernel, dims),
        [sds((peers, wide, LANES), BF), sds((peers, wide, LANES), BF)],
        info, hid, sq, squash0, frames, w_conv, grads, mean_all,
    )
    group = 8
    params = pltpu.CompilerParams(vmem_limit_bytes=50 * 2**20)
    spec = pl.BlockSpec((group, wide, LANES), lambda i: (i, 0, 0))
    packed = pl.pallas_call(
        functools.partial(add_kernel, nbias),
        grid=(peers // group,),
        out_shape=sds((peers, wide, LANES), BF),
        in_specs=[spec, spec],
        out_specs=spec,
        compiler_params=params,
    )(mine, swap_core(other))
    arrived = exchange(packed)
    block = 32
    full, bias = pl.pallas_call(
        sum_kernel,
        grid=(body // block,),
        out_shape=[sds((peers, body, LANES), BF), sds((nbias, LANES), F32)],
        in_specs=[
            pl.BlockSpec((peers, block, LANES), lambda i: (0, i, 0)),
            pl.BlockSpec((peers, 2 * nbias, LANES), lambda i: (0, body // (2 * nbias), 0)),
        ],
        out_specs=[
            pl.BlockSpec((peers, block, LANES), lambda i: (0, i, 0)),
            pl.BlockSpec((nbias, LANES), lambda i: (0, 0)),
        ],
        compiler_params=params,
    )(arrived, arrived)
    bias_got = swap_core(bias)
    full = exchange(full)
    spec = pl.BlockSpec((group, body, LANES), lambda i: (i, 0, 0))
    small = pl.BlockSpec((nbias, LANES), lambda i: (0, 0))
    g_in, g_conv, g_bias = pl.pallas_call(
        functools.partial(unpack_kernel, (in_size, conv_size, nh)),
        grid=(peers // group,),
        out_shape=[sds((features, ch), F32), sds((NL, 2 * ch, ch), F32), sds((NL + 1, ch), F32)],
        in_specs=[pl.BlockSpec(memory_space=pltpu.SMEM), spec, spec, small, small],
        out_specs=[
            pl.BlockSpec((group * in_size, ch), lambda i: (i, 0)),
            pl.BlockSpec((NL, group * conv_size, ch), lambda i: (0, i, 0)),
            pl.BlockSpec((NL + 1, ch), lambda i: (0, 0)),
        ],
        compiler_params=params,
    )(info, full, swap_core(full), bias, bias_got)
    return score[0, 0], g_in, g_bias[0], g_conv, g_bias[1:]


def solution(mesh):
    devices = mesh.devices
    trajs, segments = devices.shape
    inner = Mesh(devices.reshape(trajs // 2, 2, segments), ("x", "c", "tm"))
    return jax.shard_map(
        per_device,
        mesh=inner,
        in_specs=(P(("x", "c"), "tm", None), P(), P(), P(), P()),
        out_specs=(P(), P(), P(), P(), P()),
        check_vma=False,
    )
```

```python
import functools

import jax
import jax.numpy as jnp
from jax import lax
from jax.experimental import pallas as pl
from jax.experimental.pallas import tpu as pltpu
from jax.sharding import Mesh, PartitionSpec as P

NL = 3
LAG = 16
RIDGE = 0.0001
HALO = 32
LANES = 128
BF = jnp.bfloat16
F32 = jnp.float32
PEERS = ("x", "tm")
HI = lax.Precision.HIGHEST
C0, C1, C2, C3, C4 = 2.25, -2.4375, 1.6875, -0.5625, 0.0625

NN = (((1,), (0,)), ((), ()))
NT = (((1,), (1,)), ((), ()))
TN = (((0,), (0,)), ((), ()))


def dot(a, b, dims=NN, precision=None):
    return lax.dot_general(a, b, dims, precision=precision, preferred_element_type=F32)


def split(a):
    hi = a.astype(BF)
    return hi, (a - hi.astype(F32)).astype(BF)


def dot3(a, b, dims=NN):
    return dot(a[0], b[0], dims) + (dot(a[0], b[1], dims) + dot(a[1], b[0], dims))


def swap_core(value):
    return lax.ppermute(value, "c", [(0, 1), (1, 0)])


def shift_segment(value, steps):
    count = lax.axis_size("tm")
    first, last = max(0, -steps), min(count, count - steps)
    return lax.ppermute(value, "tm", [(i, i + steps) for i in range(first, last)])


def exchange(value):
    return lax.all_to_all(value, PEERS, 0, 0, tiled=True)


def call(kernel, outs, *args, scratch=(), flops=0, moved=0):
    specs = [
        pl.BlockSpec(memory_space=pltpu.SMEM if a.dtype == jnp.int32 else pltpu.VMEM) for a in args
    ]
    return pl.pallas_call(
        kernel,
        out_shape=outs,
        in_specs=specs,
        out_specs=[pl.BlockSpec(memory_space=pltpu.VMEM) for _ in outs],
        scratch_shapes=list(scratch),
        compiler_params=pltpu.CompilerParams(vmem_limit_bytes=50 * 2**20),
        cost_estimate=pl.CostEstimate(flops=flops, bytes_accessed=moved, transcendentals=0),
    )(*args)


def sds(shape, dtype):
    return jax.ShapeDtypeStruct(shape, dtype)


def forward_kernel(dims, info, before, own, after, w, b, hid, sq, mine, other, means, mom):
    rows, ch, length, peers, piece = dims
    core, segment = info[0], info[1]
    ext = rows + 2 * HALO
    nb = ch // LANES
    t = segment * rows - HALO + lax.broadcasted_iota(jnp.int32, (ext, 1), 0)
    h = jnp.concatenate(
        [before[...].astype(F32), own[...].astype(F32), after[...].astype(F32)], axis=0
    )
    for layer in range(NL):
        hb = h.astype(BF)
        hid[layer] = hb
        hist = pltpu.roll(h, 2**layer, 0).astype(BF)
        s = jnp.tanh(dot(hb, w[layer, :ch]) + dot(hist, w[layer, ch:]) + b[layer : layer + 1])
        sq[layer] = s
        h = jnp.where(t >= 0, (h + s).astype(BF).astype(F32), 0.0)
    hid[NL] = h.astype(BF)
    tp = segment * rows + lax.broadcasted_iota(jnp.int32, (rows, 1), 0)
    pair = jnp.where(tp < length - LAG, 1.0, 0.0).astype(F32)
    last = segment == length // rows - 1
    count = jnp.where(last, rows - LAG, rows).astype(F32)
    early = h[HALO : HALO + rows] * pair
    later = h[HALO + LAG : HALO + LAG + rows] * pair
    mean_e = jnp.sum(early, axis=0, keepdims=True) / count
    mean_l = jnp.sum(later, axis=0, keepdims=True) / count
    means[...] = jnp.concatenate([mean_e, mean_l, jnp.zeros((6, ch), F32)], axis=0)
    ce = split((early - mean_e) * pair)
    cl = split((later - mean_l) * pair)
    left_e = jnp.concatenate([ce[0], ce[0], ce[1]], axis=0)
    left_l = jnp.concatenate([cl[0], cl[0], cl[1]], axis=0)
    right_e = jnp.concatenate([ce[0], ce[1], ce[0]], axis=0)
    right_l = jnp.concatenate([cl[0], cl[1], cl[0]], axis=0)
    mom[0] = dot(left_e, right_e, TN)
    mom[1] = dot(left_e, right_l, TN)
    mom[2] = dot(left_l, right_l, TN)
    half = ch // 2

    def pack(i, carry):
        at = pl.multiple_of(core * half + i * piece, piece)
        to = pl.multiple_of((1 - core) * half + i * piece, piece)
        for m in range(3):
            for j in range(nb):
                cols = slice(j * LANES, (j + 1) * LANES)
                put = slice(m * piece, (m + 1) * piece)
                mine[i * nb + j, put, :] = mom[m, pl.ds(at, piece), cols]
                other[i * nb + j, put, :] = mom[m, pl.ds(to, piece), cols].astype(BF)
        return carry

    lax.fori_loop(0, peers // nb, pack, 0)


def pair_kernel(dims, info, mine, got, means, sib, packed, turned):
    rows, ch, length, peers, piece = dims
    core, segment = info[0], info[1]
    nb = ch // LANES
    half = ch // 2
    last = segment == length // rows - 1
    weight = 0.5 * jnp.where(last, rows - LAG, rows).astype(F32)
    gap = means[...] - sib[...]
    mid = 0.5 * (means[...] + sib[...])
    turned[...] = gap.T * weight
    hi, lo = split(mid)
    tail = []
    for part in (hi.astype(F32), lo.astype(F32)):
        for k in range(2):
            for j in range(nb):
                tail.append(part[k : k + 1, j * LANES : (j + 1) * LANES])
    tail = jnp.concatenate(tail, axis=0).astype(BF)

    def pack(i, carry):
        at = pl.multiple_of(core * half + i * piece, piece)
        col = turned[pl.ds(at, piece), :]
        for j in range(nb):
            cols = slice(j * LANES, (j + 1) * LANES)
            p = i * nb + j
            for m, (a, c) in enumerate(((0, 0), (0, 1), (1, 1))):
                put = slice(m * piece, (m + 1) * piece)
                value = mine[p, put, :] + got[p, put, :].astype(F32)
                value = value + col[:, a : a + 1] * gap[c : c + 1, cols]
                packed[p, put, :] = value.astype(BF)
            packed[p, 3 * piece :, :] = tail
        return carry

    lax.fori_loop(0, peers // nb, pack, 0)


def merge_kernel(dims, info, arrived, cov, mean_all, flat, dev, square):
    rows, ch, length, peers, piece = dims
    core, peer = info[0], info[2]
    nb = ch // LANES
    segments = length // rows
    total = 2 * (peers // segments) * (length - LAG)
    body = 3 * piece

    def add(p, acc):
        z = arrived[p, body:, :].astype(F32)
        flat[pl.ds(pl.multiple_of(p * 2 * nb, 2 * nb), 2 * nb), :] = z[: 2 * nb] + z[2 * nb :]
        return acc + arrived[p, :body, :].astype(F32)

    within = lax.fori_loop(0, peers, add, jnp.zeros((body, LANES), F32))
    seg = lax.rem(lax.broadcasted_iota(jnp.int32, (peers, 1), 0), segments)
    counts = 2.0 * jnp.where(seg == segments - 1, rows - LAG, rows).astype(F32)
    mean_all[...] = jnp.zeros_like(mean_all)
    for k in range(2):
        for j in range(nb):
            cols = slice(j * LANES, (j + 1) * LANES)
            v = flat[pl.ds(k * nb + j, peers, stride=2 * nb), :]
            mean = jnp.sum(v * counts, axis=0, keepdims=True) / total
            mean_all[k : k + 1, cols] = mean
            dev[k, :, cols] = v - mean
    start = core * (ch // 2) + (peer // nb) * piece
    block = pl.multiple_of((start // LANES) * LANES, LANES)
    inside = pl.multiple_of(lax.rem(start, LANES), piece)
    here = pl.multiple_of(lax.rem(peer, nb) * LANES, LANES)
    for m, (a, c) in enumerate(((0, 0), (0, 1), (1, 1))):
        left = dev[a, :, pl.ds(block, LANES)] * counts
        square[m] = dot(left, dev[c, :, pl.ds(here, LANES)], TN, HI)
    between = jnp.concatenate([square[m, pl.ds(inside, piece), :] for m in range(3)], axis=0)
    value = ((within + between) / total).astype(BF)
    cov[...] = jnp.broadcast_to(value[None], cov.shape)


def step_kernel(
    dims, info, half_cov, other_cov, mean_all, hid_hbm, sq_hbm, sq0_hbm, w_hbm,
    score, mine, other, dpre, cov, grads, hid, sq, sq0, w, sems,
):
    rows, ch, length, peers, piece = dims
    core = info[0]
    nb = ch // LANES
    half = ch // 2
    loads = [
        pltpu.make_async_copy(src, dst, sems.at[n])
        for n, (src, dst) in enumerate(((hid_hbm, hid), (sq_hbm, sq), (sq0_hbm, sq0), (w_hbm, w)))
    ]
    for load in loads:
        load.start()

    def place(i, carry):
        at = pl.multiple_of(core * half + i * piece, piece)
        to = pl.multiple_of((1 - core) * half + i * piece, piece)
        for m in range(3):
            for j in range(nb):
                cols = slice(j * LANES, (j + 1) * LANES)
                put = slice(m * piece, (m + 1) * piece)
                cov[m, pl.ds(at, piece), cols] = half_cov[i * nb + j, put, :].astype(F32)
                cov[m, pl.ds(to, piece), cols] = other_cov[i * nb + j, put, :].astype(F32)
        return carry

    lax.fori_loop(0, peers // nb, place, 0)
    row = lax.broadcasted_iota(jnp.int32, (ch, ch), 0)
    col = lax.broadcasted_iota(jnp.int32, (ch, ch), 1)
    unit = jnp.where(row == col, 1.0, 0.0).astype(F32)

    def forward(matrix):
        shifted = matrix + RIDGE * unit
        square = jnp.sum(shifted * shifted, keepdims=True)
        inv_scale = lax.rsqrt(square)
        a = shifted * inv_scale
        ab = a.astype(BF)
        a2 = dot(ab, ab)
        a2b = a2.astype(BF)
        poly = C0 * unit + C1 * a + C2 * a2 + dot(a2b, (C3 * a + C4 * a2).astype(BF))
        root = jnp.sqrt(inv_scale)
        return a, ab, a2b, poly, inv_scale, root, split(poly * root)

    def backward(a, ab, a2b, poly, inv_scale, root, grad):
        dscale = -0.5 * jnp.sum(grad * poly, keepdims=True) * root * inv_scale
        g = grad * root
        gb = g.astype(BF)
        y = dot(gb, ab)
        x = dot(a2b, gb)
        xs = x + x.T
        h = C2 * g + (0.5 * C3) * (y + y.T) + C4 * xs
        z = dot(ab, h.astype(BF))
        da = C1 * g + (0.5 * C3) * xs + z + z.T
        dscale = dscale - jnp.sum(da * a, keepdims=True) * inv_scale
        return da * inv_scale + dscale * a

    fe = forward(cov[0])
    fl = forward(cov[2])
    re, rl = fe[6], fl[6]
    c = split(cov[1])
    u = split(dot3(re, c))
    v = split(dot3(c, rl))
    k = dot3(u, rl)
    score[...] = jnp.broadcast_to(1.0 + jnp.sum(k * k, keepdims=True), score.shape)
    k2 = split(2.0 * k)
    gc = dot3(split(dot3(re, k2)), rl)
    grads[ch : 2 * ch] = gc.T.astype(BF)
    grads[2 * ch : 3 * ch] = gc.astype(BF)
    gre = dot3(k2, v, NT)
    grads[:ch] = backward(*fe[:6], gre + gre.T).astype(BF)
    grl = dot3(u, k2, TN)
    grads[3 * ch :] = backward(*fl[:6], grl + grl.T).astype(BF)
    for load in loads:
        load.wait()
    conv_backward(dims, info, hid, sq, sq0, w, grads, mean_all, mine, other, dpre)


def conv_backward(dims, info, hid, sq, sq0, w, grads, mean_all, mine, other, dpre):
    rows, ch, length, peers, piece = dims
    core, segment = info[0], info[1]
    segments = length // rows
    half = ch // 2
    nh = half // LANES
    total = 2 * (peers // segments) * (length - LAG)
    grows = rows + 16
    t = segment * rows + lax.broadcasted_iota(jnp.int32, (grows, 1), 0)
    has_early = t < length - LAG
    has_later = jnp.logical_and(t >= LAG, t < length)
    out = hid[NL].astype(F32)
    base = out[HALO : HALO + grows]
    mean_e, mean_l = mean_all[0:1], mean_all[1:2]
    zero = jnp.zeros((1, ch), F32)
    consts = []
    for early_on in (True, False):
        left_e, left_l = mean_e, mean_l
        for _ in range(3):
            top_e, top_l = left_e.astype(BF).astype(F32), left_l.astype(BF).astype(F32)
            parts = [top_e, top_l, zero, zero] if early_on else [zero, zero, top_e, top_l]
            consts.append(jnp.concatenate(parts, axis=1))
            left_e, left_l = left_e - top_e, left_l - top_l
    consts = jnp.concatenate(consts + [jnp.zeros((10, 4 * ch), F32)], axis=0)
    lhs = jnp.concatenate(
        [
            jnp.where(has_early, base, 0.0),
            jnp.where(has_early, out[HALO + LAG : HALO + LAG + grows], 0.0),
            jnp.where(has_later, out[HALO - LAG : HALO - LAG + grows], 0.0),
            jnp.where(has_later, base, 0.0),
        ],
        axis=1,
    )
    lhs = jnp.concatenate([lhs, consts], axis=0).astype(BF)
    grad = dot(lhs, grads[...])
    off_early = grad[grows : grows + 1] + grad[grows + 1 : grows + 2] + grad[grows + 2 : grows + 3]
    off_later = grad[grows + 3 : grows + 4] + grad[grows + 4 : grows + 5] + grad[grows + 5 : grows + 6]
    grad = grad[:grows] - jnp.where(has_early, off_early, 0.0) - jnp.where(has_later, off_later, 0.0)
    grad = grad / total
    biases = [None] * (NL + 1)
    first = core == 0

    def halves(value):
        lo, hi = value[:, :half], value[:, half:]
        return jnp.where(first, lo, hi), jnp.where(first, hi, lo)

    def store(left, value, p0, count, size, at):
        for part, ref in zip(halves(value), (mine, other)):
            res = dot(left, part.astype(BF), TN).astype(BF)
            for j in range(nh):
                piece_j = res[:, j * LANES : (j + 1) * LANES].reshape(count, size, LANES)
                ref[p0 : p0 + count, at + j * size : at + (j + 1) * size, :] = piece_j

    conv_size = 2 * ch // peers
    for layer in reversed(range(NL)):
        step = 2**layer
        s = sq[layer, HALO : HALO + grows, :]
        pre = jnp.where(t < length, grad * (1.0 - s * s), 0.0).astype(BF)
        own = pre[:rows].astype(F32)
        biases[layer + 1] = jnp.sum(own, axis=0, keepdims=True)
        h = hid[layer].astype(F32)
        hist = pltpu.roll(h, step, 0)[HALO : HALO + rows].astype(BF)
        at = layer * nh * conv_size
        count = ch // conv_size
        store(hid[layer, HALO : HALO + rows, :], own, 0, count, conv_size, at)
        store(hist, own, count, count, conv_size, at)
        back = dot(pre, w[layer, ch:], NT)
        grad = grad + dot(pre, w[layer, :ch], NT) + pltpu.roll(back, grows - step, 0)
    s = sq0[...]
    own = (grad[:rows] * (1.0 - s * s)).astype(BF)
    dpre[...] = own
    biases[0] = jnp.sum(own.astype(F32), axis=0, keepdims=True)
    bias = jnp.concatenate(biases, axis=0)
    for part, ref in zip(halves(bias), (mine, other)):
        hi, lo = split(part)
        tail = []
        for value in (hi.astype(F32), lo.astype(F32)):
            for j in range(nh):
                tail.append(value[:, j * LANES : (j + 1) * LANES])
        tail = jnp.concatenate(tail, axis=0).astype(BF)
        at = ref.shape[1] - tail.shape[0]
        ref[:, at:, :] = jnp.broadcast_to(tail[None], (peers,) + tail.shape)


def pack_kernel(nbias, info, left, left_got, dpre, dpre_got, mine, got, packed):
    count = packed.shape[0]
    ch = dpre.shape[1]
    size = left.shape[1] // count
    lhs = jnp.concatenate([left[...], left_got[...]], axis=0)
    res = dot(lhs, jnp.concatenate([dpre[...], dpre_got[...]], axis=0), TN).astype(BF)
    for j in range(ch // LANES):
        part = res[:, j * LANES : (j + 1) * LANES].reshape(count, size, LANES)
        packed[:, j * size : (j + 1) * size, :] = part
    at = size * (ch // LANES)
    body = mine.shape[1] - 2 * nbias
    value = mine[...].astype(F32) + got[...].astype(F32)
    packed[:, at : at + body, :] = value[:, :body].astype(BF)
    bias = value[0, body : body + nbias] + value[0, body + nbias :]
    hi = bias.astype(BF).astype(F32)
    tail = jnp.concatenate([hi, bias - hi], axis=0).astype(BF)
    packed[:, at + body :, :] = jnp.broadcast_to(tail[None], (count,) + tail.shape)


def sum_kernel(arrived, tails, full, bias):
    peers = arrived.shape[0]

    def add(p, acc):
        return acc + arrived[p].astype(F32)

    value = lax.fori_loop(0, peers, add, jnp.zeros(arrived.shape[1:], F32), unroll=4)
    full[...] = jnp.broadcast_to(value.astype(BF)[None], full.shape)

    @pl.when(pl.program_id(0) == 0)
    def _():
        def add_tail(p, acc):
            return acc + tails[p].astype(F32)

        t = lax.fori_loop(0, peers, add_tail, jnp.zeros(tails.shape[1:], F32))
        n = t.shape[0] // 2
        bias[...] = t[:n] + t[n:]


def unpack_kernel(sizes, info, chunks, *refs):
    in_size, conv_size, nb = sizes
    w_in, w_conv = refs[-2:]
    count = chunks.shape[0]
    for j in range(nb):
        part = chunks[:, j * in_size : (j + 1) * in_size, :].astype(F32)
        w_in[0, :, j * LANES : (j + 1) * LANES] = part.reshape(count * in_size, LANES)
    for layer in range(NL):
        for j in range(nb // 2):
            at = nb * in_size + (layer * (nb // 2) + j) * conv_size
            part = chunks[:, at : at + conv_size, :].astype(F32)
            w_conv[layer, :, j * LANES : (j + 1) * LANES] = part.reshape(count * conv_size, LANES)


def per_device(frames, w_in, b_in, w_conv, b_conv):
    frames = frames[0]
    rows, features = frames.shape
    ch = w_in.shape[1]
    core = lax.axis_index("c")
    segment = lax.axis_index("tm")
    segments = lax.axis_size("tm")
    peers = lax.axis_size("x") * segments
    length = rows * segments
    nb = ch // LANES
    nh = nb // 2
    piece = (ch // 2) * nb // peers
    dims = (rows, ch, length, peers, piece)
    info = jnp.stack([core, segment, lax.axis_index("x") * segments + segment]).astype(jnp.int32)
    ext = rows + 2 * HALO
    frames_got = swap_core(
        lax.dynamic_slice_in_dim(frames, (1 - core) * (features // 2), features // 2, 1)
    )

    squash0 = jnp.tanh(jnp.dot(frames, w_in, preferred_element_type=F32) + b_in)
    own = squash0.astype(BF)
    before = shift_segment(own[rows - HALO :], 1)
    after = shift_segment(own[:HALO], -1)
    hid, sq, mine, other, means = call(
        functools.partial(forward_kernel, dims),
        [
            sds((NL + 1, ext, ch), BF),
            sds((NL, ext, ch), F32),
            sds((peers, 3 * piece, LANES), F32),
            sds((peers, 3 * piece, LANES), BF),
            sds((8, ch), F32),
        ],
        info, before, own, after, w_conv, b_conv,
        scratch=[pltpu.VMEM((3, ch, ch), F32)],
    )
    (packed,) = call(
        functools.partial(pair_kernel, dims),
        [sds((peers, 3 * piece + 4 * nb, LANES), BF)],
        info, mine, swap_core(other), means, swap_core(means),
        scratch=[pltpu.VMEM((ch, 8), F32)],
    )
    cov, mean_all = call(
        functools.partial(merge_kernel, dims),
        [sds((peers, 3 * piece, LANES), BF), sds((8, ch), F32)],
        info, exchange(packed),
        scratch=[
            pltpu.VMEM((peers * 2 * nb, LANES), F32),
            pltpu.VMEM((2, peers, ch), F32),
            pltpu.VMEM((3, LANES, LANES), F32),
        ],
    )
    cov = exchange(cov)
    half_features = features // 2
    in_size = half_features // peers
    conv_size = 2 * ch // peers
    nbias = (NL + 1) * nh
    conv_wide = NL * nh * conv_size + 2 * nbias
    body = nb * in_size + NL * nh * conv_size
    wide = body + 2 * nbias
    vmem = pl.BlockSpec(memory_space=pltpu.VMEM)
    smem = pl.BlockSpec(memory_space=pltpu.SMEM)
    hbm = pl.BlockSpec(memory_space=pl.ANY)
    params = pltpu.CompilerParams(vmem_limit_bytes=50 * 2**20)
    score, mine, other, dpre = pl.pallas_call(
        functools.partial(step_kernel, dims),
        out_shape=[
            sds((8, LANES), F32),
            sds((peers, conv_wide, LANES), BF),
            sds((peers, conv_wide, LANES), BF),
            sds((rows, ch), BF),
        ],
        in_specs=[smem, vmem, vmem, vmem, hbm, hbm, hbm, hbm],
        out_specs=[vmem] * 4,
        scratch_shapes=[
            pltpu.VMEM((3, ch, ch), F32),
            pltpu.VMEM((4 * ch, ch), BF),
            pltpu.VMEM(hid.shape, BF),
            pltpu.VMEM(sq.shape, F32),
            pltpu.VMEM(squash0.shape, F32),
            pltpu.VMEM(w_conv.shape, BF),
            pltpu.SemaphoreType.DMA((4,)),
        ],
        compiler_params=params,
    )(info, cov, swap_core(cov), mean_all, hid, sq, squash0, w_conv)
    steps = 4
    group = peers // steps
    tile = group * in_size
    whole = pl.BlockSpec((rows, ch), lambda i, at: (0, 0))
    conv_spec = pl.BlockSpec((group, conv_wide, LANES), lambda i, at: (i, 0, 0))
    packed = pl.pallas_call(
        functools.partial(pack_kernel, nbias),
        grid_spec=pltpu.PrefetchScalarGridSpec(
            num_scalar_prefetch=1,
            grid=(steps,),
            in_specs=[
                pl.BlockSpec((rows, tile), lambda i, at: (0, at[0] * steps + i)),
                pl.BlockSpec((rows, tile), lambda i, at: (0, i)),
                whole,
                whole,
                conv_spec,
                conv_spec,
            ],
            out_specs=pl.BlockSpec((group, wide, LANES), lambda i, at: (i, 0, 0)),
        ),
        out_shape=sds((peers, wide, LANES), BF),
        compiler_params=params,
    )(info, frames, frames_got, dpre, swap_core(dpre), mine, swap_core(other))
    arrived = exchange(packed)
    block = 32
    full, bias = pl.pallas_call(
        sum_kernel,
        grid=(body // block,),
        out_shape=[sds((peers, body, LANES), BF), sds((nbias, LANES), F32)],
        in_specs=[
            pl.BlockSpec((peers, block, LANES), lambda i: (0, i, 0)),
            pl.BlockSpec((peers, 2 * nbias, LANES), lambda i: (0, body // (2 * nbias), 0)),
        ],
        out_specs=[
            pl.BlockSpec((peers, block, LANES), lambda i: (0, i, 0)),
            pl.BlockSpec((nbias, LANES), lambda i: (0, 0)),
        ],
        compiler_params=params,
    )(arrived, arrived)
    bias_got = swap_core(bias)
    full = exchange(full)
    steps = 8
    group = peers // steps

    def unpack(chunks, at, earlier):
        return pl.pallas_call(
            functools.partial(unpack_kernel, (in_size, conv_size, nb)),
            grid_spec=pltpu.PrefetchScalarGridSpec(
                num_scalar_prefetch=1,
                grid=(steps,),
                in_specs=[pl.BlockSpec((group, body, LANES), lambda i, at: (i, 0, 0))]
                + [hbm] * len(earlier),
                out_specs=[
                    pl.BlockSpec((1, group * in_size, ch), lambda i, at: (at[0], i, 0)),
                    pl.BlockSpec((NL, group * conv_size, ch // 2), lambda i, at: (0, i, at[0])),
                ],
            ),
            out_shape=[sds((2, half_features, ch), F32), sds((NL, 2 * ch, ch), F32)],
            input_output_aliases={2 + n: n for n in range(len(earlier))},
            compiler_params=params,
            cost_estimate=pl.CostEstimate(flops=0, bytes_accessed=12 * 2**20, transcendentals=0),
        )(at, chunks, *earlier)

    got = swap_core(full)
    partial = unpack(full, info[:1], [])
    g_in, g_conv = unpack(got, 1 - info[:1], partial)
    both = jnp.where(core == 0, jnp.stack([bias, bias_got]), jnp.stack([bias_got, bias]))
    g_bias = both.reshape(2, nh, NL + 1, LANES).transpose(2, 0, 1, 3).reshape(NL + 1, ch)
    return score[0, 0], g_in.reshape(features, ch), g_bias[0], g_conv, g_bias[1:]


def solution(mesh):
    devices = mesh.devices
    trajs, segments = devices.shape
    inner = Mesh(devices.reshape(trajs // 2, 2, segments), ("x", "c", "tm"))
    return jax.shard_map(
        per_device,
        mesh=inner,
        in_specs=(P(("x", "c"), "tm", None), P(), P(), P(), P()),
        out_specs=(P(), P(), P(), P(), P()),
        check_vma=False,
    )
```

```python
import functools

import jax
import jax.numpy as jnp
from jax import lax
from jax.experimental import pallas as pl
from jax.experimental.pallas import tpu as pltpu
from jax.sharding import Mesh, PartitionSpec as P

NL = 3
LAG = 16
RIDGE = 0.0001
HALO = 32
LANES = 128
BF = jnp.bfloat16
F32 = jnp.float32
PEERS = ("x", "tm")
HI = lax.Precision.HIGHEST
C0, C1, C2, C3, C4 = 2.25, -2.4375, 1.6875, -0.5625, 0.0625

NN = (((1,), (0,)), ((), ()))
NT = (((1,), (1,)), ((), ()))
TN = (((0,), (0,)), ((), ()))


def dot(a, b, dims=NN, precision=None):
    return lax.dot_general(a, b, dims, precision=precision, preferred_element_type=F32)


def split(a):
    hi = a.astype(BF)
    return hi, (a - hi.astype(F32)).astype(BF)


def dot3(a, b, dims=NN):
    return dot(a[0], b[0], dims) + (dot(a[0], b[1], dims) + dot(a[1], b[0], dims))


def swap_core(value):
    return lax.ppermute(value, "c", [(0, 1), (1, 0)])


def shift_segment(value, steps):
    count = lax.axis_size("tm")
    first, last = max(0, -steps), min(count, count - steps)
    return lax.ppermute(value, "tm", [(i, i + steps) for i in range(first, last)])


def exchange(value):
    return lax.all_to_all(value, PEERS, 0, 0, tiled=True)


def call(kernel, outs, *args, scratch=(), vmem=16):
    specs = [
        pl.BlockSpec(memory_space=pltpu.SMEM if a.dtype == jnp.int32 else pltpu.VMEM) for a in args
    ]
    return pl.pallas_call(
        kernel,
        out_shape=outs,
        in_specs=specs,
        out_specs=[pl.BlockSpec(memory_space=pltpu.VMEM) for _ in outs],
        scratch_shapes=list(scratch),
        compiler_params=pltpu.CompilerParams(vmem_limit_bytes=vmem * 2**20),
    )(*args)


def sds(shape, dtype):
    return jax.ShapeDtypeStruct(shape, dtype)


def forward_kernel(dims, info, before, own, after, w, b, hid, sq, mine, other, means, mom):
    rows, ch, length, peers, piece = dims
    core, segment = info[0], info[1]
    ext = rows + 2 * HALO
    nb = ch // LANES
    t = segment * rows - HALO + lax.broadcasted_iota(jnp.int32, (ext, 1), 0)
    h = jnp.concatenate(
        [before[...].astype(F32), own[...].astype(F32), after[...].astype(F32)], axis=0
    )
    for layer in range(NL):
        hb = h.astype(BF)
        hid[layer] = hb
        hist = pltpu.roll(h, 2**layer, 0).astype(BF)
        s = jnp.tanh(dot(hb, w[layer, :ch]) + dot(hist, w[layer, ch:]) + b[layer : layer + 1])
        sq[layer] = s
        h = jnp.where(t >= 0, (h + s).astype(BF).astype(F32), 0.0)
    hid[NL] = h.astype(BF)
    tp = segment * rows + lax.broadcasted_iota(jnp.int32, (rows, 1), 0)
    pair = jnp.where(tp < length - LAG, 1.0, 0.0).astype(F32)
    last = segment == length // rows - 1
    count = jnp.where(last, rows - LAG, rows).astype(F32)
    early = h[HALO : HALO + rows] * pair
    later = h[HALO + LAG : HALO + LAG + rows] * pair
    mean_e = jnp.sum(early, axis=0, keepdims=True) / count
    mean_l = jnp.sum(later, axis=0, keepdims=True) / count
    means[...] = jnp.concatenate([mean_e, mean_l, jnp.zeros((6, ch), F32)], axis=0)
    ce = split((early - mean_e) * pair)
    cl = split((later - mean_l) * pair)
    left_e = jnp.concatenate([ce[0], ce[0], ce[1]], axis=0)
    left_l = jnp.concatenate([cl[0], cl[0], cl[1]], axis=0)
    right_e = jnp.concatenate([ce[0], ce[1], ce[0]], axis=0)
    right_l = jnp.concatenate([cl[0], cl[1], cl[0]], axis=0)
    mom[0] = dot(left_e, right_e, TN)
    mom[1] = dot(left_e, right_l, TN)
    mom[2] = dot(left_l, right_l, TN)
    half = ch // 2

    def pack(i, carry):
        at = pl.multiple_of(core * half + i * piece, piece)
        to = pl.multiple_of((1 - core) * half + i * piece, piece)
        for m in range(3):
            for j in range(nb):
                cols = slice(j * LANES, (j + 1) * LANES)
                put = slice(m * piece, (m + 1) * piece)
                mine[i * nb + j, put, :] = mom[m, pl.ds(at, piece), cols]
                other[i * nb + j, put, :] = mom[m, pl.ds(to, piece), cols].astype(BF)
        return carry

    lax.fori_loop(0, peers // nb, pack, 0)


def pair_kernel(dims, info, mine, got, means, sib, packed, turned):
    rows, ch, length, peers, piece = dims
    core, segment = info[0], info[1]
    nb = ch // LANES
    half = ch // 2
    last = segment == length // rows - 1
    weight = 0.5 * jnp.where(last, rows - LAG, rows).astype(F32)
    gap = means[...] - sib[...]
    mid = 0.5 * (means[...] + sib[...])
    turned[...] = gap.T * weight
    hi, lo = split(mid)
    tail = []
    for part in (hi.astype(F32), lo.astype(F32)):
        for k in range(2):
            for j in range(nb):
                tail.append(part[k : k + 1, j * LANES : (j + 1) * LANES])
    tail = jnp.concatenate(tail, axis=0).astype(BF)

    def pack(i, carry):
        at = pl.multiple_of(core * half + i * piece, piece)
        col = turned[pl.ds(at, piece), :]
        for j in range(nb):
            cols = slice(j * LANES, (j + 1) * LANES)
            p = i * nb + j
            for m, (a, c) in enumerate(((0, 0), (0, 1), (1, 1))):
                put = slice(m * piece, (m + 1) * piece)
                value = mine[p, put, :] + got[p, put, :].astype(F32)
                value = value + col[:, a : a + 1] * gap[c : c + 1, cols]
                packed[p, put, :] = value.astype(BF)
            packed[p, 3 * piece :, :] = tail
        return carry

    lax.fori_loop(0, peers // nb, pack, 0)


def merge_kernel(dims, info, arrived, cov, mean_all, flat, dev, square):
    rows, ch, length, peers, piece = dims
    core, peer = info[0], info[2]
    nb = ch // LANES
    segments = length // rows
    total = 2 * (peers // segments) * (length - LAG)
    body = 3 * piece

    def add(p, acc):
        z = arrived[p, body:, :].astype(F32)
        flat[pl.ds(pl.multiple_of(p * 2 * nb, 2 * nb), 2 * nb), :] = z[: 2 * nb] + z[2 * nb :]
        return acc + arrived[p, :body, :].astype(F32)

    within = lax.fori_loop(0, peers, add, jnp.zeros((body, LANES), F32))
    seg = lax.rem(lax.broadcasted_iota(jnp.int32, (peers, 1), 0), segments)
    counts = 2.0 * jnp.where(seg == segments - 1, rows - LAG, rows).astype(F32)
    mean_all[...] = jnp.zeros_like(mean_all)
    for k in range(2):
        for j in range(nb):
            cols = slice(j * LANES, (j + 1) * LANES)
            v = flat[pl.ds(k * nb + j, peers, stride=2 * nb), :]
            mean = jnp.sum(v * counts, axis=0, keepdims=True) / total
            mean_all[k : k + 1, cols] = mean
            dev[k, :, cols] = v - mean
    start = core * (ch // 2) + (peer // nb) * piece
    block = pl.multiple_of((start // LANES) * LANES, LANES)
    inside = pl.multiple_of(lax.rem(start, LANES), piece)
    here = pl.multiple_of(lax.rem(peer, nb) * LANES, LANES)
    for m, (a, c) in enumerate(((0, 0), (0, 1), (1, 1))):
        left = dev[a, :, pl.ds(block, LANES)] * counts
        square[m] = dot(left, dev[c, :, pl.ds(here, LANES)], TN, HI)
    between = jnp.concatenate([square[m, pl.ds(inside, piece), :] for m in range(3)], axis=0)
    value = ((within + between) / total).astype(BF)
    cov[...] = jnp.broadcast_to(value[None], cov.shape)


def step_kernel(
    dims, info, half_cov, other_cov, mean_all, hid_hbm, sq_hbm, sq0_hbm, w_hbm,
    score, mine, other, dpre, cov, grads, hid, sq, sq0, w, sems,
):
    rows, ch, length, peers, piece = dims
    core = info[0]
    nb = ch // LANES
    half = ch // 2
    loads = [
        pltpu.make_async_copy(src, dst, sems.at[n])
        for n, (src, dst) in enumerate(((hid_hbm, hid), (sq_hbm, sq), (sq0_hbm, sq0), (w_hbm, w)))
    ]
    for load in loads:
        load.start()

    def place(i, carry):
        at = pl.multiple_of(core * half + i * piece, piece)
        to = pl.multiple_of((1 - core) * half + i * piece, piece)
        for m in range(3):
            for j in range(nb):
                cols = slice(j * LANES, (j + 1) * LANES)
                put = slice(m * piece, (m + 1) * piece)
                cov[m, pl.ds(at, piece), cols] = half_cov[i * nb + j, put, :].astype(F32)
                cov[m, pl.ds(to, piece), cols] = other_cov[i * nb + j, put, :].astype(F32)
        return carry

    lax.fori_loop(0, peers // nb, place, 0)
    row = lax.broadcasted_iota(jnp.int32, (ch, ch), 0)
    col = lax.broadcasted_iota(jnp.int32, (ch, ch), 1)
    unit = jnp.where(row == col, 1.0, 0.0).astype(F32)

    def forward(matrix):
        shifted = matrix + RIDGE * unit
        square = jnp.sum(shifted * shifted, keepdims=True)
        inv_scale = lax.rsqrt(square)
        a = shifted * inv_scale
        ab = a.astype(BF)
        a2 = dot(ab, ab)
        a2b = a2.astype(BF)
        poly = C0 * unit + C1 * a + C2 * a2 + dot(a2b, (C3 * a + C4 * a2).astype(BF))
        root = jnp.sqrt(inv_scale)
        return a, ab, a2b, poly, inv_scale, root, split(poly * root)

    def backward(a, ab, a2b, poly, inv_scale, root, grad):
        dscale = -0.5 * jnp.sum(grad * poly, keepdims=True) * root * inv_scale
        g = grad * root
        gb = g.astype(BF)
        y = dot(gb, ab)
        x = dot(a2b, gb)
        xs = x + x.T
        h = C2 * g + (0.5 * C3) * (y + y.T) + C4 * xs
        z = dot(ab, h.astype(BF))
        da = C1 * g + (0.5 * C3) * xs + z + z.T
        dscale = dscale - jnp.sum(da * a, keepdims=True) * inv_scale
        return da * inv_scale + dscale * a

    fe = forward(cov[0])
    fl = forward(cov[2])
    re, rl = fe[6], fl[6]
    c = split(cov[1])
    u = split(dot3(re, c))
    v = dot(c[0], rl[0]).astype(BF)
    k = dot3(u, rl)
    score[...] = jnp.broadcast_to(1.0 + jnp.sum(k * k, keepdims=True), score.shape)
    k2 = split(2.0 * k)
    gc = dot3(split(dot3(re, k2)), rl)
    grads[ch : 2 * ch] = gc.T.astype(BF)
    grads[2 * ch : 3 * ch] = gc.astype(BF)
    gre = dot(k2[0], v, NT)
    grads[:ch] = backward(*fe[:6], gre + gre.T).astype(BF)
    grl = dot(u[0], k2[0], TN)
    grads[3 * ch :] = backward(*fl[:6], grl + grl.T).astype(BF)
    for load in loads:
        load.wait()
    conv_backward(dims, info, hid, sq, sq0, w, grads, mean_all, mine, other, dpre)


def conv_backward(dims, info, hid, sq, sq0, w, grads, mean_all, mine, other, dpre):
    rows, ch, length, peers, piece = dims
    core, segment = info[0], info[1]
    segments = length // rows
    half = ch // 2
    nh = half // LANES
    total = 2 * (peers // segments) * (length - LAG)
    grows = rows + 16
    t = segment * rows + lax.broadcasted_iota(jnp.int32, (grows, 1), 0)
    has_early = t < length - LAG
    has_later = jnp.logical_and(t >= LAG, t < length)
    out = hid[NL].astype(F32)
    base = out[HALO : HALO + grows]
    mean_e, mean_l = mean_all[0:1], mean_all[1:2]
    zero = jnp.zeros((1, ch), F32)
    consts = []
    for early_on in (True, False):
        left_e, left_l = mean_e, mean_l
        for _ in range(3):
            top_e, top_l = left_e.astype(BF).astype(F32), left_l.astype(BF).astype(F32)
            parts = [top_e, top_l, zero, zero] if early_on else [zero, zero, top_e, top_l]
            consts.append(jnp.concatenate(parts, axis=1))
            left_e, left_l = left_e - top_e, left_l - top_l
    consts = jnp.concatenate(consts + [jnp.zeros((10, 4 * ch), F32)], axis=0)
    lhs = jnp.concatenate(
        [
            jnp.where(has_early, base, 0.0),
            jnp.where(has_early, out[HALO + LAG : HALO + LAG + grows], 0.0),
            jnp.where(has_later, out[HALO - LAG : HALO - LAG + grows], 0.0),
            jnp.where(has_later, base, 0.0),
        ],
        axis=1,
    )
    lhs = jnp.concatenate([lhs, consts], axis=0).astype(BF)
    grad = dot(lhs, grads[...])
    off_early = grad[grows : grows + 1] + grad[grows + 1 : grows + 2] + grad[grows + 2 : grows + 3]
    off_later = grad[grows + 3 : grows + 4] + grad[grows + 4 : grows + 5] + grad[grows + 5 : grows + 6]
    grad = grad[:grows] - jnp.where(has_early, off_early, 0.0) - jnp.where(has_later, off_later, 0.0)
    grad = grad / total
    biases = [None] * (NL + 1)
    first = core == 0

    def halves(value):
        lo, hi = value[:, :half], value[:, half:]
        return jnp.where(first, lo, hi), jnp.where(first, hi, lo)

    def store(left, value, p0, count, size, at):
        for part, ref in zip(halves(value), (mine, other)):
            res = dot(left, part.astype(BF), TN).astype(BF)
            for j in range(nh):
                piece_j = res[:, j * LANES : (j + 1) * LANES].reshape(count, size, LANES)
                ref[p0 : p0 + count, at + j * size : at + (j + 1) * size, :] = piece_j

    conv_size = 2 * ch // peers
    for layer in reversed(range(NL)):
        step = 2**layer
        s = sq[layer, HALO : HALO + grows, :]
        pre = jnp.where(t < length, grad * (1.0 - s * s), 0.0).astype(BF)
        own = pre[:rows].astype(F32)
        biases[layer + 1] = jnp.sum(own, axis=0, keepdims=True)
        h = hid[layer].astype(F32)
        hist = pltpu.roll(h, step, 0)[HALO : HALO + rows].astype(BF)
        at = layer * nh * conv_size
        count = ch // conv_size
        store(hid[layer, HALO : HALO + rows, :], own, 0, count, conv_size, at)
        store(hist, own, count, count, conv_size, at)
        back = dot(pre, w[layer, ch:], NT)
        grad = grad + dot(pre, w[layer, :ch], NT) + pltpu.roll(back, grows - step, 0)
    s = sq0[...]
    own = (grad[:rows] * (1.0 - s * s)).astype(BF)
    dpre[...] = own
    biases[0] = jnp.sum(own.astype(F32), axis=0, keepdims=True)
    bias = jnp.concatenate(biases, axis=0)
    for part, ref in zip(halves(bias), (mine, other)):
        hi, lo = split(part)
        tail = []
        for value in (hi.astype(F32), lo.astype(F32)):
            for j in range(nh):
                tail.append(value[:, j * LANES : (j + 1) * LANES])
        tail = jnp.concatenate(tail, axis=0).astype(BF)
        at = ref.shape[1] - tail.shape[0]
        ref[:, at:, :] = jnp.broadcast_to(tail[None], (peers,) + tail.shape)


def pack_kernel(nbias, info, left, left_got, dpre, dpre_got, mine, got, packed):
    count = packed.shape[0]
    ch = dpre.shape[1]
    size = left.shape[1] // count
    lhs = jnp.concatenate([left[...], left_got[...]], axis=0)
    res = dot(lhs, jnp.concatenate([dpre[...], dpre_got[...]], axis=0), TN).astype(BF)
    for j in range(ch // LANES):
        part = res[:, j * LANES : (j + 1) * LANES].reshape(count, size, LANES)
        packed[:, j * size : (j + 1) * size, :] = part
    at = size * (ch // LANES)
    body = mine.shape[1] - 2 * nbias
    value = mine[...].astype(F32) + got[...].astype(F32)
    packed[:, at : at + body, :] = value[:, :body].astype(BF)
    bias = value[0, body : body + nbias] + value[0, body + nbias :]
    hi = bias.astype(BF).astype(F32)
    tail = jnp.concatenate([hi, bias - hi], axis=0).astype(BF)
    packed[:, at + body :, :] = jnp.broadcast_to(tail[None], (count,) + tail.shape)


def sum_kernel(arrived, tails, full, bias):
    peers = arrived.shape[0]

    def add(p, acc):
        return acc + arrived[p].astype(F32)

    value = lax.fori_loop(0, peers, add, jnp.zeros(arrived.shape[1:], F32), unroll=4)
    full[...] = jnp.broadcast_to(value.astype(BF)[None], full.shape)

    @pl.when(pl.program_id(0) == 0)
    def _():
        def add_tail(p, acc):
            return acc + tails[p].astype(F32)

        t = lax.fori_loop(0, peers, add_tail, jnp.zeros(tails.shape[1:], F32))
        n = t.shape[0] // 2
        bias[...] = t[:n] + t[n:]


def unpack_kernel(sizes, nbiases, info, chunks, *refs):
    in_size, conv_size, nb = sizes
    if nbiases:
        bias, bias_got = refs[:2]
        w_in, w_conv, b_in, b_conv = refs[-4:]
    else:
        w_in, w_conv = refs[-2:]
    count = chunks.shape[0]
    for j in range(nb):
        part = chunks[:, j * in_size : (j + 1) * in_size, :].astype(F32)
        w_in[0, :, j * LANES : (j + 1) * LANES] = part.reshape(count * in_size, LANES)
    for layer in range(NL):
        for j in range(nb // 2):
            at = nb * in_size + (layer * (nb // 2) + j) * conv_size
            part = chunks[:, at : at + conv_size, :].astype(F32)
            w_conv[layer, :, j * LANES : (j + 1) * LANES] = part.reshape(count * conv_size, LANES)
    if nbiases:

        @pl.when(pl.program_id(0) == 0)
        def _():
            swapped = info[0] == 0
            n = NL + 1
            rows = []
            for side in range(2):
                keep = bias_got[...] if side == 0 else bias[...]
                swap = bias[...] if side == 0 else bias_got[...]
                value = jnp.where(swapped, keep, swap)
                rows += [value[j * n : (j + 1) * n] for j in range(nb // 2)]
            full = jnp.concatenate(rows, axis=1)
            b_in[...] = full[0]
            b_conv[...] = full[1:]


def per_device(frames, w_in, b_in, w_conv, b_conv):
    frames = frames[0]
    rows, features = frames.shape
    ch = w_in.shape[1]
    core = lax.axis_index("c")
    segment = lax.axis_index("tm")
    segments = lax.axis_size("tm")
    peers = lax.axis_size("x") * segments
    length = rows * segments
    nb = ch // LANES
    nh = nb // 2
    piece = (ch // 2) * nb // peers
    dims = (rows, ch, length, peers, piece)
    info = jnp.stack([core, segment, lax.axis_index("x") * segments + segment]).astype(jnp.int32)
    ext = rows + 2 * HALO
    frames_got = swap_core(
        lax.dynamic_slice_in_dim(frames, (1 - core) * (features // 2), features // 2, 1)
    )

    squash0 = jnp.tanh(jnp.dot(frames, w_in, preferred_element_type=F32) + b_in)
    own = squash0.astype(BF)
    before = shift_segment(own[rows - HALO :], 1)
    after = shift_segment(own[:HALO], -1)
    before, after, frames_got = lax.optimization_barrier((before, after, frames_got))
    hid, sq, mine, other, means = call(
        functools.partial(forward_kernel, dims),
        [
            sds((NL + 1, ext, ch), BF),
            sds((NL, ext, ch), F32),
            sds((peers, 3 * piece, LANES), F32),
            sds((peers, 3 * piece, LANES), BF),
            sds((8, ch), F32),
        ],
        info, before, own, after, w_conv, b_conv,
        scratch=[pltpu.VMEM((3, ch, ch), F32)],
        vmem=36,
    )
    (packed,) = call(
        functools.partial(pair_kernel, dims),
        [sds((peers, 3 * piece + 4 * nb, LANES), BF)],
        info, mine, swap_core(other), means, swap_core(means),
        scratch=[pltpu.VMEM((ch, 8), F32)],
    )
    cov, mean_all = call(
        functools.partial(merge_kernel, dims),
        [sds((peers, 3 * piece, LANES), BF), sds((8, ch), F32)],
        info, exchange(packed),
        scratch=[
            pltpu.VMEM((peers * 2 * nb, LANES), F32),
            pltpu.VMEM((2, peers, ch), F32),
            pltpu.VMEM((3, LANES, LANES), F32),
        ],
    )
    cov = exchange(cov)
    half_features = features // 2
    in_size = half_features // peers
    conv_size = 2 * ch // peers
    nbias = (NL + 1) * nh
    conv_wide = NL * nh * conv_size + 2 * nbias
    body = nb * in_size + NL * nh * conv_size
    wide = body + 2 * nbias
    vmem = pl.BlockSpec(memory_space=pltpu.VMEM)
    smem = pl.BlockSpec(memory_space=pltpu.SMEM)
    hbm = pl.BlockSpec(memory_space=pl.ANY)
    params = pltpu.CompilerParams(vmem_limit_bytes=50 * 2**20)
    small_params = pltpu.CompilerParams(vmem_limit_bytes=16 * 2**20)
    score, mine, other, dpre = pl.pallas_call(
        functools.partial(step_kernel, dims),
        out_shape=[
            sds((8, LANES), F32),
            sds((peers, conv_wide, LANES), BF),
            sds((peers, conv_wide, LANES), BF),
            sds((rows, ch), BF),
        ],
        in_specs=[smem, vmem, vmem, vmem, hbm, hbm, hbm, hbm],
        out_specs=[vmem] * 4,
        scratch_shapes=[
            pltpu.VMEM((3, ch, ch), F32),
            pltpu.VMEM((4 * ch, ch), BF),
            pltpu.VMEM(hid.shape, BF),
            pltpu.VMEM(sq.shape, F32),
            pltpu.VMEM(squash0.shape, F32),
            pltpu.VMEM(w_conv.shape, BF),
            pltpu.SemaphoreType.DMA((4,)),
        ],
        compiler_params=params,
    )(info, cov, swap_core(cov), mean_all, hid, sq, squash0, w_conv)
    steps = 4
    group = peers // steps
    tile = group * in_size
    whole = pl.BlockSpec((rows, ch), lambda i, at: (0, 0))
    conv_spec = pl.BlockSpec((group, conv_wide, LANES), lambda i, at: (i, 0, 0))
    packed = pl.pallas_call(
        functools.partial(pack_kernel, nbias),
        grid_spec=pltpu.PrefetchScalarGridSpec(
            num_scalar_prefetch=1,
            grid=(steps,),
            in_specs=[
                pl.BlockSpec((rows, tile), lambda i, at: (0, at[0] * steps + i)),
                pl.BlockSpec((rows, tile), lambda i, at: (0, i)),
                whole,
                whole,
                conv_spec,
                conv_spec,
            ],
            out_specs=pl.BlockSpec((group, wide, LANES), lambda i, at: (i, 0, 0)),
        ),
        out_shape=sds((peers, wide, LANES), BF),
        compiler_params=small_params,
    )(info, frames, frames_got, dpre, swap_core(dpre), mine, swap_core(other))
    arrived = exchange(packed)
    block = 32
    full, bias = pl.pallas_call(
        sum_kernel,
        grid=(body // block,),
        out_shape=[sds((peers, body, LANES), BF), sds((nbias, LANES), F32)],
        in_specs=[
            pl.BlockSpec((peers, block, LANES), lambda i: (0, i, 0)),
            pl.BlockSpec((peers, 2 * nbias, LANES), lambda i: (0, body // (2 * nbias), 0)),
        ],
        out_specs=[
            pl.BlockSpec((peers, block, LANES), lambda i: (0, i, 0)),
            pl.BlockSpec((nbias, LANES), lambda i: (0, 0)),
        ],
        compiler_params=small_params,
    )(arrived, arrived)
    bias_got = swap_core(bias)
    full = exchange(full)
    steps = 8
    group = peers // steps

    def unpack(chunks, at, biases, earlier):
        spare = [sds((ch,), F32), sds((NL, ch), F32)] if biases else []
        return pl.pallas_call(
            functools.partial(unpack_kernel, (in_size, conv_size, nb), len(biases)),
            grid_spec=pltpu.PrefetchScalarGridSpec(
                num_scalar_prefetch=1,
                grid=(steps,),
                in_specs=[pl.BlockSpec((group, body, LANES), lambda i, at: (i, 0, 0))]
                + [pl.BlockSpec(b.shape, lambda i, at: (0, 0)) for b in biases]
                + [hbm] * len(earlier),
                out_specs=[
                    pl.BlockSpec((1, group * in_size, ch), lambda i, at: (at[0], i, 0)),
                    pl.BlockSpec((NL, group * conv_size, ch // 2), lambda i, at: (0, i, at[0])),
                ]
                + [pl.BlockSpec(b.shape, lambda i, at, n=len(b.shape): (0,) * n) for b in spare],
            ),
            out_shape=[sds((2, half_features, ch), F32), sds((NL, 2 * ch, ch), F32)] + spare,
            input_output_aliases={2 + len(biases) + n: n for n in range(len(earlier))},
            compiler_params=small_params,
            cost_estimate=pl.CostEstimate(flops=0, bytes_accessed=12 * 2**20, transcendentals=0),
        )(at, chunks, *biases, *earlier)

    got = swap_core(full)
    partial = unpack(full, info[:1], [], [])
    got, bias_got = lax.optimization_barrier((got, bias_got))
    g_in, g_conv, g_b_in, g_b_conv = unpack(got, 1 - info[:1], [bias, bias_got], partial)
    return score[0, 0], g_in.reshape(features, ch), g_b_in, g_conv, g_b_conv


def solution(mesh):
    devices = mesh.devices
    trajs, segments = devices.shape
    inner = Mesh(devices.reshape(trajs // 2, 2, segments), ("x", "c", "tm"))
    return jax.shard_map(
        per_device,
        mesh=inner,
        in_specs=(P(("x", "c"), "tm", None), P(), P(), P(), P()),
        out_specs=(P(), P(), P(), P(), P()),
        check_vma=False,
    )
```

```python
import functools

import jax
import jax.numpy as jnp
from jax import lax
from jax.experimental import pallas as pl
from jax.experimental.pallas import tpu as pltpu
from jax.sharding import Mesh, PartitionSpec as P

NL = 3
LAG = 16
RIDGE = 0.0001
HALO = 32
LANES = 128
BF = jnp.bfloat16
F32 = jnp.float32
PEERS = ("x", "tm")
HI = lax.Precision.HIGHEST
C0, C1, C2, C3, C4 = 2.25, -2.4375, 1.6875, -0.5625, 0.0625

NN = (((1,), (0,)), ((), ()))
NT = (((1,), (1,)), ((), ()))
TN = (((0,), (0,)), ((), ()))


def dot(a, b, dims=NN, precision=None):
    return lax.dot_general(a, b, dims, precision=precision, preferred_element_type=F32)


def split(a):
    hi = a.astype(BF)
    return hi, (a - hi.astype(F32)).astype(BF)


def dot3(a, b, dims=NN):
    return dot(a[0], b[0], dims) + (dot(a[0], b[1], dims) + dot(a[1], b[0], dims))


def swap_core(value):
    return lax.ppermute(value, "c", [(0, 1), (1, 0)])


def shift_segment(value, steps):
    count = lax.axis_size("tm")
    first, last = max(0, -steps), min(count, count - steps)
    return lax.ppermute(value, "tm", [(i, i + steps) for i in range(first, last)])


def exchange(value):
    return lax.all_to_all(value, PEERS, 0, 0, tiled=True)


def call(kernel, outs, *args, scratch=(), vmem=16):
    specs = [
        pl.BlockSpec(memory_space=pltpu.SMEM if a.dtype == jnp.int32 else pltpu.VMEM) for a in args
    ]
    return pl.pallas_call(
        kernel,
        out_shape=outs,
        in_specs=specs,
        out_specs=[pl.BlockSpec(memory_space=pltpu.VMEM) for _ in outs],
        scratch_shapes=list(scratch),
        compiler_params=pltpu.CompilerParams(vmem_limit_bytes=vmem * 2**20),
    )(*args)


def sds(shape, dtype):
    return jax.ShapeDtypeStruct(shape, dtype)


def forward_kernel(dims, info, before, own, after, w, b, hid, sq, mine, other, means, mom):
    rows, ch, length, peers, piece = dims
    core, segment = info[0], info[1]
    ext = rows + 2 * HALO
    nb = ch // LANES
    t = segment * rows - HALO + lax.broadcasted_iota(jnp.int32, (ext, 1), 0)
    h = jnp.concatenate(
        [before[...].astype(F32), own[...].astype(F32), after[...].astype(F32)], axis=0
    )
    for layer in range(NL):
        hb = h.astype(BF)
        hid[layer] = hb
        hist = pltpu.roll(h, 2**layer, 0).astype(BF)
        s = jnp.tanh(dot(hb, w[layer, :ch]) + dot(hist, w[layer, ch:]) + b[layer : layer + 1])
        sq[layer] = s
        h = jnp.where(t >= 0, (h + s).astype(BF).astype(F32), 0.0)
    hid[NL] = h.astype(BF)
    tp = segment * rows + lax.broadcasted_iota(jnp.int32, (rows, 1), 0)
    pair = jnp.where(tp < length - LAG, 1.0, 0.0).astype(F32)
    last = segment == length // rows - 1
    count = jnp.where(last, rows - LAG, rows).astype(F32)
    early = h[HALO : HALO + rows] * pair
    later = h[HALO + LAG : HALO + LAG + rows] * pair
    mean_e = jnp.sum(early, axis=0, keepdims=True) / count
    mean_l = jnp.sum(later, axis=0, keepdims=True) / count
    means[...] = jnp.concatenate([mean_e, mean_l, jnp.zeros((6, ch), F32)], axis=0)
    ce = split((early - mean_e) * pair)
    cl = split((later - mean_l) * pair)
    left_e = jnp.concatenate([ce[0], ce[0], ce[1]], axis=0)
    left_l = jnp.concatenate([cl[0], cl[0], cl[1]], axis=0)
    right_e = jnp.concatenate([ce[0], ce[1], ce[0]], axis=0)
    right_l = jnp.concatenate([cl[0], cl[1], cl[0]], axis=0)
    mom[0] = dot(left_e, right_e, TN)
    mom[1] = dot(left_e, right_l, TN)
    mom[2] = dot(left_l, right_l, TN)
    half = ch // 2

    def pack(i, carry):
        at = pl.multiple_of(core * half + i * piece, piece)
        to = pl.multiple_of((1 - core) * half + i * piece, piece)
        for m in range(3):
            for j in range(nb):
                cols = slice(j * LANES, (j + 1) * LANES)
                put = slice(m * piece, (m + 1) * piece)
                mine[i * nb + j, put, :] = mom[m, pl.ds(at, piece), cols]
                other[i * nb + j, put, :] = mom[m, pl.ds(to, piece), cols].astype(BF)
        return carry

    lax.fori_loop(0, peers // nb, pack, 0)


def pair_kernel(dims, info, mine, got, means, sib, packed, turned):
    rows, ch, length, peers, piece = dims
    core, segment = info[0], info[1]
    nb = ch // LANES
    half = ch // 2
    last = segment == length // rows - 1
    weight = 0.5 * jnp.where(last, rows - LAG, rows).astype(F32)
    gap = means[...] - sib[...]
    mid = 0.5 * (means[...] + sib[...])
    turned[...] = gap.T * weight
    hi, lo = split(mid)
    tail = []
    for part in (hi.astype(F32), lo.astype(F32)):
        for k in range(2):
            for j in range(nb):
                tail.append(part[k : k + 1, j * LANES : (j + 1) * LANES])
    tail = jnp.concatenate(tail, axis=0).astype(BF)

    def pack(i, carry):
        at = pl.multiple_of(core * half + i * piece, piece)
        col = turned[pl.ds(at, piece), :]
        for j in range(nb):
            cols = slice(j * LANES, (j + 1) * LANES)
            p = i * nb + j
            for m, (a, c) in enumerate(((0, 0), (0, 1), (1, 1))):
                put = slice(m * piece, (m + 1) * piece)
                value = mine[p, put, :] + got[p, put, :].astype(F32)
                value = value + col[:, a : a + 1] * gap[c : c + 1, cols]
                packed[p, put, :] = value.astype(BF)
            packed[p, 3 * piece :, :] = tail
        return carry

    lax.fori_loop(0, peers // nb, pack, 0)


def merge_kernel(dims, info, arrived, cov, mean_all, flat, dev, square):
    rows, ch, length, peers, piece = dims
    core, peer = info[0], info[2]
    nb = ch // LANES
    segments = length // rows
    total = 2 * (peers // segments) * (length - LAG)
    body = 3 * piece

    def add(p, acc):
        z = arrived[p, body:, :].astype(F32)
        flat[pl.ds(pl.multiple_of(p * 2 * nb, 2 * nb), 2 * nb), :] = z[: 2 * nb] + z[2 * nb :]
        return acc + arrived[p, :body, :].astype(F32)

    within = lax.fori_loop(0, peers, add, jnp.zeros((body, LANES), F32))
    seg = lax.rem(lax.broadcasted_iota(jnp.int32, (peers, 1), 0), segments)
    counts = 2.0 * jnp.where(seg == segments - 1, rows - LAG, rows).astype(F32)
    mean_all[...] = jnp.zeros_like(mean_all)
    for k in range(2):
        for j in range(nb):
            cols = slice(j * LANES, (j + 1) * LANES)
            v = flat[pl.ds(k * nb + j, peers, stride=2 * nb), :]
            mean = jnp.sum(v * counts, axis=0, keepdims=True) / total
            mean_all[k : k + 1, cols] = mean
            dev[k, :, cols] = v - mean
    start = core * (ch // 2) + (peer // nb) * piece
    block = pl.multiple_of((start // LANES) * LANES, LANES)
    inside = pl.multiple_of(lax.rem(start, LANES), piece)
    here = pl.multiple_of(lax.rem(peer, nb) * LANES, LANES)
    for m, (a, c) in enumerate(((0, 0), (0, 1), (1, 1))):
        left = dev[a, :, pl.ds(block, LANES)] * counts
        square[m] = dot(left, dev[c, :, pl.ds(here, LANES)], TN, HI)
    between = jnp.concatenate([square[m, pl.ds(inside, piece), :] for m in range(3)], axis=0)
    value = ((within + between) / total).astype(BF)
    cov[...] = jnp.broadcast_to(value[None], cov.shape)


def step_kernel(
    dims, info, half_cov, other_cov, mean_all, hid_hbm, sq_hbm, sq0_hbm, w_hbm,
    score, mine, other, dpre, cov, grads, hid, sq, sq0, w, sems,
):
    rows, ch, length, peers, piece = dims
    core = info[0]
    nb = ch // LANES
    half = ch // 2
    loads = [
        pltpu.make_async_copy(src, dst, sems.at[n])
        for n, (src, dst) in enumerate(((hid_hbm, hid), (sq_hbm, sq), (sq0_hbm, sq0), (w_hbm, w)))
    ]
    for load in loads:
        load.start()

    def place(i, carry):
        at = pl.multiple_of(core * half + i * piece, piece)
        to = pl.multiple_of((1 - core) * half + i * piece, piece)
        for m in range(3):
            for j in range(nb):
                cols = slice(j * LANES, (j + 1) * LANES)
                put = slice(m * piece, (m + 1) * piece)
                cov[m, pl.ds(at, piece), cols] = half_cov[i * nb + j, put, :].astype(F32)
                cov[m, pl.ds(to, piece), cols] = other_cov[i * nb + j, put, :].astype(F32)
        return carry

    lax.fori_loop(0, peers // nb, place, 0)
    row = lax.broadcasted_iota(jnp.int32, (ch, ch), 0)
    col = lax.broadcasted_iota(jnp.int32, (ch, ch), 1)
    unit = jnp.where(row == col, 1.0, 0.0).astype(F32)

    def forward(matrix):
        shifted = matrix + RIDGE * unit
        square = jnp.sum(shifted * shifted, keepdims=True)
        inv_scale = lax.rsqrt(square)
        a = shifted * inv_scale
        ab = a.astype(BF)
        a2 = dot(ab, ab)
        a2b = a2.astype(BF)
        rest = C1 * a + C2 * a2 + dot(a2b, (C3 * a + C4 * a2).astype(BF))
        root = jnp.sqrt(inv_scale)
        return a, ab, a2b, rest, inv_scale, root, C0 * root, (rest * root).astype(BF)

    def backward(a, ab, a2b, rest, inv_scale, root, grad):
        poly = C0 * unit + rest
        dscale = -0.5 * jnp.sum(grad * poly, keepdims=True) * root * inv_scale
        g = grad * root
        gb = g.astype(BF)
        y = dot(gb, ab)
        x = dot(a2b, gb)
        xs = x + x.T
        h = C2 * g + (0.5 * C3) * (y + y.T) + C4 * xs
        z = dot(ab, h.astype(BF))
        da = C1 * g + (0.5 * C3) * xs + z + z.T
        dscale = dscale - jnp.sum(da * a, keepdims=True) * inv_scale
        return da * inv_scale + dscale * a

    fe = forward(cov[0])
    fl = forward(cov[2])
    alpha, re = fe[6:]
    beta, rl = fl[6:]
    c = cov[1]
    cb = c.astype(BF)
    u = alpha * c + dot(re, cb)
    ub = u.astype(BF)
    vb = (beta * c + dot(cb, rl)).astype(BF)
    k = beta * u + dot(ub, rl)
    score[...] = jnp.broadcast_to(1.0 + jnp.sum(k * k, keepdims=True), score.shape)
    k2 = 2.0 * k
    kb = k2.astype(BF)
    rk = alpha * k2 + dot(re, kb)
    gc = beta * rk + dot(rk.astype(BF), rl)
    grads[ch : 2 * ch] = gc.T.astype(BF)
    grads[2 * ch : 3 * ch] = gc.astype(BF)
    gre = dot(kb, vb, NT)
    grads[:ch] = backward(*fe[:6], gre + gre.T).astype(BF)
    grl = dot(ub, kb, TN)
    grads[3 * ch :] = backward(*fl[:6], grl + grl.T).astype(BF)
    for load in loads:
        load.wait()
    conv_backward(dims, info, hid, sq, sq0, w, grads, mean_all, mine, other, dpre)


def conv_backward(dims, info, hid, sq, sq0, w, grads, mean_all, mine, other, dpre):
    rows, ch, length, peers, piece = dims
    core, segment = info[0], info[1]
    segments = length // rows
    half = ch // 2
    nh = half // LANES
    total = 2 * (peers // segments) * (length - LAG)
    grows = rows + 16
    t = segment * rows + lax.broadcasted_iota(jnp.int32, (grows, 1), 0)
    has_early = t < length - LAG
    has_later = jnp.logical_and(t >= LAG, t < length)
    out = hid[NL].astype(F32)
    base = out[HALO : HALO + grows]
    mean_e, mean_l = mean_all[0:1], mean_all[1:2]
    zero = jnp.zeros((1, ch), F32)
    consts = []
    for early_on in (True, False):
        left_e, left_l = mean_e, mean_l
        for _ in range(3):
            top_e, top_l = left_e.astype(BF).astype(F32), left_l.astype(BF).astype(F32)
            parts = [top_e, top_l, zero, zero] if early_on else [zero, zero, top_e, top_l]
            consts.append(jnp.concatenate(parts, axis=1))
            left_e, left_l = left_e - top_e, left_l - top_l
    consts = jnp.concatenate(consts + [jnp.zeros((10, 4 * ch), F32)], axis=0)
    lhs = jnp.concatenate(
        [
            jnp.where(has_early, base, 0.0),
            jnp.where(has_early, out[HALO + LAG : HALO + LAG + grows], 0.0),
            jnp.where(has_later, out[HALO - LAG : HALO - LAG + grows], 0.0),
            jnp.where(has_later, base, 0.0),
        ],
        axis=1,
    )
    lhs = jnp.concatenate([lhs, consts], axis=0).astype(BF)
    grad = dot(lhs, grads[...])
    off_early = grad[grows : grows + 1] + grad[grows + 1 : grows + 2] + grad[grows + 2 : grows + 3]
    off_later = grad[grows + 3 : grows + 4] + grad[grows + 4 : grows + 5] + grad[grows + 5 : grows + 6]
    grad = grad[:grows] - jnp.where(has_early, off_early, 0.0) - jnp.where(has_later, off_later, 0.0)
    grad = grad / total
    biases = [None] * (NL + 1)
    first = core == 0

    def halves(value):
        lo, hi = value[:, :half], value[:, half:]
        return jnp.where(first, lo, hi), jnp.where(first, hi, lo)

    def store(left, value, p0, count, size, at):
        for part, ref in zip(halves(value), (mine, other)):
            res = dot(left, part.astype(BF), TN).astype(BF)
            for j in range(nh):
                piece_j = res[:, j * LANES : (j + 1) * LANES].reshape(count, size, LANES)
                ref[p0 : p0 + count, at + j * size : at + (j + 1) * size, :] = piece_j

    conv_size = 2 * ch // peers
    for layer in reversed(range(NL)):
        step = 2**layer
        s = sq[layer, HALO : HALO + grows, :]
        pre = jnp.where(t < length, grad * (1.0 - s * s), 0.0).astype(BF)
        own = pre[:rows].astype(F32)
        biases[layer + 1] = jnp.sum(own, axis=0, keepdims=True)
        h = hid[layer].astype(F32)
        hist = pltpu.roll(h, step, 0)[HALO : HALO + rows].astype(BF)
        at = layer * nh * conv_size
        count = ch // conv_size
        store(hid[layer, HALO : HALO + rows, :], own, 0, count, conv_size, at)
        store(hist, own, count, count, conv_size, at)
        back = dot(pre, w[layer, ch:], NT)
        grad = grad + dot(pre, w[layer, :ch], NT) + pltpu.roll(back, grows - step, 0)
    s = sq0[...]
    own = (grad[:rows] * (1.0 - s * s)).astype(BF)
    dpre[...] = own
    biases[0] = jnp.sum(own.astype(F32), axis=0, keepdims=True)
    bias = jnp.concatenate(biases, axis=0)
    for part, ref in zip(halves(bias), (mine, other)):
        hi, lo = split(part)
        tail = []
        for value in (hi.astype(F32), lo.astype(F32)):
            for j in range(nh):
                tail.append(value[:, j * LANES : (j + 1) * LANES])
        tail = jnp.concatenate(tail, axis=0).astype(BF)
        at = ref.shape[1] - tail.shape[0]
        ref[:, at:, :] = jnp.broadcast_to(tail[None], (peers,) + tail.shape)


def pack_kernel(nbias, info, left, left_got, dpre, dpre_got, mine, got, packed):
    count = packed.shape[0]
    ch = dpre.shape[1]
    size = left.shape[1] // count
    lhs = jnp.concatenate([left[...], left_got[...]], axis=0)
    res = dot(lhs, jnp.concatenate([dpre[...], dpre_got[...]], axis=0), TN).astype(BF)
    for j in range(ch // LANES):
        part = res[:, j * LANES : (j + 1) * LANES].reshape(count, size, LANES)
        packed[:, j * size : (j + 1) * size, :] = part
    at = size * (ch // LANES)
    body = mine.shape[1] - 2 * nbias
    value = mine[...].astype(F32) + got[...].astype(F32)
    packed[:, at : at + body, :] = value[:, :body].astype(BF)
    bias = value[0, body : body + nbias] + value[0, body + nbias :]
    hi = bias.astype(BF).astype(F32)
    tail = jnp.concatenate([hi, bias - hi], axis=0).astype(BF)
    packed[:, at + body :, :] = jnp.broadcast_to(tail[None], (count,) + tail.shape)


def sum_kernel(arrived, tails, full, bias):
    peers = arrived.shape[0]

    def add(p, acc):
        return acc + arrived[p].astype(F32)

    value = lax.fori_loop(0, peers, add, jnp.zeros(arrived.shape[1:], F32), unroll=4)
    full[...] = jnp.broadcast_to(value.astype(BF)[None], full.shape)

    @pl.when(pl.program_id(0) == 0)
    def _():
        def add_tail(p, acc):
            return acc + tails[p].astype(F32)

        t = lax.fori_loop(0, peers, add_tail, jnp.zeros(tails.shape[1:], F32))
        n = t.shape[0] // 2
        bias[...] = t[:n] + t[n:]


def unpack_kernel(sizes, nbiases, info, chunks, *refs):
    in_size, conv_size, nb = sizes
    if nbiases:
        bias, bias_got = refs[:2]
        w_in, w_conv, b_in, b_conv = refs[-4:]
    else:
        w_in, w_conv = refs[-2:]
    count = chunks.shape[0]
    for j in range(nb):
        part = chunks[:, j * in_size : (j + 1) * in_size, :].astype(F32)
        w_in[0, :, j * LANES : (j + 1) * LANES] = part.reshape(count * in_size, LANES)
    for layer in range(NL):
        for j in range(nb // 2):
            at = nb * in_size + (layer * (nb // 2) + j) * conv_size
            part = chunks[:, at : at + conv_size, :].astype(F32)
            w_conv[layer, :, j * LANES : (j + 1) * LANES] = part.reshape(count * conv_size, LANES)
    if nbiases:

        @pl.when(pl.program_id(0) == 0)
        def _():
            swapped = info[0] == 0
            n = NL + 1
            rows = []
            for side in range(2):
                keep = bias_got[...] if side == 0 else bias[...]
                swap = bias[...] if side == 0 else bias_got[...]
                value = jnp.where(swapped, keep, swap)
                rows += [value[j * n : (j + 1) * n] for j in range(nb // 2)]
            full = jnp.concatenate(rows, axis=1)
            b_in[...] = full[0]
            b_conv[...] = full[1:]


def per_device(frames, w_in, b_in, w_conv, b_conv):
    frames = frames[0]
    rows, features = frames.shape
    ch = w_in.shape[1]
    core = lax.axis_index("c")
    segment = lax.axis_index("tm")
    segments = lax.axis_size("tm")
    peers = lax.axis_size("x") * segments
    length = rows * segments
    nb = ch // LANES
    nh = nb // 2
    piece = (ch // 2) * nb // peers
    dims = (rows, ch, length, peers, piece)
    info = jnp.stack([core, segment, lax.axis_index("x") * segments + segment]).astype(jnp.int32)
    ext = rows + 2 * HALO
    frames_got = swap_core(frames)

    squash0 = jnp.tanh(jnp.dot(frames, w_in, preferred_element_type=F32) + b_in)
    own = squash0.astype(BF)
    before = shift_segment(own[rows - HALO :], 1)
    after = shift_segment(own[:HALO], -1)
    hid, sq, mine, other, means = call(
        functools.partial(forward_kernel, dims),
        [
            sds((NL + 1, ext, ch), BF),
            sds((NL, ext, ch), F32),
            sds((peers, 3 * piece, LANES), F32),
            sds((peers, 3 * piece, LANES), BF),
            sds((8, ch), F32),
        ],
        info, before, own, after, w_conv, b_conv,
        scratch=[pltpu.VMEM((3, ch, ch), F32)],
        vmem=36,
    )
    got, sib, frames_got = lax.optimization_barrier(
        (swap_core(other), swap_core(means), frames_got)
    )
    (packed,) = call(
        functools.partial(pair_kernel, dims),
        [sds((peers, 3 * piece + 4 * nb, LANES), BF)],
        info, mine, got, means, sib,
        scratch=[pltpu.VMEM((ch, 8), F32)],
    )
    cov, mean_all = call(
        functools.partial(merge_kernel, dims),
        [sds((peers, 3 * piece, LANES), BF), sds((8, ch), F32)],
        info, exchange(packed),
        scratch=[
            pltpu.VMEM((peers * 2 * nb, LANES), F32),
            pltpu.VMEM((2, peers, ch), F32),
            pltpu.VMEM((3, LANES, LANES), F32),
        ],
    )
    cov = exchange(cov)
    half_features = features // 2
    in_size = half_features // peers
    conv_size = 2 * ch // peers
    nbias = (NL + 1) * nh
    conv_wide = NL * nh * conv_size + 2 * nbias
    body = nb * in_size + NL * nh * conv_size
    wide = body + 2 * nbias
    vmem = pl.BlockSpec(memory_space=pltpu.VMEM)
    smem = pl.BlockSpec(memory_space=pltpu.SMEM)
    hbm = pl.BlockSpec(memory_space=pl.ANY)
    params = pltpu.CompilerParams(vmem_limit_bytes=40 * 2**20)
    small_params = pltpu.CompilerParams(vmem_limit_bytes=16 * 2**20)
    score, mine, other, dpre = pl.pallas_call(
        functools.partial(step_kernel, dims),
        out_shape=[
            sds((8, LANES), F32),
            sds((peers, conv_wide, LANES), BF),
            sds((peers, conv_wide, LANES), BF),
            sds((rows, ch), BF),
        ],
        in_specs=[smem, vmem, vmem, vmem, hbm, hbm, hbm, hbm],
        out_specs=[vmem] * 4,
        scratch_shapes=[
            pltpu.VMEM((3, ch, ch), F32),
            pltpu.VMEM((4 * ch, ch), BF),
            pltpu.VMEM(hid.shape, BF),
            pltpu.VMEM(sq.shape, F32),
            pltpu.VMEM(squash0.shape, F32),
            pltpu.VMEM(w_conv.shape, BF),
            pltpu.SemaphoreType.DMA((4,)),
        ],
        compiler_params=params,
    )(info, cov, swap_core(cov), mean_all, hid, sq, squash0, w_conv)
    steps = 4
    group = peers // steps
    tile = group * in_size
    whole = pl.BlockSpec((rows, ch), lambda i, at: (0, 0))
    conv_spec = pl.BlockSpec((group, conv_wide, LANES), lambda i, at: (i, 0, 0))
    packed = pl.pallas_call(
        functools.partial(pack_kernel, nbias),
        grid_spec=pltpu.PrefetchScalarGridSpec(
            num_scalar_prefetch=1,
            grid=(steps,),
            in_specs=[
                pl.BlockSpec((rows, tile), lambda i, at: (0, at[0] * steps + i)),
                pl.BlockSpec((rows, tile), lambda i, at: (0, at[0] * steps + i)),
                whole,
                whole,
                conv_spec,
                conv_spec,
            ],
            out_specs=pl.BlockSpec((group, wide, LANES), lambda i, at: (i, 0, 0)),
        ),
        out_shape=sds((peers, wide, LANES), BF),
        compiler_params=small_params,
    )(info, frames, frames_got, dpre, swap_core(dpre), mine, swap_core(other))
    arrived = exchange(packed)
    block = 32
    full, bias = pl.pallas_call(
        sum_kernel,
        grid=(body // block,),
        out_shape=[sds((peers, body, LANES), BF), sds((nbias, LANES), F32)],
        in_specs=[
            pl.BlockSpec((peers, block, LANES), lambda i: (0, i, 0)),
            pl.BlockSpec((peers, 2 * nbias, LANES), lambda i: (0, body // (2 * nbias), 0)),
        ],
        out_specs=[
            pl.BlockSpec((peers, block, LANES), lambda i: (0, i, 0)),
            pl.BlockSpec((nbias, LANES), lambda i: (0, 0)),
        ],
        compiler_params=small_params,
    )(arrived, arrived)
    bias_got = swap_core(bias)
    full = exchange(full)
    steps = 8
    group = peers // steps

    def unpack(chunks, at, biases, earlier):
        spare = [sds((ch,), F32), sds((NL, ch), F32)] if biases else []
        return pl.pallas_call(
            functools.partial(unpack_kernel, (in_size, conv_size, nb), len(biases)),
            grid_spec=pltpu.PrefetchScalarGridSpec(
                num_scalar_prefetch=1,
                grid=(steps,),
                in_specs=[pl.BlockSpec((group, body, LANES), lambda i, at: (i, 0, 0))]
                + [pl.BlockSpec(b.shape, lambda i, at: (0, 0)) for b in biases]
                + [hbm] * len(earlier),
                out_specs=[
                    pl.BlockSpec((1, group * in_size, ch), lambda i, at: (at[0], i, 0)),
                    pl.BlockSpec((NL, group * conv_size, ch // 2), lambda i, at: (0, i, at[0])),
                ]
                + [pl.BlockSpec(b.shape, lambda i, at, n=len(b.shape): (0,) * n) for b in spare],
            ),
            out_shape=[sds((2, half_features, ch), F32), sds((NL, 2 * ch, ch), F32)] + spare,
            input_output_aliases={2 + len(biases) + n: n for n in range(len(earlier))},
            compiler_params=small_params,
            cost_estimate=pl.CostEstimate(flops=0, bytes_accessed=12 * 2**20, transcendentals=0),
        )(at, chunks, *biases, *earlier)

    got = swap_core(full)
    partial = unpack(full, info[:1], [], [])
    got, bias_got = lax.optimization_barrier((got, bias_got))
    g_in, g_conv, g_b_in, g_b_conv = unpack(got, 1 - info[:1], [bias, bias_got], partial)
    return score[0, 0], g_in.reshape(features, ch), g_b_in, g_conv, g_b_conv


def solution(mesh):
    devices = mesh.devices
    trajs, segments = devices.shape
    inner = Mesh(devices.reshape(trajs // 2, 2, segments), ("x", "c", "tm"))
    return jax.shard_map(
        per_device,
        mesh=inner,
        in_specs=(P(("x", "c"), "tm", None), P(), P(), P(), P()),
        out_specs=(P(), P(), P(), P(), P()),
        check_vma=False,
    )
```

```python
import functools

import jax
import jax.numpy as jnp
from jax import lax
from jax.experimental import pallas as pl
from jax.experimental.pallas import tpu as pltpu
from jax.sharding import Mesh, PartitionSpec as P

NL = 3
LAG = 16
RIDGE = 0.0001
HALO = 32
LANES = 128
BF = jnp.bfloat16
F32 = jnp.float32
PEERS = ("x", "tm")
HI = lax.Precision.HIGHEST
C0, C1, C2, C3, C4 = 2.25, -2.4375, 1.6875, -0.5625, 0.0625

NN = (((1,), (0,)), ((), ()))
NT = (((1,), (1,)), ((), ()))
TN = (((0,), (0,)), ((), ()))


def dot(a, b, dims=NN, precision=None):
    return lax.dot_general(a, b, dims, precision=precision, preferred_element_type=F32)


def split(a):
    hi = a.astype(BF)
    return hi, (a - hi.astype(F32)).astype(BF)


def dot3(a, b, dims=NN):
    return dot(a[0], b[0], dims) + (dot(a[0], b[1], dims) + dot(a[1], b[0], dims))


def swap_core(value):
    return lax.ppermute(value, "c", [(0, 1), (1, 0)])


def shift_segment(value, steps):
    count = lax.axis_size("tm")
    first, last = max(0, -steps), min(count, count - steps)
    return lax.ppermute(value, "tm", [(i, i + steps) for i in range(first, last)])


def exchange(value):
    return lax.all_to_all(value, PEERS, 0, 0, tiled=True)


def call(kernel, outs, *args, scratch=(), vmem=16):
    specs = [
        pl.BlockSpec(memory_space=pltpu.SMEM if a.dtype == jnp.int32 else pltpu.VMEM) for a in args
    ]
    return pl.pallas_call(
        kernel,
        out_shape=outs,
        in_specs=specs,
        out_specs=[pl.BlockSpec(memory_space=pltpu.VMEM) for _ in outs],
        scratch_shapes=list(scratch),
        compiler_params=pltpu.CompilerParams(vmem_limit_bytes=vmem * 2**20),
    )(*args)


def sds(shape, dtype):
    return jax.ShapeDtypeStruct(shape, dtype)


def forward_kernel(dims, info, before, own, after, w, b, hid, sq, mine, other, means, mom):
    rows, ch, length, peers, piece = dims
    core, segment = info[0], info[1]
    ext = rows + 2 * HALO
    nb = ch // LANES
    t = segment * rows - HALO + lax.broadcasted_iota(jnp.int32, (ext, 1), 0)
    h = jnp.concatenate(
        [before[...].astype(F32), own[...].astype(F32), after[...].astype(F32)], axis=0
    )
    for layer in range(NL):
        hb = h.astype(BF)
        hid[layer] = hb
        hist = pltpu.roll(h, 2**layer, 0).astype(BF)
        s = jnp.tanh(dot(hb, w[layer, :ch]) + dot(hist, w[layer, ch:]) + b[layer : layer + 1])
        sq[layer] = s
        h = jnp.where(t >= 0, (h + s).astype(BF).astype(F32), 0.0)
    hid[NL] = h.astype(BF)
    tp = segment * rows + lax.broadcasted_iota(jnp.int32, (rows, 1), 0)
    pair = jnp.where(tp < length - LAG, 1.0, 0.0).astype(F32)
    last = segment == length // rows - 1
    count = jnp.where(last, rows - LAG, rows).astype(F32)
    early = h[HALO : HALO + rows] * pair
    later = h[HALO + LAG : HALO + LAG + rows] * pair
    mean_e = jnp.sum(early, axis=0, keepdims=True) / count
    mean_l = jnp.sum(later, axis=0, keepdims=True) / count
    means[...] = jnp.concatenate([mean_e, mean_l, jnp.zeros((6, ch), F32)], axis=0)
    ce = split((early - mean_e) * pair)
    cl = split((later - mean_l) * pair)
    left_e = jnp.concatenate([ce[0], ce[0], ce[1]], axis=0)
    left_l = jnp.concatenate([cl[0], cl[0], cl[1]], axis=0)
    right_e = jnp.concatenate([ce[0], ce[1], ce[0]], axis=0)
    right_l = jnp.concatenate([cl[0], cl[1], cl[0]], axis=0)
    mom[0] = dot(left_e, right_e, TN)
    mom[1] = dot(left_e, right_l, TN)
    mom[2] = dot(left_l, right_l, TN)
    half = ch // 2

    def pack(i, carry):
        at = pl.multiple_of(core * half + i * piece, piece)
        to = pl.multiple_of((1 - core) * half + i * piece, piece)
        for m in range(3):
            for j in range(nb):
                cols = slice(j * LANES, (j + 1) * LANES)
                put = slice(m * piece, (m + 1) * piece)
                mine[i * nb + j, put, :] = mom[m, pl.ds(at, piece), cols]
                other[i * nb + j, put, :] = mom[m, pl.ds(to, piece), cols].astype(BF)
        return carry

    lax.fori_loop(0, peers // nb, pack, 0)


def pair_kernel(dims, info, mine, got, means, sib, packed, turned):
    rows, ch, length, peers, piece = dims
    core, segment = info[0], info[1]
    nb = ch // LANES
    half = ch // 2
    last = segment == length // rows - 1
    weight = 0.5 * jnp.where(last, rows - LAG, rows).astype(F32)
    gap = means[...] - sib[...]
    mid = 0.5 * (means[...] + sib[...])
    turned[...] = gap.T * weight
    hi, lo = split(mid)
    tail = []
    for part in (hi.astype(F32), lo.astype(F32)):
        for k in range(2):
            for j in range(nb):
                tail.append(part[k : k + 1, j * LANES : (j + 1) * LANES])
    tail = jnp.concatenate(tail, axis=0).astype(BF)

    def pack(i, carry):
        at = pl.multiple_of(core * half + i * piece, piece)
        col = turned[pl.ds(at, piece), :]
        for j in range(nb):
            cols = slice(j * LANES, (j + 1) * LANES)
            p = i * nb + j
            for m, (a, c) in enumerate(((0, 0), (0, 1), (1, 1))):
                put = slice(m * piece, (m + 1) * piece)
                value = mine[p, put, :] + got[p, put, :].astype(F32)
                value = value + col[:, a : a + 1] * gap[c : c + 1, cols]
                packed[p, put, :] = value.astype(BF)
            packed[p, 3 * piece :, :] = tail
        return carry

    lax.fori_loop(0, peers // nb, pack, 0)


def merge_kernel(dims, info, arrived, cov, mean_all, flat, dev, square):
    rows, ch, length, peers, piece = dims
    core, peer = info[0], info[2]
    nb = ch // LANES
    segments = length // rows
    total = 2 * (peers // segments) * (length - LAG)
    body = 3 * piece

    def add(p, acc):
        z = arrived[p, body:, :].astype(F32)
        flat[pl.ds(pl.multiple_of(p * 2 * nb, 2 * nb), 2 * nb), :] = z[: 2 * nb] + z[2 * nb :]
        return acc + arrived[p, :body, :].astype(F32)

    within = lax.fori_loop(0, peers, add, jnp.zeros((body, LANES), F32))
    seg = lax.rem(lax.broadcasted_iota(jnp.int32, (peers, 1), 0), segments)
    counts = 2.0 * jnp.where(seg == segments - 1, rows - LAG, rows).astype(F32)
    mean_all[...] = jnp.zeros_like(mean_all)
    for k in range(2):
        for j in range(nb):
            cols = slice(j * LANES, (j + 1) * LANES)
            v = flat[pl.ds(k * nb + j, peers, stride=2 * nb), :]
            mean = jnp.sum(v * counts, axis=0, keepdims=True) / total
            mean_all[k : k + 1, cols] = mean
            dev[k, :, cols] = v - mean
    start = core * (ch // 2) + (peer // nb) * piece
    block = pl.multiple_of((start // LANES) * LANES, LANES)
    inside = pl.multiple_of(lax.rem(start, LANES), piece)
    here = pl.multiple_of(lax.rem(peer, nb) * LANES, LANES)
    for m, (a, c) in enumerate(((0, 0), (0, 1), (1, 1))):
        left = dev[a, :, pl.ds(block, LANES)] * counts
        square[m] = dot(left, dev[c, :, pl.ds(here, LANES)], TN, HI)
    between = jnp.concatenate([square[m, pl.ds(inside, piece), :] for m in range(3)], axis=0)
    value = ((within + between) / total).astype(BF)
    cov[...] = jnp.broadcast_to(value[None], cov.shape)


def step_kernel(
    dims, info, half_cov, other_cov, mean_all, hid_hbm, sq_hbm, sq0_hbm, w_hbm,
    score, mine, other, dpre, cov, grads, hid, sq, sq0, w, sems,
):
    rows, ch, length, peers, piece = dims
    core = info[0]
    nb = ch // LANES
    half = ch // 2
    loads = [
        pltpu.make_async_copy(src, dst, sems.at[n])
        for n, (src, dst) in enumerate(((hid_hbm, hid), (sq_hbm, sq), (sq0_hbm, sq0), (w_hbm, w)))
    ]
    for load in loads:
        load.start()

    def place(i, carry):
        at = pl.multiple_of(core * half + i * piece, piece)
        to = pl.multiple_of((1 - core) * half + i * piece, piece)
        for m in range(3):
            for j in range(nb):
                cols = slice(j * LANES, (j + 1) * LANES)
                put = slice(m * piece, (m + 1) * piece)
                cov[m, pl.ds(at, piece), cols] = half_cov[i * nb + j, put, :].astype(F32)
                cov[m, pl.ds(to, piece), cols] = other_cov[i * nb + j, put, :].astype(F32)
        return carry

    lax.fori_loop(0, peers // nb, place, 0)
    row = lax.broadcasted_iota(jnp.int32, (ch, ch), 0)
    col = lax.broadcasted_iota(jnp.int32, (ch, ch), 1)
    unit = jnp.where(row == col, 1.0, 0.0).astype(F32)

    def forward(matrix):
        shifted = matrix + RIDGE * unit
        square = jnp.sum(shifted * shifted, keepdims=True)
        inv_scale = lax.rsqrt(square)
        a = shifted * inv_scale
        ab = a.astype(BF)
        a2 = dot(ab, ab)
        a2b = a2.astype(BF)
        rest = C1 * a + C2 * a2 + dot(a2b, (C3 * a + C4 * a2).astype(BF))
        root = jnp.sqrt(inv_scale)
        return a, ab, a2b, rest, inv_scale, root, C0 * root, (rest * root).astype(BF)

    def backward(a, ab, a2b, rest, inv_scale, root, grad):
        poly = C0 * unit + rest
        dscale = -0.5 * jnp.sum(grad * poly, keepdims=True) * root * inv_scale
        g = grad * root
        gb = g.astype(BF)
        y = dot(gb, ab)
        x = dot(a2b, gb)
        xs = x + x.T
        h = C2 * g + (0.5 * C3) * (y + y.T) + C4 * xs
        z = dot(ab, h.astype(BF))
        da = C1 * g + (0.5 * C3) * xs + z + z.T
        dscale = dscale - jnp.sum(da * a, keepdims=True) * inv_scale
        return da * inv_scale + dscale * a

    fe = forward(cov[0])
    fl = forward(cov[2])
    alpha, re = fe[6:]
    beta, rl = fl[6:]
    c = cov[1]
    cb = c.astype(BF)
    u = alpha * c + dot(re, cb)
    ub = u.astype(BF)
    vb = (beta * c + dot(cb, rl)).astype(BF)
    k = beta * u + dot(ub, rl)
    score[...] = jnp.broadcast_to(1.0 + jnp.sum(k * k, keepdims=True), score.shape)
    k2 = 2.0 * k
    kb = k2.astype(BF)
    rk = alpha * k2 + dot(re, kb)
    gc = beta * rk + dot(rk.astype(BF), rl)
    grads[ch : 2 * ch] = gc.T.astype(BF)
    grads[2 * ch : 3 * ch] = gc.astype(BF)
    gre = dot(kb, vb, NT)
    grads[:ch] = backward(*fe[:6], gre + gre.T).astype(BF)
    grl = dot(ub, kb, TN)
    grads[3 * ch :] = backward(*fl[:6], grl + grl.T).astype(BF)
    for load in loads:
        load.wait()
    conv_backward(dims, info, hid, sq, sq0, w, grads, mean_all, mine, other, dpre)


def conv_backward(dims, info, hid, sq, sq0, w, grads, mean_all, mine, other, dpre):
    rows, ch, length, peers, piece = dims
    core, segment = info[0], info[1]
    segments = length // rows
    half = ch // 2
    nh = half // LANES
    total = 2 * (peers // segments) * (length - LAG)
    grows = rows + 16
    t = segment * rows + lax.broadcasted_iota(jnp.int32, (grows, 1), 0)
    has_early = t < length - LAG
    has_later = jnp.logical_and(t >= LAG, t < length)
    out = hid[NL].astype(F32)
    base = out[HALO : HALO + grows]
    mean_e, mean_l = mean_all[0:1], mean_all[1:2]
    zero = jnp.zeros((1, ch), F32)
    consts = []
    for early_on in (True, False):
        left_e, left_l = mean_e, mean_l
        for _ in range(3):
            top_e, top_l = left_e.astype(BF).astype(F32), left_l.astype(BF).astype(F32)
            parts = [top_e, top_l, zero, zero] if early_on else [zero, zero, top_e, top_l]
            consts.append(jnp.concatenate(parts, axis=1))
            left_e, left_l = left_e - top_e, left_l - top_l
    consts = jnp.concatenate(consts + [jnp.zeros((10, 4 * ch), F32)], axis=0)
    lhs = jnp.concatenate(
        [
            jnp.where(has_early, base, 0.0),
            jnp.where(has_early, out[HALO + LAG : HALO + LAG + grows], 0.0),
            jnp.where(has_later, out[HALO - LAG : HALO - LAG + grows], 0.0),
            jnp.where(has_later, base, 0.0),
        ],
        axis=1,
    )
    lhs = jnp.concatenate([lhs, consts], axis=0).astype(BF)
    grad = dot(lhs, grads[...])
    off_early = grad[grows : grows + 1] + grad[grows + 1 : grows + 2] + grad[grows + 2 : grows + 3]
    off_later = grad[grows + 3 : grows + 4] + grad[grows + 4 : grows + 5] + grad[grows + 5 : grows + 6]
    grad = grad[:grows] - jnp.where(has_early, off_early, 0.0) - jnp.where(has_later, off_later, 0.0)
    grad = grad / total
    biases = [None] * (NL + 1)
    first = core == 0

    def halves(value):
        lo, hi = value[:, :half], value[:, half:]
        return jnp.where(first, lo, hi), jnp.where(first, hi, lo)

    def store(left, value, p0, count, size, at):
        for part, ref in zip(halves(value), (mine, other)):
            res = dot(left, part.astype(BF), TN).astype(BF)
            for j in range(nh):
                piece_j = res[:, j * LANES : (j + 1) * LANES].reshape(count, size, LANES)
                ref[p0 : p0 + count, at + j * size : at + (j + 1) * size, :] = piece_j

    conv_size = 2 * ch // peers
    for layer in reversed(range(NL)):
        step = 2**layer
        s = sq[layer, HALO : HALO + grows, :]
        pre = jnp.where(t < length, grad * (1.0 - s * s), 0.0).astype(BF)
        own = pre[:rows].astype(F32)
        biases[layer + 1] = jnp.sum(own, axis=0, keepdims=True)
        h = hid[layer].astype(F32)
        hist = pltpu.roll(h, step, 0)[HALO : HALO + rows].astype(BF)
        at = layer * nh * conv_size
        count = ch // conv_size
        store(hid[layer, HALO : HALO + rows, :], own, 0, count, conv_size, at)
        store(hist, own, count, count, conv_size, at)
        back = dot(pre, w[layer, ch:], NT)
        grad = grad + dot(pre, w[layer, :ch], NT) + pltpu.roll(back, grows - step, 0)
    s = sq0[...]
    own = (grad[:rows] * (1.0 - s * s)).astype(BF)
    dpre[...] = own
    biases[0] = jnp.sum(own.astype(F32), axis=0, keepdims=True)
    bias = jnp.concatenate(biases, axis=0)
    for part, ref in zip(halves(bias), (mine, other)):
        hi, lo = split(part)
        tail = []
        for value in (hi.astype(F32), lo.astype(F32)):
            for j in range(nh):
                tail.append(value[:, j * LANES : (j + 1) * LANES])
        tail = jnp.concatenate(tail, axis=0).astype(BF)
        at = ref.shape[1] - tail.shape[0]
        ref[:, at:, :] = jnp.broadcast_to(tail[None], (peers,) + tail.shape)


def product_kernel(info, left, dpre, res):
    res[...] = dot(left[...], dpre[...], TN)


def pack_kernel(nbias, info, earlier, left_got, dpre_got, mine, got, packed):
    count = packed.shape[0]
    ch = dpre_got.shape[1]
    size = left_got.shape[1] // count
    res = (earlier[...] + dot(left_got[...], dpre_got[...], TN)).astype(BF)
    for j in range(ch // LANES):
        part = res[:, j * LANES : (j + 1) * LANES].reshape(count, size, LANES)
        packed[:, j * size : (j + 1) * size, :] = part
    at = size * (ch // LANES)
    body = mine.shape[1] - 2 * nbias
    value = mine[...].astype(F32) + got[...].astype(F32)
    packed[:, at : at + body, :] = value[:, :body].astype(BF)
    bias = value[0, body : body + nbias] + value[0, body + nbias :]
    hi = bias.astype(BF).astype(F32)
    tail = jnp.concatenate([hi, bias - hi], axis=0).astype(BF)
    packed[:, at + body :, :] = jnp.broadcast_to(tail[None], (count,) + tail.shape)


def sum_kernel(arrived, tails, full, bias):
    peers = arrived.shape[0]

    def add(p, acc):
        return acc + arrived[p].astype(F32)

    value = lax.fori_loop(0, peers, add, jnp.zeros(arrived.shape[1:], F32), unroll=4)
    full[...] = jnp.broadcast_to(value.astype(BF)[None], full.shape)

    @pl.when(pl.program_id(0) == 0)
    def _():
        def add_tail(p, acc):
            return acc + tails[p].astype(F32)

        t = lax.fori_loop(0, peers, add_tail, jnp.zeros(tails.shape[1:], F32))
        n = t.shape[0] // 2
        bias[...] = t[:n] + t[n:]


def unpack_kernel(sizes, nbiases, info, chunks, *refs):
    in_size, conv_size, nb = sizes
    if nbiases:
        bias, bias_got = refs[:2]
        w_in, w_conv, b_in, b_conv = refs[-4:]
    else:
        w_in, w_conv = refs[-2:]
    count = chunks.shape[0]
    for j in range(nb):
        part = chunks[:, j * in_size : (j + 1) * in_size, :].astype(F32)
        w_in[0, :, j * LANES : (j + 1) * LANES] = part.reshape(count * in_size, LANES)
    for layer in range(NL):
        for j in range(nb // 2):
            at = nb * in_size + (layer * (nb // 2) + j) * conv_size
            part = chunks[:, at : at + conv_size, :].astype(F32)
            w_conv[layer, :, j * LANES : (j + 1) * LANES] = part.reshape(count * conv_size, LANES)
    if nbiases:

        @pl.when(pl.program_id(0) == 0)
        def _():
            swapped = info[0] == 0
            n = NL + 1
            rows = []
            for side in range(2):
                keep = bias_got[...] if side == 0 else bias[...]
                swap = bias[...] if side == 0 else bias_got[...]
                value = jnp.where(swapped, keep, swap)
                rows += [value[j * n : (j + 1) * n] for j in range(nb // 2)]
            full = jnp.concatenate(rows, axis=1)
            b_in[...] = full[0]
            b_conv[...] = full[1:]


def per_device(frames, w_in, b_in, w_conv, b_conv):
    frames = frames[0]
    rows, features = frames.shape
    ch = w_in.shape[1]
    core = lax.axis_index("c")
    segment = lax.axis_index("tm")
    segments = lax.axis_size("tm")
    peers = lax.axis_size("x") * segments
    length = rows * segments
    nb = ch // LANES
    nh = nb // 2
    piece = (ch // 2) * nb // peers
    dims = (rows, ch, length, peers, piece)
    info = jnp.stack([core, segment, lax.axis_index("x") * segments + segment]).astype(jnp.int32)
    ext = rows + 2 * HALO
    frames_got = swap_core(frames)

    edges = jnp.concatenate([frames[:HALO], frames[rows - HALO :]], axis=0)
    edges = jnp.tanh(jnp.dot(edges, w_in, preferred_element_type=F32) + b_in).astype(BF)
    before = shift_segment(edges[HALO:], 1)
    after = shift_segment(edges[:HALO], -1)
    squash0 = jnp.tanh(jnp.dot(frames, w_in, preferred_element_type=F32) + b_in)
    own = squash0.astype(BF)
    hid, sq, mine, other, means = call(
        functools.partial(forward_kernel, dims),
        [
            sds((NL + 1, ext, ch), BF),
            sds((NL, ext, ch), F32),
            sds((peers, 3 * piece, LANES), F32),
            sds((peers, 3 * piece, LANES), BF),
            sds((8, ch), F32),
        ],
        info, before, own, after, w_conv, b_conv,
        scratch=[pltpu.VMEM((3, ch, ch), F32)],
        vmem=36,
    )
    got, sib, frames_got = lax.optimization_barrier(
        (swap_core(other), swap_core(means), frames_got)
    )
    (packed,) = call(
        functools.partial(pair_kernel, dims),
        [sds((peers, 3 * piece + 4 * nb, LANES), BF)],
        info, mine, got, means, sib,
        scratch=[pltpu.VMEM((ch, 8), F32)],
    )
    cov, mean_all = call(
        functools.partial(merge_kernel, dims),
        [sds((peers, 3 * piece, LANES), BF), sds((8, ch), F32)],
        info, exchange(packed),
        scratch=[
            pltpu.VMEM((peers * 2 * nb, LANES), F32),
            pltpu.VMEM((2, peers, ch), F32),
            pltpu.VMEM((3, LANES, LANES), F32),
        ],
    )
    cov = exchange(cov)
    half_features = features // 2
    in_size = half_features // peers
    conv_size = 2 * ch // peers
    nbias = (NL + 1) * nh
    conv_wide = NL * nh * conv_size + 2 * nbias
    body = nb * in_size + NL * nh * conv_size
    wide = body + 2 * nbias
    vmem = pl.BlockSpec(memory_space=pltpu.VMEM)
    smem = pl.BlockSpec(memory_space=pltpu.SMEM)
    hbm = pl.BlockSpec(memory_space=pl.ANY)
    params = pltpu.CompilerParams(vmem_limit_bytes=40 * 2**20)
    small_params = pltpu.CompilerParams(vmem_limit_bytes=16 * 2**20)
    score, mine, other, dpre = pl.pallas_call(
        functools.partial(step_kernel, dims),
        out_shape=[
            sds((8, LANES), F32),
            sds((peers, conv_wide, LANES), BF),
            sds((peers, conv_wide, LANES), BF),
            sds((rows, ch), BF),
        ],
        in_specs=[smem, vmem, vmem, vmem, hbm, hbm, hbm, hbm],
        out_specs=[vmem] * 4,
        scratch_shapes=[
            pltpu.VMEM((3, ch, ch), F32),
            pltpu.VMEM((4 * ch, ch), BF),
            pltpu.VMEM(hid.shape, BF),
            pltpu.VMEM(sq.shape, F32),
            pltpu.VMEM(squash0.shape, F32),
            pltpu.VMEM(w_conv.shape, BF),
            pltpu.SemaphoreType.DMA((4,)),
        ],
        compiler_params=params,
    )(info, cov, swap_core(cov), mean_all, hid, sq, squash0, w_conv)
    steps = 4
    group = peers // steps
    tile = group * in_size
    whole = pl.BlockSpec((rows, ch), lambda i, at: (0, 0))
    conv_spec = pl.BlockSpec((group, conv_wide, LANES), lambda i, at: (i, 0, 0))
    left_spec = pl.BlockSpec((rows, tile), lambda i, at: (0, at[0] * steps + i))
    res_spec = pl.BlockSpec((tile, ch), lambda i, at: (i, 0))
    dpre_got, got = swap_core(dpre), swap_core(other)
    earlier = pl.pallas_call(
        product_kernel,
        grid_spec=pltpu.PrefetchScalarGridSpec(
            num_scalar_prefetch=1,
            grid=(steps,),
            in_specs=[left_spec, whole],
            out_specs=res_spec,
        ),
        out_shape=sds((half_features, ch), F32),
        compiler_params=small_params,
        cost_estimate=pl.CostEstimate(
            flops=2 * rows * half_features * ch, bytes_accessed=6 * 2**20, transcendentals=0
        ),
    )(info, frames, dpre)
    packed = pl.pallas_call(
        functools.partial(pack_kernel, nbias),
        grid_spec=pltpu.PrefetchScalarGridSpec(
            num_scalar_prefetch=1,
            grid=(steps,),
            in_specs=[res_spec, left_spec, whole, conv_spec, conv_spec],
            out_specs=pl.BlockSpec((group, wide, LANES), lambda i, at: (i, 0, 0)),
        ),
        out_shape=sds((peers, wide, LANES), BF),
        compiler_params=small_params,
    )(info, earlier, frames_got, dpre_got, mine, got)
    arrived = exchange(packed)
    block = 32
    full, bias = pl.pallas_call(
        sum_kernel,
        grid=(body // block,),
        out_shape=[sds((peers, body, LANES), BF), sds((nbias, LANES), F32)],
        in_specs=[
            pl.BlockSpec((peers, block, LANES), lambda i: (0, i, 0)),
            pl.BlockSpec((peers, 2 * nbias, LANES), lambda i: (0, body // (2 * nbias), 0)),
        ],
        out_specs=[
            pl.BlockSpec((peers, block, LANES), lambda i: (0, i, 0)),
            pl.BlockSpec((nbias, LANES), lambda i: (0, 0)),
        ],
        compiler_params=small_params,
    )(arrived, arrived)
    bias_got = swap_core(bias)
    full = exchange(full)
    steps = 8
    group = peers // steps

    def unpack(chunks, at, biases, earlier):
        spare = [sds((ch,), F32), sds((NL, ch), F32)] if biases else []
        return pl.pallas_call(
            functools.partial(unpack_kernel, (in_size, conv_size, nb), len(biases)),
            grid_spec=pltpu.PrefetchScalarGridSpec(
                num_scalar_prefetch=1,
                grid=(steps,),
                in_specs=[pl.BlockSpec((group, body, LANES), lambda i, at: (i, 0, 0))]
                + [pl.BlockSpec(b.shape, lambda i, at: (0, 0)) for b in biases]
                + [hbm] * len(earlier),
                out_specs=[
                    pl.BlockSpec((1, group * in_size, ch), lambda i, at: (at[0], i, 0)),
                    pl.BlockSpec((NL, group * conv_size, ch // 2), lambda i, at: (0, i, at[0])),
                ]
                + [pl.BlockSpec(b.shape, lambda i, at, n=len(b.shape): (0,) * n) for b in spare],
            ),
            out_shape=[sds((2, half_features, ch), F32), sds((NL, 2 * ch, ch), F32)] + spare,
            input_output_aliases={2 + len(biases) + n: n for n in range(len(earlier))},
            compiler_params=small_params,
            cost_estimate=pl.CostEstimate(flops=0, bytes_accessed=12 * 2**20, transcendentals=0),
        )(at, chunks, *biases, *earlier)

    got = swap_core(full)
    partial = unpack(full, info[:1], [], [])
    got, bias_got = lax.optimization_barrier((got, bias_got))
    g_in, g_conv, g_b_in, g_b_conv = unpack(got, 1 - info[:1], [bias, bias_got], partial)
    return score[0, 0], g_in.reshape(features, ch), g_b_in, g_conv, g_b_conv


def solution(mesh):
    devices = mesh.devices
    trajs, segments = devices.shape
    inner = Mesh(devices.reshape(trajs // 2, 2, segments), ("x", "c", "tm"))
    return jax.shard_map(
        per_device,
        mesh=inner,
        in_specs=(P(("x", "c"), "tm", None), P(), P(), P(), P()),
        out_specs=(P(), P(), P(), P(), P()),
        check_vma=False,
    )
```

```python
import functools

import jax
import jax.numpy as jnp
from jax import lax
from jax.experimental import pallas as pl
from jax.experimental.pallas import tpu as pltpu
from jax.sharding import Mesh, PartitionSpec as P

NL = 3
LAG = 16
RIDGE = 0.0001
HALO = 32
LANES = 128
BF = jnp.bfloat16
F32 = jnp.float32
PEERS = ("x", "tm")
HI = lax.Precision.HIGHEST
C0, C1, C2, C3, C4 = 2.25, -2.4375, 1.6875, -0.5625, 0.0625

NN = (((1,), (0,)), ((), ()))
NT = (((1,), (1,)), ((), ()))
TN = (((0,), (0,)), ((), ()))


def dot(a, b, dims=NN, precision=None):
    return lax.dot_general(a, b, dims, precision=precision, preferred_element_type=F32)


def split(a):
    hi = a.astype(BF)
    return hi, (a - hi.astype(F32)).astype(BF)


def dot3(a, b, dims=NN):
    return dot(a[0], b[0], dims) + (dot(a[0], b[1], dims) + dot(a[1], b[0], dims))


def swap_core(value):
    return lax.ppermute(value, "c", [(0, 1), (1, 0)])


def shift_segment(value, steps):
    count = lax.axis_size("tm")
    first, last = max(0, -steps), min(count, count - steps)
    return lax.ppermute(value, "tm", [(i, i + steps) for i in range(first, last)])


def exchange(value):
    return lax.all_to_all(value, PEERS, 0, 0, tiled=True)


def call(kernel, outs, *args, scratch=(), vmem=16):
    specs = [
        pl.BlockSpec(memory_space=pltpu.SMEM if a.dtype == jnp.int32 else pltpu.VMEM) for a in args
    ]
    return pl.pallas_call(
        kernel,
        out_shape=outs,
        in_specs=specs,
        out_specs=[pl.BlockSpec(memory_space=pltpu.VMEM) for _ in outs],
        scratch_shapes=list(scratch),
        compiler_params=pltpu.CompilerParams(vmem_limit_bytes=vmem * 2**20),
    )(*args)


def sds(shape, dtype):
    return jax.ShapeDtypeStruct(shape, dtype)


def forward_kernel(dims, info, before, own, after, w, b, hid, sq, mine, other, means, mom):
    rows, ch, length, peers, piece = dims
    core, segment = info[0], info[1]
    ext = rows + 2 * HALO
    nb = ch // LANES
    t = segment * rows - HALO + lax.broadcasted_iota(jnp.int32, (ext, 1), 0)
    h = jnp.concatenate(
        [before[...].astype(F32), own[...].astype(F32), after[...].astype(F32)], axis=0
    )
    for layer in range(NL):
        hb = h.astype(BF)
        hid[layer] = hb
        hist = pltpu.roll(h, 2**layer, 0).astype(BF)
        s = jnp.tanh(dot(hb, w[layer, :ch]) + dot(hist, w[layer, ch:]) + b[layer : layer + 1])
        sq[layer] = s
        h = jnp.where(t >= 0, (h + s).astype(BF).astype(F32), 0.0)
    hid[NL] = h.astype(BF)
    tp = segment * rows + lax.broadcasted_iota(jnp.int32, (rows, 1), 0)
    pair = jnp.where(tp < length - LAG, 1.0, 0.0).astype(F32)
    last = segment == length // rows - 1
    count = jnp.where(last, rows - LAG, rows).astype(F32)
    early = h[HALO : HALO + rows] * pair
    later = h[HALO + LAG : HALO + LAG + rows] * pair
    mean_e = jnp.sum(early, axis=0, keepdims=True) / count
    mean_l = jnp.sum(later, axis=0, keepdims=True) / count
    means[...] = jnp.concatenate([mean_e, mean_l, jnp.zeros((6, ch), F32)], axis=0)
    ce = split((early - mean_e) * pair)
    cl = split((later - mean_l) * pair)
    left_e = jnp.concatenate([ce[0], ce[0], ce[1]], axis=0)
    left_l = jnp.concatenate([cl[0], cl[0], cl[1]], axis=0)
    right_e = jnp.concatenate([ce[0], ce[1], ce[0]], axis=0)
    right_l = jnp.concatenate([cl[0], cl[1], cl[0]], axis=0)
    mom[0] = dot(left_e, right_e, TN)
    mom[1] = dot(left_e, right_l, TN)
    mom[2] = dot(left_l, right_l, TN)
    half = ch // 2

    def pack(i, carry):
        at = pl.multiple_of(core * half + i * piece, piece)
        to = pl.multiple_of((1 - core) * half + i * piece, piece)
        for m in range(3):
            for j in range(nb):
                cols = slice(j * LANES, (j + 1) * LANES)
                put = slice(m * piece, (m + 1) * piece)
                mine[i * nb + j, put, :] = mom[m, pl.ds(at, piece), cols]
                other[i * nb + j, put, :] = mom[m, pl.ds(to, piece), cols].astype(BF)
        return carry

    lax.fori_loop(0, peers // nb, pack, 0)


def pair_kernel(dims, info, mine, got, means, sib, packed, turned):
    rows, ch, length, peers, piece = dims
    core, segment = info[0], info[1]
    nb = ch // LANES
    half = ch // 2
    last = segment == length // rows - 1
    weight = 0.5 * jnp.where(last, rows - LAG, rows).astype(F32)
    gap = means[...] - sib[...]
    mid = 0.5 * (means[...] + sib[...])
    turned[...] = gap.T * weight
    hi, lo = split(mid)
    tail = []
    for part in (hi.astype(F32), lo.astype(F32)):
        for k in range(2):
            for j in range(nb):
                tail.append(part[k : k + 1, j * LANES : (j + 1) * LANES])
    tail = jnp.concatenate(tail, axis=0).astype(BF)

    def pack(i, carry):
        at = pl.multiple_of(core * half + i * piece, piece)
        col = turned[pl.ds(at, piece), :]
        for j in range(nb):
            cols = slice(j * LANES, (j + 1) * LANES)
            p = i * nb + j
            for m, (a, c) in enumerate(((0, 0), (0, 1), (1, 1))):
                put = slice(m * piece, (m + 1) * piece)
                value = mine[p, put, :] + got[p, put, :].astype(F32)
                value = value + col[:, a : a + 1] * gap[c : c + 1, cols]
                packed[p, put, :] = value.astype(BF)
            packed[p, 3 * piece :, :] = tail
        return carry

    lax.fori_loop(0, peers // nb, pack, 0)


def merge_kernel(dims, info, arrived, cov, mean_all, flat, dev, square):
    rows, ch, length, peers, piece = dims
    core, peer = info[0], info[2]
    nb = ch // LANES
    segments = length // rows
    total = 2 * (peers // segments) * (length - LAG)
    body = 3 * piece

    def add(p, acc):
        z = arrived[p, body:, :].astype(F32)
        flat[pl.ds(pl.multiple_of(p * 2 * nb, 2 * nb), 2 * nb), :] = z[: 2 * nb] + z[2 * nb :]
        return acc + arrived[p, :body, :].astype(F32)

    within = lax.fori_loop(0, peers, add, jnp.zeros((body, LANES), F32))
    seg = lax.rem(lax.broadcasted_iota(jnp.int32, (peers, 1), 0), segments)
    counts = 2.0 * jnp.where(seg == segments - 1, rows - LAG, rows).astype(F32)
    mean_all[...] = jnp.zeros_like(mean_all)
    for k in range(2):
        for j in range(nb):
            cols = slice(j * LANES, (j + 1) * LANES)
            v = flat[pl.ds(k * nb + j, peers, stride=2 * nb), :]
            mean = jnp.sum(v * counts, axis=0, keepdims=True) / total
            mean_all[k : k + 1, cols] = mean
            dev[k, :, cols] = v - mean
    start = core * (ch // 2) + (peer // nb) * piece
    block = pl.multiple_of((start // LANES) * LANES, LANES)
    inside = pl.multiple_of(lax.rem(start, LANES), piece)
    here = pl.multiple_of(lax.rem(peer, nb) * LANES, LANES)
    for m, (a, c) in enumerate(((0, 0), (0, 1), (1, 1))):
        left = dev[a, :, pl.ds(block, LANES)] * counts
        square[m] = dot(left, dev[c, :, pl.ds(here, LANES)], TN, HI)
    between = jnp.concatenate([square[m, pl.ds(inside, piece), :] for m in range(3)], axis=0)
    value = ((within + between) / total).astype(BF)
    cov[...] = jnp.broadcast_to(value[None], cov.shape)


def step_kernel(
    dims, info, half_cov, other_cov, mean_all, hid_hbm, sq_hbm, sq0_hbm, w_hbm,
    score, mine, other, dpre, cov, grads, hid, sq, sq0, w, sems,
):
    rows, ch, length, peers, piece = dims
    core = info[0]
    nb = ch // LANES
    half = ch // 2
    loads = [
        pltpu.make_async_copy(src, dst, sems.at[n])
        for n, (src, dst) in enumerate(((hid_hbm, hid), (sq_hbm, sq), (sq0_hbm, sq0), (w_hbm, w)))
    ]
    for load in loads:
        load.start()

    def place(i, carry):
        at = pl.multiple_of(core * half + i * piece, piece)
        to = pl.multiple_of((1 - core) * half + i * piece, piece)
        for m in range(3):
            for j in range(nb):
                cols = slice(j * LANES, (j + 1) * LANES)
                put = slice(m * piece, (m + 1) * piece)
                cov[m, pl.ds(at, piece), cols] = half_cov[i * nb + j, put, :].astype(F32)
                cov[m, pl.ds(to, piece), cols] = other_cov[i * nb + j, put, :].astype(F32)
        return carry

    lax.fori_loop(0, peers // nb, place, 0)
    row = lax.broadcasted_iota(jnp.int32, (ch, ch), 0)
    col = lax.broadcasted_iota(jnp.int32, (ch, ch), 1)
    unit = jnp.where(row == col, 1.0, 0.0).astype(F32)

    def forward(matrix):
        shifted = matrix + RIDGE * unit
        square = jnp.sum(shifted * shifted, keepdims=True)
        inv_scale = lax.rsqrt(square)
        a = shifted * inv_scale
        ab = a.astype(BF)
        a2 = dot(ab, ab)
        a2b = a2.astype(BF)
        rest = C1 * a + C2 * a2 + dot(a2b, (C3 * a + C4 * a2).astype(BF))
        root = jnp.sqrt(inv_scale)
        return a, ab, a2b, rest, inv_scale, root, C0 * root, (rest * root).astype(BF)

    def backward(a, ab, a2b, rest, inv_scale, root, grad):
        poly = C0 * unit + rest
        dscale = -0.5 * jnp.sum(grad * poly, keepdims=True) * root * inv_scale
        g = grad * root
        gb = g.astype(BF)
        y = dot(gb, ab)
        x = dot(a2b, gb)
        xs = x + x.T
        h = C2 * g + (0.5 * C3) * (y + y.T) + C4 * xs
        z = dot(ab, h.astype(BF))
        da = C1 * g + (0.5 * C3) * xs + z + z.T
        dscale = dscale - jnp.sum(da * a, keepdims=True) * inv_scale
        return da * inv_scale + dscale * a

    fe = forward(cov[0])
    fl = forward(cov[2])
    alpha, re = fe[6:]
    beta, rl = fl[6:]
    c = cov[1]
    cb = c.astype(BF)
    u = alpha * c + dot(re, cb)
    ub = u.astype(BF)
    vb = (beta * c + dot(cb, rl)).astype(BF)
    k = beta * u + dot(ub, rl)
    score[...] = jnp.broadcast_to(1.0 + jnp.sum(k * k, keepdims=True), score.shape)
    k2 = 2.0 * k
    kb = k2.astype(BF)
    rk = alpha * k2 + dot(re, kb)
    gc = beta * rk + dot(rk.astype(BF), rl)
    grads[ch : 2 * ch] = gc.T.astype(BF)
    grads[2 * ch : 3 * ch] = gc.astype(BF)
    gre = dot(kb, vb, NT)
    grads[:ch] = backward(*fe[:6], gre + gre.T).astype(BF)
    grl = dot(ub, kb, TN)
    grads[3 * ch :] = backward(*fl[:6], grl + grl.T).astype(BF)
    for load in loads:
        load.wait()
    conv_backward(dims, info, hid, sq, sq0, w, grads, mean_all, mine, other, dpre)


def conv_backward(dims, info, hid, sq, sq0, w, grads, mean_all, mine, other, dpre):
    rows, ch, length, peers, piece = dims
    core, segment = info[0], info[1]
    segments = length // rows
    half = ch // 2
    nh = half // LANES
    total = 2 * (peers // segments) * (length - LAG)
    grows = rows + 16
    t = segment * rows + lax.broadcasted_iota(jnp.int32, (grows, 1), 0)
    has_early = t < length - LAG
    has_later = jnp.logical_and(t >= LAG, t < length)
    out = hid[NL].astype(F32)
    base = out[HALO : HALO + grows]
    mean_e, mean_l = mean_all[0:1], mean_all[1:2]
    zero = jnp.zeros((1, ch), F32)
    consts = []
    for early_on in (True, False):
        left_e, left_l = mean_e, mean_l
        for _ in range(3):
            top_e, top_l = left_e.astype(BF).astype(F32), left_l.astype(BF).astype(F32)
            parts = [top_e, top_l, zero, zero] if early_on else [zero, zero, top_e, top_l]
            consts.append(jnp.concatenate(parts, axis=1))
            left_e, left_l = left_e - top_e, left_l - top_l
    consts = jnp.concatenate(consts + [jnp.zeros((10, 4 * ch), F32)], axis=0)
    lhs = jnp.concatenate(
        [
            jnp.where(has_early, base, 0.0),
            jnp.where(has_early, out[HALO + LAG : HALO + LAG + grows], 0.0),
            jnp.where(has_later, out[HALO - LAG : HALO - LAG + grows], 0.0),
            jnp.where(has_later, base, 0.0),
        ],
        axis=1,
    )
    lhs = jnp.concatenate([lhs, consts], axis=0).astype(BF)
    grad = dot(lhs, grads[...])
    off_early = grad[grows : grows + 1] + grad[grows + 1 : grows + 2] + grad[grows + 2 : grows + 3]
    off_later = grad[grows + 3 : grows + 4] + grad[grows + 4 : grows + 5] + grad[grows + 5 : grows + 6]
    grad = grad[:grows] - jnp.where(has_early, off_early, 0.0) - jnp.where(has_later, off_later, 0.0)
    grad = grad / total
    biases = [None] * (NL + 1)
    first = core == 0

    def halves(value):
        lo, hi = value[:, :half], value[:, half:]
        return jnp.where(first, lo, hi), jnp.where(first, hi, lo)

    def store(left, value, p0, count, size, at):
        for part, ref in zip(halves(value), (mine, other)):
            res = dot(left, part.astype(BF), TN).astype(BF)
            for j in range(nh):
                piece_j = res[:, j * LANES : (j + 1) * LANES].reshape(count, size, LANES)
                ref[p0 : p0 + count, at + j * size : at + (j + 1) * size, :] = piece_j

    conv_size = 2 * ch // peers
    for layer in reversed(range(NL)):
        step = 2**layer
        s = sq[layer, HALO : HALO + grows, :]
        pre = jnp.where(t < length, grad * (1.0 - s * s), 0.0).astype(BF)
        own = pre[:rows].astype(F32)
        biases[layer + 1] = jnp.sum(own, axis=0, keepdims=True)
        h = hid[layer].astype(F32)
        hist = pltpu.roll(h, step, 0)[HALO : HALO + rows].astype(BF)
        at = layer * nh * conv_size
        count = ch // conv_size
        store(hid[layer, HALO : HALO + rows, :], own, 0, count, conv_size, at)
        store(hist, own, count, count, conv_size, at)
        back = dot(pre, w[layer, ch:], NT)
        grad = grad + dot(pre, w[layer, :ch], NT) + pltpu.roll(back, grows - step, 0)
    s = sq0[...]
    own = (grad[:rows] * (1.0 - s * s)).astype(BF)
    dpre[...] = own
    biases[0] = jnp.sum(own.astype(F32), axis=0, keepdims=True)
    bias = jnp.concatenate(biases, axis=0)
    for part, ref in zip(halves(bias), (mine, other)):
        hi, lo = split(part)
        tail = []
        for value in (hi.astype(F32), lo.astype(F32)):
            for j in range(nh):
                tail.append(value[:, j * LANES : (j + 1) * LANES])
        tail = jnp.concatenate(tail, axis=0).astype(BF)
        at = ref.shape[1] - tail.shape[0]
        ref[:, at:, :] = jnp.broadcast_to(tail[None], (peers,) + tail.shape)


def product_kernel(info, left, dpre, res):
    res[...] = dot(left[...], dpre[...], TN)


def pack_kernel(info, earlier, left_got, dpre_got, packed):
    count = packed.shape[0]
    size = left_got.shape[1] // count
    res = (earlier[...] + dot(left_got[...], dpre_got[...], TN)).astype(BF)
    for j in range(res.shape[1] // LANES):
        part = res[:, j * LANES : (j + 1) * LANES].reshape(count, size, LANES)
        packed[:, j * size : (j + 1) * size, :] = part


def add_kernel(nbias, mine, got, packed):
    body = mine.shape[1] - 2 * nbias
    value = mine[...].astype(F32) + got[...].astype(F32)
    packed[:, :body, :] = value[:, :body].astype(BF)
    bias = value[0, body : body + nbias] + value[0, body + nbias :]
    hi = bias.astype(BF).astype(F32)
    tail = jnp.concatenate([hi, bias - hi], axis=0).astype(BF)
    packed[:, body:, :] = jnp.broadcast_to(tail[None], (mine.shape[0],) + tail.shape)


def total_of(arrived):
    def add(p, acc):
        return acc + arrived[p].astype(F32)

    return lax.fori_loop(0, arrived.shape[0], add, jnp.zeros(arrived.shape[1:], F32), unroll=4)


def sum_conv_kernel(nbias, arrived, chunk, bias):
    value = total_of(arrived)
    body = chunk.shape[0]
    chunk[...] = value[:body].astype(BF)
    bias[...] = value[body : body + nbias] + value[body + nbias :]


def sum_in_kernel(arrived, full):
    full[...] = jnp.broadcast_to(total_of(arrived).astype(BF)[None], full.shape)


def unpack_in_kernel(info, chunks, *refs):
    w_in = refs[-1]
    count, wide = chunks.shape[:2]
    nb = w_in.shape[2] // LANES
    size = wide // nb
    for j in range(nb):
        part = chunks[:, j * size : (j + 1) * size, :].astype(F32)
        w_in[0, :, j * LANES : (j + 1) * LANES] = part.reshape(count * size, LANES)


def unpack_conv_kernel(info, low, high, bias, bias_got, w_conv, b_in, b_conv):
    count = low.shape[0]
    nh = w_conv.shape[2] // LANES // 2
    size = low.shape[1] // (NL * nh)
    for side, chunks in enumerate((low, high)):
        for layer in range(NL):
            for j in range(nh):
                at = (layer * nh + j) * size
                col = (side * nh + j) * LANES
                part = chunks[:, at : at + size, :].astype(F32)
                w_conv[layer, :, col : col + LANES] = part.reshape(count * size, LANES)

    @pl.when(pl.program_id(0) == 0)
    def _():
        first = info[0] == 0
        n = NL + 1
        parts = []
        for side in range(2):
            mine_side = first if side == 0 else jnp.logical_not(first)
            value = jnp.where(mine_side, bias[...], bias_got[...])
            parts += [value[j * n : (j + 1) * n] for j in range(nh)]
        full = jnp.concatenate(parts, axis=1)
        b_in[...] = full[0]
        b_conv[...] = full[1:]


def per_device(frames, w_in, b_in, w_conv, b_conv):
    frames = frames[0]
    rows, features = frames.shape
    ch = w_in.shape[1]
    core = lax.axis_index("c")
    segment = lax.axis_index("tm")
    segments = lax.axis_size("tm")
    peers = lax.axis_size("x") * segments
    length = rows * segments
    nb = ch // LANES
    nh = nb // 2
    piece = (ch // 2) * nb // peers
    dims = (rows, ch, length, peers, piece)
    info = jnp.stack([core, segment, lax.axis_index("x") * segments + segment]).astype(jnp.int32)
    ext = rows + 2 * HALO
    frames_got = swap_core(frames)

    squash0 = jnp.tanh(jnp.dot(frames, w_in, preferred_element_type=F32) + b_in)
    own = squash0.astype(BF)
    before = shift_segment(own[rows - HALO :], 1)
    after = shift_segment(own[:HALO], -1)
    hid, sq, mine, other, means = call(
        functools.partial(forward_kernel, dims),
        [
            sds((NL + 1, ext, ch), BF),
            sds((NL, ext, ch), F32),
            sds((peers, 3 * piece, LANES), F32),
            sds((peers, 3 * piece, LANES), BF),
            sds((8, ch), F32),
        ],
        info, before, own, after, w_conv, b_conv,
        scratch=[pltpu.VMEM((3, ch, ch), F32)],
        vmem=36,
    )
    got, sib, frames_got = lax.optimization_barrier(
        (swap_core(other), swap_core(means), frames_got)
    )
    (packed,) = call(
        functools.partial(pair_kernel, dims),
        [sds((peers, 3 * piece + 4 * nb, LANES), BF)],
        info, mine, got, means, sib,
        scratch=[pltpu.VMEM((ch, 8), F32)],
    )
    cov, mean_all = call(
        functools.partial(merge_kernel, dims),
        [sds((peers, 3 * piece, LANES), BF), sds((8, ch), F32)],
        info, exchange(packed),
        scratch=[
            pltpu.VMEM((peers * 2 * nb, LANES), F32),
            pltpu.VMEM((2, peers, ch), F32),
            pltpu.VMEM((3, LANES, LANES), F32),
        ],
    )
    cov = exchange(cov)
    half_features = features // 2
    in_size = half_features // peers
    conv_size = 2 * ch // peers
    nbias = (NL + 1) * nh
    conv_wide = NL * nh * conv_size + 2 * nbias
    vmem = pl.BlockSpec(memory_space=pltpu.VMEM)
    smem = pl.BlockSpec(memory_space=pltpu.SMEM)
    hbm = pl.BlockSpec(memory_space=pl.ANY)
    params = pltpu.CompilerParams(vmem_limit_bytes=40 * 2**20)
    small_params = pltpu.CompilerParams(vmem_limit_bytes=16 * 2**20)
    score, mine, other, dpre = pl.pallas_call(
        functools.partial(step_kernel, dims),
        out_shape=[
            sds((8, LANES), F32),
            sds((peers, conv_wide, LANES), BF),
            sds((peers, conv_wide, LANES), BF),
            sds((rows, ch), BF),
        ],
        in_specs=[smem, vmem, vmem, vmem, hbm, hbm, hbm, hbm],
        out_specs=[vmem] * 4,
        scratch_shapes=[
            pltpu.VMEM((3, ch, ch), F32),
            pltpu.VMEM((4 * ch, ch), BF),
            pltpu.VMEM(hid.shape, BF),
            pltpu.VMEM(sq.shape, F32),
            pltpu.VMEM(squash0.shape, F32),
            pltpu.VMEM(w_conv.shape, BF),
            pltpu.SemaphoreType.DMA((4,)),
        ],
        compiler_params=params,
    )(info, cov, swap_core(cov), mean_all, hid, sq, squash0, w_conv)
    steps = 4
    group = peers // steps
    tile = group * in_size
    whole = pl.BlockSpec((rows, ch), lambda i, at: (0, 0))
    conv_spec = pl.BlockSpec((group, conv_wide, LANES), lambda i, at: (i, 0, 0))
    left_spec = pl.BlockSpec((rows, tile), lambda i, at: (0, at[0] * steps + i))
    res_spec = pl.BlockSpec((tile, ch), lambda i, at: (i, 0))
    dpre_got, got = swap_core(dpre), swap_core(other)
    earlier = pl.pallas_call(
        product_kernel,
        grid_spec=pltpu.PrefetchScalarGridSpec(
            num_scalar_prefetch=1,
            grid=(steps,),
            in_specs=[left_spec, whole],
            out_specs=res_spec,
        ),
        out_shape=sds((half_features, ch), F32),
        compiler_params=small_params,
        cost_estimate=pl.CostEstimate(
            flops=2 * rows * half_features * ch, bytes_accessed=6 * 2**20, transcendentals=0
        ),
    )(info, frames, dpre)
    conv_packed = pl.pallas_call(
        functools.partial(add_kernel, nbias),
        grid=(steps,),
        in_specs=[pl.BlockSpec((group, conv_wide, LANES), lambda i: (i, 0, 0))] * 2,
        out_specs=pl.BlockSpec((group, conv_wide, LANES), lambda i: (i, 0, 0)),
        out_shape=sds((peers, conv_wide, LANES), BF),
        compiler_params=small_params,
    )(mine, got)
    in_wide = nb * in_size
    packed = pl.pallas_call(
        pack_kernel,
        grid_spec=pltpu.PrefetchScalarGridSpec(
            num_scalar_prefetch=1,
            grid=(steps,),
            in_specs=[res_spec, left_spec, whole],
            out_specs=pl.BlockSpec((group, in_wide, LANES), lambda i, at: (i, 0, 0)),
        ),
        out_shape=sds((peers, in_wide, LANES), BF),
        compiler_params=small_params,
    )(info, earlier, frames_got, dpre_got)
    conv_body = conv_wide - 2 * nbias
    chunk, bias = pl.pallas_call(
        functools.partial(sum_conv_kernel, nbias),
        in_specs=[vmem],
        out_specs=[vmem, vmem],
        out_shape=[sds((conv_body, LANES), BF), sds((nbias, LANES), F32)],
        compiler_params=small_params,
    )(exchange(conv_packed))
    packed, chunk, bias = lax.optimization_barrier((packed, chunk, bias))
    conv_all = lax.all_gather(chunk[None], ("c",) + PEERS, axis=0, tiled=True)
    bias_got = swap_core(bias)
    block = 32
    full = pl.pallas_call(
        sum_in_kernel,
        grid=(in_wide // block,),
        out_shape=sds((peers, in_wide, LANES), BF),
        in_specs=[pl.BlockSpec((peers, block, LANES), lambda i: (0, i, 0))],
        out_specs=pl.BlockSpec((peers, block, LANES), lambda i: (0, i, 0)),
        compiler_params=small_params,
    )(exchange(packed))
    full = exchange(full)
    steps = 8
    group = peers // steps

    def unpack(chunks, at, earlier):
        return pl.pallas_call(
            unpack_in_kernel,
            grid_spec=pltpu.PrefetchScalarGridSpec(
                num_scalar_prefetch=1,
                grid=(steps,),
                in_specs=[pl.BlockSpec((group, in_wide, LANES), lambda i, at: (i, 0, 0))]
                + [hbm] * len(earlier),
                out_specs=pl.BlockSpec((1, group * in_size, ch), lambda i, at: (at[0], i, 0)),
            ),
            out_shape=sds((2, half_features, ch), F32),
            input_output_aliases={2 + n: 0 for n in range(len(earlier))},
            compiler_params=small_params,
            cost_estimate=pl.CostEstimate(flops=0, bytes_accessed=6 * 2**20, transcendentals=0),
        )(at, chunks, *earlier)

    got = swap_core(full)
    partial = unpack(full, info[:1], [])
    small = pl.BlockSpec((nbias, LANES), lambda i, at: (0, 0))
    conv_block = (group, conv_body, LANES)
    g_conv, g_b_in, g_b_conv = pl.pallas_call(
        unpack_conv_kernel,
        grid_spec=pltpu.PrefetchScalarGridSpec(
            num_scalar_prefetch=1,
            grid=(steps,),
            in_specs=[
                pl.BlockSpec(conv_block, lambda i, at: (i, 0, 0)),
                pl.BlockSpec(conv_block, lambda i, at: (steps + i, 0, 0)),
                small,
                small,
            ],
            out_specs=[
                pl.BlockSpec((NL, group * conv_size, ch), lambda i, at: (0, i, 0)),
                pl.BlockSpec((ch,), lambda i, at: (0,)),
                pl.BlockSpec((NL, ch), lambda i, at: (0, 0)),
            ],
        ),
        out_shape=[sds((NL, 2 * ch, ch), F32), sds((ch,), F32), sds((NL, ch), F32)],
        compiler_params=small_params,
        cost_estimate=pl.CostEstimate(flops=0, bytes_accessed=10 * 2**20, transcendentals=0),
    )(info, conv_all, conv_all, bias, bias_got)
    g_in = unpack(got, 1 - info[:1], [partial])
    return score[0, 0], g_in.reshape(features, ch), g_b_in, g_conv, g_b_conv


def solution(mesh):
    devices = mesh.devices
    trajs, segments = devices.shape
    inner = Mesh(devices.reshape(trajs // 2, 2, segments), ("x", "c", "tm"))
    return jax.shard_map(
        per_device,
        mesh=inner,
        in_specs=(P(("x", "c"), "tm", None), P(), P(), P(), P()),
        out_specs=(P(), P(), P(), P(), P()),
        check_vma=False,
    )
```

```python
import functools

import jax
import jax.numpy as jnp
from jax import lax
from jax.experimental import pallas as pl
from jax.experimental.pallas import tpu as pltpu
from jax.sharding import Mesh, PartitionSpec as P

NL = 3
LAG = 16
RIDGE = 0.0001
HALO = 32
LANES = 128
BF = jnp.bfloat16
F32 = jnp.float32
PEERS = ("x", "tm")
HI = lax.Precision.HIGHEST
C0, C1, C2, C3, C4 = 2.25, -2.4375, 1.6875, -0.5625, 0.0625

NN = (((1,), (0,)), ((), ()))
NT = (((1,), (1,)), ((), ()))
TN = (((0,), (0,)), ((), ()))


def dot(a, b, dims=NN, precision=None):
    return lax.dot_general(a, b, dims, precision=precision, preferred_element_type=F32)


def split(a):
    hi = a.astype(BF)
    return hi, (a - hi.astype(F32)).astype(BF)


def dot3(a, b, dims=NN):
    return dot(a[0], b[0], dims) + (dot(a[0], b[1], dims) + dot(a[1], b[0], dims))


def swap_core(value):
    return lax.ppermute(value, "c", [(0, 1), (1, 0)])


def shift_segment(value, steps):
    count = lax.axis_size("tm")
    first, last = max(0, -steps), min(count, count - steps)
    return lax.ppermute(value, "tm", [(i, i + steps) for i in range(first, last)])


def shifts(count):
    return (0, 1, 3, 2) if count == 4 else tuple(range(count))


def spin(value, axis, steps):
    segments = lax.axis_size("tm")
    nz = grid_side(segments)
    ny = segments // nz
    if axis == "x":
        n = lax.axis_size("x")
        return lax.ppermute(value, "x", [(i, (i + steps) % n) for i in range(n)])
    pairs = []
    for i in range(segments):
        y, z = divmod(i, nz)
        y, z = ((y + steps) % ny, z) if axis == "y" else (y, (z + steps) % nz)
        pairs.append((i, y * nz + z))
    return lax.ppermute(value, "tm", pairs)


def grid_side(count):
    side = 1
    while (side * 2) * (side * 2) <= count:
        side *= 2
    return side


def along(value, axis, count):
    return jnp.stack([value] + [spin(value, axis, k) for k in shifts(count)[1:]])


def exchange(value):
    return lax.all_to_all(value, PEERS, 0, 0, tiled=True)


def call(kernel, outs, *args, scratch=(), vmem=16):
    specs = [
        pl.BlockSpec(memory_space=pltpu.SMEM if a.dtype == jnp.int32 else pltpu.VMEM) for a in args
    ]
    return pl.pallas_call(
        kernel,
        out_shape=outs,
        in_specs=specs,
        out_specs=[pl.BlockSpec(memory_space=pltpu.VMEM) for _ in outs],
        scratch_shapes=list(scratch),
        compiler_params=pltpu.CompilerParams(vmem_limit_bytes=vmem * 2**20),
    )(*args)


def sds(shape, dtype):
    return jax.ShapeDtypeStruct(shape, dtype)


def forward_kernel(dims, info, before, own, after, w, b, hid, sq, mine, other, means, mom):
    rows, ch, length, peers, piece = dims
    core, segment = info[0], info[1]
    ext = rows + 2 * HALO
    nb = ch // LANES
    t = segment * rows - HALO + lax.broadcasted_iota(jnp.int32, (ext, 1), 0)
    h = jnp.concatenate(
        [before[...].astype(F32), own[...].astype(F32), after[...].astype(F32)], axis=0
    )
    for layer in range(NL):
        hb = h.astype(BF)
        hid[layer] = hb
        hist = pltpu.roll(h, 2**layer, 0).astype(BF)
        s = jnp.tanh(dot(hb, w[layer, :ch]) + dot(hist, w[layer, ch:]) + b[layer : layer + 1])
        sq[layer] = s
        h = jnp.where(t >= 0, (h + s).astype(BF).astype(F32), 0.0)
    hid[NL] = h.astype(BF)
    tp = segment * rows + lax.broadcasted_iota(jnp.int32, (rows, 1), 0)
    pair = jnp.where(tp < length - LAG, 1.0, 0.0).astype(F32)
    last = segment == length // rows - 1
    count = jnp.where(last, rows - LAG, rows).astype(F32)
    early = h[HALO : HALO + rows] * pair
    later = h[HALO + LAG : HALO + LAG + rows] * pair
    mean_e = jnp.sum(early, axis=0, keepdims=True) / count
    mean_l = jnp.sum(later, axis=0, keepdims=True) / count
    means[...] = jnp.concatenate([mean_e, mean_l, jnp.zeros((6, ch), F32)], axis=0)
    ce = split((early - mean_e) * pair)
    cl = split((later - mean_l) * pair)
    left_e = jnp.concatenate([ce[0], ce[0], ce[1]], axis=0)
    left_l = jnp.concatenate([cl[0], cl[0], cl[1]], axis=0)
    right_e = jnp.concatenate([ce[0], ce[1], ce[0]], axis=0)
    right_l = jnp.concatenate([cl[0], cl[1], cl[0]], axis=0)
    mom[0] = dot(left_e, right_e, TN)
    mom[1] = dot(left_e, right_l, TN)
    mom[2] = dot(left_l, right_l, TN)
    half = ch // 2

    def pack(i, carry):
        at = pl.multiple_of(core * half + i * piece, piece)
        to = pl.multiple_of((1 - core) * half + i * piece, piece)
        for m in range(3):
            for j in range(nb):
                cols = slice(j * LANES, (j + 1) * LANES)
                put = slice(m * piece, (m + 1) * piece)
                mine[i * nb + j, put, :] = mom[m, pl.ds(at, piece), cols]
                other[i * nb + j, put, :] = mom[m, pl.ds(to, piece), cols].astype(BF)
        return carry

    lax.fori_loop(0, peers // nb, pack, 0)


def pair_kernel(dims, info, mine, got, means, sib, packed, turned):
    rows, ch, length, peers, piece = dims
    core, segment = info[0], info[1]
    nb = ch // LANES
    half = ch // 2
    last = segment == length // rows - 1
    weight = 0.5 * jnp.where(last, rows - LAG, rows).astype(F32)
    gap = means[...] - sib[...]
    mid = 0.5 * (means[...] + sib[...])
    turned[...] = gap.T * weight
    hi, lo = split(mid)
    tail = []
    for part in (hi.astype(F32), lo.astype(F32)):
        for k in range(2):
            for j in range(nb):
                tail.append(part[k : k + 1, j * LANES : (j + 1) * LANES])
    tail = jnp.concatenate(tail, axis=0).astype(BF)

    def pack(i, carry):
        at = pl.multiple_of(core * half + i * piece, piece)
        col = turned[pl.ds(at, piece), :]
        for j in range(nb):
            cols = slice(j * LANES, (j + 1) * LANES)
            p = i * nb + j
            for m, (a, c) in enumerate(((0, 0), (0, 1), (1, 1))):
                put = slice(m * piece, (m + 1) * piece)
                value = mine[p, put, :] + got[p, put, :].astype(F32)
                value = value + col[:, a : a + 1] * gap[c : c + 1, cols]
                packed[p, put, :] = value.astype(BF)
            packed[p, 3 * piece :, :] = tail
        return carry

    lax.fori_loop(0, peers // nb, pack, 0)


def merge_kernel(dims, info, arrived, cov, mean_all, flat, dev, square):
    rows, ch, length, peers, piece = dims
    core, peer = info[0], info[2]
    nb = ch // LANES
    segments = length // rows
    total = 2 * (peers // segments) * (length - LAG)
    body = 3 * piece

    def add(p, acc):
        z = arrived[p, body:, :].astype(F32)
        flat[pl.ds(pl.multiple_of(p * 2 * nb, 2 * nb), 2 * nb), :] = z[: 2 * nb] + z[2 * nb :]
        return acc + arrived[p, :body, :].astype(F32)

    within = lax.fori_loop(0, peers, add, jnp.zeros((body, LANES), F32))
    seg = lax.rem(lax.broadcasted_iota(jnp.int32, (peers, 1), 0), segments)
    counts = 2.0 * jnp.where(seg == segments - 1, rows - LAG, rows).astype(F32)
    mean_all[...] = jnp.zeros_like(mean_all)
    for k in range(2):
        for j in range(nb):
            cols = slice(j * LANES, (j + 1) * LANES)
            v = flat[pl.ds(k * nb + j, peers, stride=2 * nb), :]
            mean = jnp.sum(v * counts, axis=0, keepdims=True) / total
            mean_all[k : k + 1, cols] = mean
            dev[k, :, cols] = v - mean
    start = core * (ch // 2) + (peer // nb) * piece
    block = pl.multiple_of((start // LANES) * LANES, LANES)
    inside = pl.multiple_of(lax.rem(start, LANES), piece)
    here = pl.multiple_of(lax.rem(peer, nb) * LANES, LANES)
    for m, (a, c) in enumerate(((0, 0), (0, 1), (1, 1))):
        left = dev[a, :, pl.ds(block, LANES)] * counts
        square[m] = dot(left, dev[c, :, pl.ds(here, LANES)], TN, HI)
    between = jnp.concatenate([square[m, pl.ds(inside, piece), :] for m in range(3)], axis=0)
    value = ((within + between) / total).astype(BF)
    cov[...] = jnp.broadcast_to(value[None], cov.shape)


def step_kernel(
    dims, info, half_cov, other_cov, mean_all, hid_hbm, sq_hbm, sq0_hbm, w_hbm,
    score, mine, other, dpre, cov, grads, hid, sq, sq0, w, sems,
):
    rows, ch, length, peers, piece = dims
    core = info[0]
    nb = ch // LANES
    half = ch // 2
    loads = [
        pltpu.make_async_copy(src, dst, sems.at[n])
        for n, (src, dst) in enumerate(((hid_hbm, hid), (sq_hbm, sq), (sq0_hbm, sq0), (w_hbm, w)))
    ]
    for load in loads:
        load.start()

    def place(i, carry):
        at = pl.multiple_of(core * half + i * piece, piece)
        to = pl.multiple_of((1 - core) * half + i * piece, piece)
        for m in range(3):
            for j in range(nb):
                cols = slice(j * LANES, (j + 1) * LANES)
                put = slice(m * piece, (m + 1) * piece)
                cov[m, pl.ds(at, piece), cols] = half_cov[i * nb + j, put, :].astype(F32)
                cov[m, pl.ds(to, piece), cols] = other_cov[i * nb + j, put, :].astype(F32)
        return carry

    lax.fori_loop(0, peers // nb, place, 0)
    row = lax.broadcasted_iota(jnp.int32, (ch, ch), 0)
    col = lax.broadcasted_iota(jnp.int32, (ch, ch), 1)
    unit = jnp.where(row == col, 1.0, 0.0).astype(F32)

    def forward(matrix):
        shifted = matrix + RIDGE * unit
        square = jnp.sum(shifted * shifted, keepdims=True)
        inv_scale = lax.rsqrt(square)
        a = shifted * inv_scale
        ab = a.astype(BF)
        a2 = dot(ab, ab)
        a2b = a2.astype(BF)
        rest = C1 * a + C2 * a2 + dot(a2b, (C3 * a + C4 * a2).astype(BF))
        root = jnp.sqrt(inv_scale)
        return a, ab, a2b, rest, inv_scale, root, C0 * root, (rest * root).astype(BF)

    def backward(a, ab, a2b, rest, inv_scale, root, grad):
        poly = C0 * unit + rest
        dscale = -0.5 * jnp.sum(grad * poly, keepdims=True) * root * inv_scale
        g = grad * root
        gb = g.astype(BF)
        y = dot(gb, ab)
        x = dot(a2b, gb)
        xs = x + x.T
        h = C2 * g + (0.5 * C3) * (y + y.T) + C4 * xs
        z = dot(ab, h.astype(BF))
        da = C1 * g + (0.5 * C3) * xs + z + z.T
        dscale = dscale - jnp.sum(da * a, keepdims=True) * inv_scale
        return da * inv_scale + dscale * a

    fe = forward(cov[0])
    fl = forward(cov[2])
    alpha, re = fe[6:]
    beta, rl = fl[6:]
    c = cov[1]
    cb = c.astype(BF)
    u = alpha * c + dot(re, cb)
    ub = u.astype(BF)
    vb = (beta * c + dot(cb, rl)).astype(BF)
    k = beta * u + dot(ub, rl)
    score[...] = jnp.broadcast_to(1.0 + jnp.sum(k * k, keepdims=True), score.shape)
    k2 = 2.0 * k
    kb = k2.astype(BF)
    rk = alpha * k2 + dot(re, kb)
    gc = beta * rk + dot(rk.astype(BF), rl)
    grads[ch : 2 * ch] = gc.T.astype(BF)
    grads[2 * ch : 3 * ch] = gc.astype(BF)
    gre = dot(kb, vb, NT)
    grads[:ch] = backward(*fe[:6], gre + gre.T).astype(BF)
    grl = dot(ub, kb, TN)
    grads[3 * ch :] = backward(*fl[:6], grl + grl.T).astype(BF)
    for load in loads:
        load.wait()
    conv_backward(dims, info, hid, sq, sq0, w, grads, mean_all, mine, other, dpre)


def conv_backward(dims, info, hid, sq, sq0, w, grads, mean_all, mine, other, dpre):
    rows, ch, length, peers, piece = dims
    core, segment = info[0], info[1]
    segments = length // rows
    half = ch // 2
    nh = half // LANES
    total = 2 * (peers // segments) * (length - LAG)
    grows = rows + 16
    t = segment * rows + lax.broadcasted_iota(jnp.int32, (grows, 1), 0)
    has_early = t < length - LAG
    has_later = jnp.logical_and(t >= LAG, t < length)
    out = hid[NL].astype(F32)
    base = out[HALO : HALO + grows]
    mean_e, mean_l = mean_all[0:1], mean_all[1:2]
    zero = jnp.zeros((1, ch), F32)
    consts = []
    for early_on in (True, False):
        left_e, left_l = mean_e, mean_l
        for _ in range(3):
            top_e, top_l = left_e.astype(BF).astype(F32), left_l.astype(BF).astype(F32)
            parts = [top_e, top_l, zero, zero] if early_on else [zero, zero, top_e, top_l]
            consts.append(jnp.concatenate(parts, axis=1))
            left_e, left_l = left_e - top_e, left_l - top_l
    consts = jnp.concatenate(consts + [jnp.zeros((10, 4 * ch), F32)], axis=0)
    lhs = jnp.concatenate(
        [
            jnp.where(has_early, base, 0.0),
            jnp.where(has_early, out[HALO + LAG : HALO + LAG + grows], 0.0),
            jnp.where(has_later, out[HALO - LAG : HALO - LAG + grows], 0.0),
            jnp.where(has_later, base, 0.0),
        ],
        axis=1,
    )
    lhs = jnp.concatenate([lhs, consts], axis=0).astype(BF)
    grad = dot(lhs, grads[...])
    off_early = grad[grows : grows + 1] + grad[grows + 1 : grows + 2] + grad[grows + 2 : grows + 3]
    off_later = grad[grows + 3 : grows + 4] + grad[grows + 4 : grows + 5] + grad[grows + 5 : grows + 6]
    grad = grad[:grows] - jnp.where(has_early, off_early, 0.0) - jnp.where(has_later, off_later, 0.0)
    grad = grad / total
    biases = [None] * (NL + 1)
    first = core == 0

    def halves(value):
        lo, hi = value[:, :half], value[:, half:]
        return jnp.where(first, lo, hi), jnp.where(first, hi, lo)

    def store(left, value, p0, count, size, at):
        for part, ref in zip(halves(value), (mine, other)):
            res = dot(left, part.astype(BF), TN).astype(BF)
            for j in range(nh):
                piece_j = res[:, j * LANES : (j + 1) * LANES].reshape(count, size, LANES)
                ref[p0 : p0 + count, at + j * size : at + (j + 1) * size, :] = piece_j

    conv_size = 2 * ch // peers
    for layer in reversed(range(NL)):
        step = 2**layer
        s = sq[layer, HALO : HALO + grows, :]
        pre = jnp.where(t < length, grad * (1.0 - s * s), 0.0).astype(BF)
        own = pre[:rows].astype(F32)
        biases[layer + 1] = jnp.sum(own, axis=0, keepdims=True)
        h = hid[layer].astype(F32)
        hist = pltpu.roll(h, step, 0)[HALO : HALO + rows].astype(BF)
        at = layer * nh * conv_size
        count = ch // conv_size
        store(hid[layer, HALO : HALO + rows, :], own, 0, count, conv_size, at)
        store(hist, own, count, count, conv_size, at)
        back = dot(pre, w[layer, ch:], NT)
        grad = grad + dot(pre, w[layer, :ch], NT) + pltpu.roll(back, grows - step, 0)
    s = sq0[...]
    own = (grad[:rows] * (1.0 - s * s)).astype(BF)
    dpre[...] = own
    biases[0] = jnp.sum(own.astype(F32), axis=0, keepdims=True)
    bias = jnp.concatenate(biases, axis=0)
    for part, ref in zip(halves(bias), (mine, other)):
        hi, lo = split(part)
        tail = []
        for value in (hi.astype(F32), lo.astype(F32)):
            for j in range(nh):
                tail.append(value[:, j * LANES : (j + 1) * LANES])
        tail = jnp.concatenate(tail, axis=0).astype(BF)
        at = ref.shape[1] - tail.shape[0]
        ref[:, at:, :] = jnp.broadcast_to(tail[None], (peers,) + tail.shape)


def product_kernel(info, left, dpre, res):
    res[...] = dot(left[...], dpre[...], TN)


def pack_kernel(nbias, info, earlier, left_got, dpre_got, mine, got, packed):
    count = packed.shape[0]
    ch = dpre_got.shape[1]
    size = left_got.shape[1] // count
    res = (earlier[...] + dot(left_got[...], dpre_got[...], TN)).astype(BF)
    for j in range(ch // LANES):
        part = res[:, j * LANES : (j + 1) * LANES].reshape(count, size, LANES)
        packed[:, j * size : (j + 1) * size, :] = part
    at = size * (ch // LANES)
    body = mine.shape[1] - 2 * nbias
    value = mine[...].astype(F32) + got[...].astype(F32)
    packed[:, at : at + body, :] = value[:, :body].astype(BF)
    bias = value[0, body : body + nbias] + value[0, body + nbias :]
    hi = bias.astype(BF).astype(F32)
    tail = jnp.concatenate([hi, bias - hi], axis=0).astype(BF)
    packed[:, at + body :, :] = jnp.broadcast_to(tail[None], (count,) + tail.shape)


def sum_kernel(sizes, arrived, half_a, half_b, bias):
    in_size, conv_size, nb = sizes
    peers, wide = arrived.shape[:2]
    nh = nb // 2

    def total_of(at, count):
        def add(p, acc):
            return acc + arrived[p, at : at + count, :].astype(F32)

        return lax.fori_loop(0, peers, add, jnp.zeros((count, LANES), F32), unroll=4)

    for side, ref in enumerate((half_a, half_b)):
        count = nh * in_size
        ref[:count] = total_of(side * count, count).astype(BF)
        ch = nh // 2 * conv_size
        for layer in range(NL):
            at = nb * in_size + (layer * nh) * conv_size + side * ch
            ref[count + layer * ch : count + (layer + 1) * ch] = total_of(at, ch).astype(BF)
    nbias = bias.shape[0]
    t = total_of(wide - 2 * nbias, 2 * nbias)
    bias[...] = t[:nbias] + t[nbias:]


def unpack_kernel(sizes, nbiases, inner_x, info, chunks, *refs):
    in_size, conv_size, nb, ny, nz, inner = sizes
    core, peer, inner_at, z_at = info[0], info[2], info[3], info[4]
    if nbiases:
        bias, bias_got = refs[:2]
        w_in, w_conv, b_in, b_conv = refs[-4:]
    else:
        w_in, w_conv = refs[-2:]
    nh = nb // 2
    half = nh * LANES
    ch = nh // 2 * conv_size
    for a, shift_a in enumerate(shifts(inner)):
        i = lax.rem(inner_at + inner - shift_a, inner)
        for b, shift_b in enumerate(shifts(nz)):
            z = lax.rem(z_at + nz - shift_b, nz)
            value = chunks[0, a, b].astype(F32)
            rows = pl.ds(pl.multiple_of(z * in_size, in_size), in_size)
            left = jnp.concatenate(
                [value[j * in_size : (j + 1) * in_size] for j in range(nh)], axis=1
            )
            crow = pl.ds(pl.multiple_of(z * conv_size, conv_size), conv_size)
            if inner_x:
                w_in[0, i, 0, rows, :] = left
            else:
                w_in[0, 0, i, rows, :] = left
            for layer in range(NL):
                at = nh * in_size + layer * ch
                part = jnp.concatenate(
                    [
                        value[at + j * conv_size : at + (j + 1) * conv_size]
                        for j in range(nh // 2)
                    ],
                    axis=1,
                )
                if inner_x:
                    w_conv[layer, i, 0, crow, :] = part
                else:
                    w_conv[layer, 0, i, crow, :] = part
    if nbiases:

        @pl.when(pl.program_id(0) == 0)
        def _():
            first = info[5] == 0
            n = NL + 1
            parts = []
            for side in range(2):
                mine_side = first if side == 0 else jnp.logical_not(first)
                value = jnp.where(mine_side, bias[...], bias_got[...])
                parts += [value[j * n : (j + 1) * n] for j in range(nh)]
            full = jnp.concatenate(parts, axis=1)
            b_in[...] = full[0]
            b_conv[...] = full[1:]


def per_device(frames, w_in, b_in, w_conv, b_conv):
    frames = frames[0]
    rows, features = frames.shape
    ch = w_in.shape[1]
    core = lax.axis_index("c")
    segment = lax.axis_index("tm")
    segments = lax.axis_size("tm")
    peers = lax.axis_size("x") * segments
    length = rows * segments
    nb = ch // LANES
    nh = nb // 2
    piece = (ch // 2) * nb // peers
    dims = (rows, ch, length, peers, piece)
    info = jnp.stack([core, segment, lax.axis_index("x") * segments + segment]).astype(jnp.int32)
    ext = rows + 2 * HALO
    frames_got = swap_core(frames)

    squash0 = jnp.tanh(jnp.dot(frames, w_in, preferred_element_type=F32) + b_in)
    own = squash0.astype(BF)
    before = shift_segment(own[rows - HALO :], 1)
    after = shift_segment(own[:HALO], -1)
    hid, sq, mine, other, means = call(
        functools.partial(forward_kernel, dims),
        [
            sds((NL + 1, ext, ch), BF),
            sds((NL, ext, ch), F32),
            sds((peers, 3 * piece, LANES), F32),
            sds((peers, 3 * piece, LANES), BF),
            sds((8, ch), F32),
        ],
        info, before, own, after, w_conv, b_conv,
        scratch=[pltpu.VMEM((3, ch, ch), F32)],
        vmem=36,
    )
    got, sib, frames_got = lax.optimization_barrier(
        (swap_core(other), swap_core(means), frames_got)
    )
    (packed,) = call(
        functools.partial(pair_kernel, dims),
        [sds((peers, 3 * piece + 4 * nb, LANES), BF)],
        info, mine, got, means, sib,
        scratch=[pltpu.VMEM((ch, 8), F32)],
    )
    cov, mean_all = call(
        functools.partial(merge_kernel, dims),
        [sds((peers, 3 * piece, LANES), BF), sds((8, ch), F32)],
        info, exchange(packed),
        scratch=[
            pltpu.VMEM((peers * 2 * nb, LANES), F32),
            pltpu.VMEM((2, peers, ch), F32),
            pltpu.VMEM((3, LANES, LANES), F32),
        ],
    )
    cov = exchange(cov)
    half_features = features // 2
    in_size = half_features // peers
    conv_size = 2 * ch // peers
    nbias = (NL + 1) * nh
    conv_wide = NL * nh * conv_size + 2 * nbias
    body = nb * in_size + NL * nh * conv_size
    wide = body + 2 * nbias
    vmem = pl.BlockSpec(memory_space=pltpu.VMEM)
    smem = pl.BlockSpec(memory_space=pltpu.SMEM)
    hbm = pl.BlockSpec(memory_space=pl.ANY)
    params = pltpu.CompilerParams(vmem_limit_bytes=40 * 2**20)
    small_params = pltpu.CompilerParams(vmem_limit_bytes=16 * 2**20)
    score, mine, other, dpre = pl.pallas_call(
        functools.partial(step_kernel, dims),
        out_shape=[
            sds((8, LANES), F32),
            sds((peers, conv_wide, LANES), BF),
            sds((peers, conv_wide, LANES), BF),
            sds((rows, ch), BF),
        ],
        in_specs=[smem, vmem, vmem, vmem, hbm, hbm, hbm, hbm],
        out_specs=[vmem] * 4,
        scratch_shapes=[
            pltpu.VMEM((3, ch, ch), F32),
            pltpu.VMEM((4 * ch, ch), BF),
            pltpu.VMEM(hid.shape, BF),
            pltpu.VMEM(sq.shape, F32),
            pltpu.VMEM(squash0.shape, F32),
            pltpu.VMEM(w_conv.shape, BF),
            pltpu.SemaphoreType.DMA((4,)),
        ],
        compiler_params=params,
    )(info, cov, swap_core(cov), mean_all, hid, sq, squash0, w_conv)
    steps = 4
    group = peers // steps
    tile = group * in_size
    whole = pl.BlockSpec((rows, ch), lambda i, at: (0, 0))
    conv_spec = pl.BlockSpec((group, conv_wide, LANES), lambda i, at: (i, 0, 0))
    left_spec = pl.BlockSpec((rows, tile), lambda i, at: (0, at[0] * steps + i))
    res_spec = pl.BlockSpec((tile, ch), lambda i, at: (i, 0))
    dpre_got, got = swap_core(dpre), swap_core(other)
    earlier = pl.pallas_call(
        product_kernel,
        grid_spec=pltpu.PrefetchScalarGridSpec(
            num_scalar_prefetch=1,
            grid=(steps,),
            in_specs=[left_spec, whole],
            out_specs=res_spec,
        ),
        out_shape=sds((half_features, ch), F32),
        compiler_params=small_params,
        cost_estimate=pl.CostEstimate(
            flops=2 * rows * half_features * ch, bytes_accessed=6 * 2**20, transcendentals=0
        ),
    )(info, frames, dpre)
    packed = pl.pallas_call(
        functools.partial(pack_kernel, nbias),
        grid_spec=pltpu.PrefetchScalarGridSpec(
            num_scalar_prefetch=1,
            grid=(steps,),
            in_specs=[res_spec, left_spec, whole, conv_spec, conv_spec],
            out_specs=pl.BlockSpec((group, wide, LANES), lambda i, at: (i, 0, 0)),
        ),
        out_shape=sds((peers, wide, LANES), BF),
        compiler_params=small_params,
    )(info, earlier, frames_got, dpre_got, mine, got)
    nz = grid_side(segments)
    ny = segments // nz
    nx = peers // segments
    part = nh * in_size + NL * (nh // 2) * conv_size
    half_a, half_b, bias = pl.pallas_call(
        functools.partial(sum_kernel, (in_size, conv_size, nb)),
        in_specs=[vmem],
        out_specs=[vmem] * 3,
        out_shape=[sds((part, LANES), BF), sds((part, LANES), BF), sds((nbias, LANES), F32)],
        compiler_params=small_params,
    )(exchange(packed))
    both = along(jnp.stack([half_a, half_b]), "z", nz)
    plane_a, plane_b = lax.optimization_barrier(
        (along(both[:, 0], "y", ny), along(both[:, 1], "x", nx))
    )
    full_a, full_b = along(plane_a, "x", nx), along(plane_b, "y", ny)
    bias_got = swap_core(bias)
    full_a, full_b, bias_got = lax.optimization_barrier((full_a, full_b, bias_got))
    peer = lax.axis_index("x") * segments + segment
    place = jnp.stack([lax.axis_index("x"), segment // nz, segment % nz])

    def unpack(chunks, side, inner_x, owner, biases, earlier):
        spare = [sds((ch,), F32), sds((NL, ch), F32)] if biases else []
        outer, inner = (ny, nx) if inner_x else (nx, ny)
        outer_at, inner_at = (place[1], place[0]) if inner_x else (place[0], place[1])
        table = [lax.rem(outer_at + outer - k, outer) for k in shifts(outer)]
        head = [owner, outer_at, peer, inner_at, place[2], core]
        info = jnp.stack(head + table).astype(jnp.int32)
        if inner_x:
            in_map = lambda i, at: (at[0], 0, at[6 + i], 0, side)
            conv_map = lambda i, at: (0, 0, at[6 + i], 0, 2 * at[0] + side)
            xs, ys = nx, 1
        else:
            in_map = lambda i, at: (at[0], at[6 + i], 0, 0, side)
            conv_map = lambda i, at: (0, at[6 + i], 0, 0, 2 * at[0] + side)
            xs, ys = 1, ny
        return pl.pallas_call(
            functools.partial(
                unpack_kernel, (in_size, conv_size, nb, ny, nz, inner), len(biases), inner_x
            ),
            grid_spec=pltpu.PrefetchScalarGridSpec(
                num_scalar_prefetch=1,
                grid=(outer,),
                in_specs=[
                    pl.BlockSpec((1, inner, nz, part, LANES), lambda i, at: (i, 0, 0, 0, 0))
                ]
                + [pl.BlockSpec(b.shape, lambda i, at: (0, 0)) for b in biases]
                + [hbm] * len(earlier),
                out_specs=[
                    pl.BlockSpec((1, xs, ys, nz * in_size, ch // 2), in_map),
                    pl.BlockSpec((NL, xs, ys, nz * conv_size, ch // 4), conv_map),
                ]
                + [pl.BlockSpec(b.shape, lambda i, at, n=len(b.shape): (0,) * n) for b in spare],
            ),
            out_shape=[
                sds((2, nx, ny, nz * in_size, ch), F32),
                sds((NL, nx, ny, nz * conv_size, ch), F32),
            ]
            + spare,
            input_output_aliases={2 + len(biases) + n: n for n in range(len(earlier))},
            compiler_params=small_params,
            cost_estimate=pl.CostEstimate(flops=0, bytes_accessed=6 * 2**20, transcendentals=0),
        )(info, chunks, *biases, *earlier)

    got_a, got_b = swap_core(full_a), swap_core(full_b)
    partial = unpack(full_a, 0, False, core, [], [])
    partial = unpack(full_b, 1, True, core, [], partial)
    partial = unpack(got_a, 0, False, 1 - core, [], partial)
    g_in, g_conv, g_b_in, g_b_conv = unpack(got_b, 1, True, 1 - core, [bias, bias_got], partial)
    return (
        score[0, 0],
        g_in.reshape(features, ch),
        g_b_in,
        g_conv.reshape(NL, 2 * ch, ch),
        g_b_conv,
    )


def solution(mesh):
    devices = mesh.devices
    trajs, segments = devices.shape
    inner = Mesh(devices.reshape(trajs // 2, 2, segments), ("x", "c", "tm"))
    return jax.shard_map(
        per_device,
        mesh=inner,
        in_specs=(P(("x", "c"), "tm", None), P(), P(), P(), P()),
        out_specs=(P(), P(), P(), P(), P()),
        check_vma=False,
    )
```

```python
import functools

import jax
import jax.numpy as jnp
from jax import lax
from jax.experimental import pallas as pl
from jax.experimental.pallas import tpu as pltpu
from jax.sharding import Mesh, PartitionSpec as P

NL = 3
LAG = 16
RIDGE = 0.0001
HALO = 32
LANES = 128
BF = jnp.bfloat16
F32 = jnp.float32
PEERS = ("x", "tm")
HI = lax.Precision.HIGHEST
C0, C1, C2, C3, C4 = 2.25, -2.4375, 1.6875, -0.5625, 0.0625

NN = (((1,), (0,)), ((), ()))
NT = (((1,), (1,)), ((), ()))
TN = (((0,), (0,)), ((), ()))


def dot(a, b, dims=NN, precision=None):
    return lax.dot_general(a, b, dims, precision=precision, preferred_element_type=F32)


def split(a):
    hi = a.astype(BF)
    return hi, (a - hi.astype(F32)).astype(BF)


def dot3(a, b, dims=NN):
    return dot(a[0], b[0], dims) + (dot(a[0], b[1], dims) + dot(a[1], b[0], dims))


def swap_core(value):
    return lax.ppermute(value, "c", [(0, 1), (1, 0)])


def shift_segment(value, steps):
    count = lax.axis_size("tm")
    first, last = max(0, -steps), min(count, count - steps)
    return lax.ppermute(value, "tm", [(i, i + steps) for i in range(first, last)])


def shifts(count):
    return (0, 1, 3, 2) if count == 4 else tuple(range(count))


def spin(value, axis, steps):
    segments = lax.axis_size("tm")
    nz = grid_side(segments)
    ny = segments // nz
    if axis == "x":
        n = lax.axis_size("x")
        return lax.ppermute(value, "x", [(i, (i + steps) % n) for i in range(n)])
    pairs = []
    for i in range(segments):
        y, z = divmod(i, nz)
        y, z = ((y + steps) % ny, z) if axis == "y" else (y, (z + steps) % nz)
        pairs.append((i, y * nz + z))
    return lax.ppermute(value, "tm", pairs)


def grid_side(count):
    side = 1
    while (side * 2) * (side * 2) <= count:
        side *= 2
    return side


def along(value, axis, count):
    return jnp.stack([value] + [spin(value, axis, k) for k in shifts(count)[1:]])


def exchange(value):
    return lax.all_to_all(value, PEERS, 0, 0, tiled=True)


def call(kernel, outs, *args, scratch=(), vmem=16):
    specs = [
        pl.BlockSpec(memory_space=pltpu.SMEM if a.dtype == jnp.int32 else pltpu.VMEM) for a in args
    ]
    return pl.pallas_call(
        kernel,
        out_shape=outs,
        in_specs=specs,
        out_specs=[pl.BlockSpec(memory_space=pltpu.VMEM) for _ in outs],
        scratch_shapes=list(scratch),
        compiler_params=pltpu.CompilerParams(vmem_limit_bytes=vmem * 2**20),
    )(*args)


def sds(shape, dtype):
    return jax.ShapeDtypeStruct(shape, dtype)


def forward_kernel(dims, info, before, own, after, w, b, hid, sq, mine, other, means, mom):
    rows, ch, length, peers, piece = dims
    core, segment = info[0], info[1]
    ext = rows + 2 * HALO
    nb = ch // LANES
    t = segment * rows - HALO + lax.broadcasted_iota(jnp.int32, (ext, 1), 0)
    h = jnp.concatenate(
        [before[...].astype(F32), own[...].astype(F32), after[...].astype(F32)], axis=0
    )
    for layer in range(NL):
        hb = h.astype(BF)
        hid[layer] = hb
        hist = pltpu.roll(h, 2**layer, 0).astype(BF)
        s = jnp.tanh(dot(hb, w[layer, :ch]) + dot(hist, w[layer, ch:]) + b[layer : layer + 1])
        sq[layer] = s
        h = jnp.where(t >= 0, (h + s).astype(BF).astype(F32), 0.0)
    hid[NL] = h.astype(BF)
    tp = segment * rows + lax.broadcasted_iota(jnp.int32, (rows, 1), 0)
    pair = jnp.where(tp < length - LAG, 1.0, 0.0).astype(F32)
    last = segment == length // rows - 1
    count = jnp.where(last, rows - LAG, rows).astype(F32)
    early = h[HALO : HALO + rows] * pair
    later = h[HALO + LAG : HALO + LAG + rows] * pair
    mean_e = jnp.sum(early, axis=0, keepdims=True) / count
    mean_l = jnp.sum(later, axis=0, keepdims=True) / count
    means[...] = jnp.concatenate([mean_e, mean_l, jnp.zeros((6, ch), F32)], axis=0)
    ce = split((early - mean_e) * pair)
    cl = split((later - mean_l) * pair)
    left_e = jnp.concatenate([ce[0], ce[0], ce[1]], axis=0)
    left_l = jnp.concatenate([cl[0], cl[0], cl[1]], axis=0)
    right_e = jnp.concatenate([ce[0], ce[1], ce[0]], axis=0)
    right_l = jnp.concatenate([cl[0], cl[1], cl[0]], axis=0)
    mom[0] = dot(left_e, right_e, TN)
    mom[1] = dot(left_e, right_l, TN)
    mom[2] = dot(left_l, right_l, TN)
    half = ch // 2

    def pack(i, carry):
        at = pl.multiple_of(core * half + i * piece, piece)
        to = pl.multiple_of((1 - core) * half + i * piece, piece)
        for m in range(3):
            for j in range(nb):
                cols = slice(j * LANES, (j + 1) * LANES)
                put = slice(m * piece, (m + 1) * piece)
                mine[i * nb + j, put, :] = mom[m, pl.ds(at, piece), cols]
                other[i * nb + j, put, :] = mom[m, pl.ds(to, piece), cols].astype(BF)
        return carry

    lax.fori_loop(0, peers // nb, pack, 0)


def pair_kernel(dims, info, mine, got, means, sib, packed, turned):
    rows, ch, length, peers, piece = dims
    core, segment = info[0], info[1]
    nb = ch // LANES
    half = ch // 2
    last = segment == length // rows - 1
    weight = 0.5 * jnp.where(last, rows - LAG, rows).astype(F32)
    gap = means[...] - sib[...]
    mid = 0.5 * (means[...] + sib[...])
    turned[...] = gap.T * weight
    hi, lo = split(mid)
    tail = []
    for part in (hi.astype(F32), lo.astype(F32)):
        for k in range(2):
            for j in range(nb):
                tail.append(part[k : k + 1, j * LANES : (j + 1) * LANES])
    tail = jnp.concatenate(tail, axis=0).astype(BF)

    def pack(i, carry):
        at = pl.multiple_of(core * half + i * piece, piece)
        col = turned[pl.ds(at, piece), :]
        for j in range(nb):
            cols = slice(j * LANES, (j + 1) * LANES)
            p = i * nb + j
            for m, (a, c) in enumerate(((0, 0), (0, 1), (1, 1))):
                put = slice(m * piece, (m + 1) * piece)
                value = mine[p, put, :] + got[p, put, :].astype(F32)
                value = value + col[:, a : a + 1] * gap[c : c + 1, cols]
                packed[p, put, :] = value.astype(BF)
            packed[p, 3 * piece :, :] = tail
        return carry

    lax.fori_loop(0, peers // nb, pack, 0)


def merge_kernel(dims, info, arrived, cov, mean_all, flat, dev, square):
    rows, ch, length, peers, piece = dims
    core, peer = info[0], info[2]
    nb = ch // LANES
    segments = length // rows
    total = 2 * (peers // segments) * (length - LAG)
    body = 3 * piece

    def add(p, acc):
        z = arrived[p, body:, :].astype(F32)
        flat[pl.ds(pl.multiple_of(p * 2 * nb, 2 * nb), 2 * nb), :] = z[: 2 * nb] + z[2 * nb :]
        return acc + arrived[p, :body, :].astype(F32)

    within = lax.fori_loop(0, peers, add, jnp.zeros((body, LANES), F32))
    seg = lax.rem(lax.broadcasted_iota(jnp.int32, (peers, 1), 0), segments)
    counts = 2.0 * jnp.where(seg == segments - 1, rows - LAG, rows).astype(F32)
    mean_all[...] = jnp.zeros_like(mean_all)
    for k in range(2):
        for j in range(nb):
            cols = slice(j * LANES, (j + 1) * LANES)
            v = flat[pl.ds(k * nb + j, peers, stride=2 * nb), :]
            mean = jnp.sum(v * counts, axis=0, keepdims=True) / total
            mean_all[k : k + 1, cols] = mean
            dev[k, :, cols] = v - mean
    start = core * (ch // 2) + (peer // nb) * piece
    block = pl.multiple_of((start // LANES) * LANES, LANES)
    inside = pl.multiple_of(lax.rem(start, LANES), piece)
    here = pl.multiple_of(lax.rem(peer, nb) * LANES, LANES)
    for m, (a, c) in enumerate(((0, 0), (0, 1), (1, 1))):
        left = dev[a, :, pl.ds(block, LANES)] * counts
        square[m] = dot(left, dev[c, :, pl.ds(here, LANES)], TN, HI)
    between = jnp.concatenate([square[m, pl.ds(inside, piece), :] for m in range(3)], axis=0)
    value = ((within + between) / total).astype(BF)
    cov[...] = jnp.broadcast_to(value[None], cov.shape)


def step_kernel(
    dims, info, half_cov, other_cov, mean_all, hid_hbm, sq_hbm, sq0_hbm, w_hbm,
    score, mine, other, dpre, cov, grads, hid, sq, sq0, w, sems,
):
    rows, ch, length, peers, piece = dims
    core = info[0]
    nb = ch // LANES
    half = ch // 2
    loads = [
        pltpu.make_async_copy(src, dst, sems.at[n])
        for n, (src, dst) in enumerate(((hid_hbm, hid), (sq_hbm, sq), (sq0_hbm, sq0), (w_hbm, w)))
    ]
    for load in loads:
        load.start()

    def place(i, carry):
        at = pl.multiple_of(core * half + i * piece, piece)
        to = pl.multiple_of((1 - core) * half + i * piece, piece)
        for m in range(3):
            for j in range(nb):
                cols = slice(j * LANES, (j + 1) * LANES)
                put = slice(m * piece, (m + 1) * piece)
                cov[m, pl.ds(at, piece), cols] = half_cov[i * nb + j, put, :].astype(F32)
                cov[m, pl.ds(to, piece), cols] = other_cov[i * nb + j, put, :].astype(F32)
        return carry

    lax.fori_loop(0, peers // nb, place, 0)
    row = lax.broadcasted_iota(jnp.int32, (ch, ch), 0)
    col = lax.broadcasted_iota(jnp.int32, (ch, ch), 1)
    unit = jnp.where(row == col, 1.0, 0.0).astype(F32)

    def forward(matrix):
        shifted = matrix + RIDGE * unit
        square = jnp.sum(shifted * shifted, keepdims=True)
        inv_scale = lax.rsqrt(square)
        a = shifted * inv_scale
        ab = a.astype(BF)
        a2 = dot(ab, ab)
        a2b = a2.astype(BF)
        rest = C1 * a + C2 * a2 + dot(a2b, (C3 * a + C4 * a2).astype(BF))
        root = jnp.sqrt(inv_scale)
        return a, ab, a2b, rest, inv_scale, root, C0 * root, (rest * root).astype(BF)

    def backward(a, ab, a2b, rest, inv_scale, root, grad):
        poly = C0 * unit + rest
        dscale = -0.5 * jnp.sum(grad * poly, keepdims=True) * root * inv_scale
        g = grad * root
        gb = g.astype(BF)
        y = dot(gb, ab)
        x = dot(a2b, gb)
        xs = x + x.T
        h = C2 * g + (0.5 * C3) * (y + y.T) + C4 * xs
        z = dot(ab, h.astype(BF))
        da = C1 * g + (0.5 * C3) * xs + z + z.T
        dscale = dscale - jnp.sum(da * a, keepdims=True) * inv_scale
        return da * inv_scale + dscale * a

    fe = forward(cov[0])
    fl = forward(cov[2])
    alpha, re = fe[6:]
    beta, rl = fl[6:]
    c = cov[1]
    cb = c.astype(BF)
    u = alpha * c + dot(re, cb)
    ub = u.astype(BF)
    vb = (beta * c + dot(cb, rl)).astype(BF)
    k = beta * u + dot(ub, rl)
    score[...] = jnp.broadcast_to(1.0 + jnp.sum(k * k, keepdims=True), score.shape)
    k2 = 2.0 * k
    kb = k2.astype(BF)
    rk = alpha * k2 + dot(re, kb)
    gc = beta * rk + dot(rk.astype(BF), rl)
    grads[ch : 2 * ch] = gc.T.astype(BF)
    grads[2 * ch : 3 * ch] = gc.astype(BF)
    gre = dot(kb, vb, NT)
    grads[:ch] = backward(*fe[:6], gre + gre.T).astype(BF)
    grl = dot(ub, kb, TN)
    grads[3 * ch :] = backward(*fl[:6], grl + grl.T).astype(BF)
    for load in loads:
        load.wait()
    conv_backward(dims, info, hid, sq, sq0, w, grads, mean_all, mine, other, dpre)


def conv_backward(dims, info, hid, sq, sq0, w, grads, mean_all, mine, other, dpre):
    rows, ch, length, peers, piece = dims
    core, segment = info[0], info[1]
    segments = length // rows
    half = ch // 2
    nh = half // LANES
    total = 2 * (peers // segments) * (length - LAG)
    grows = rows + 16
    t = segment * rows + lax.broadcasted_iota(jnp.int32, (grows, 1), 0)
    has_early = t < length - LAG
    has_later = jnp.logical_and(t >= LAG, t < length)
    out = hid[NL].astype(F32)
    base = out[HALO : HALO + grows]
    mean_e, mean_l = mean_all[0:1], mean_all[1:2]
    zero = jnp.zeros((1, ch), F32)
    consts = []
    for early_on in (True, False):
        left_e, left_l = mean_e, mean_l
        for _ in range(3):
            top_e, top_l = left_e.astype(BF).astype(F32), left_l.astype(BF).astype(F32)
            parts = [top_e, top_l, zero, zero] if early_on else [zero, zero, top_e, top_l]
            consts.append(jnp.concatenate(parts, axis=1))
            left_e, left_l = left_e - top_e, left_l - top_l
    consts = jnp.concatenate(consts + [jnp.zeros((10, 4 * ch), F32)], axis=0)
    lhs = jnp.concatenate(
        [
            jnp.where(has_early, base, 0.0),
            jnp.where(has_early, out[HALO + LAG : HALO + LAG + grows], 0.0),
            jnp.where(has_later, out[HALO - LAG : HALO - LAG + grows], 0.0),
            jnp.where(has_later, base, 0.0),
        ],
        axis=1,
    )
    lhs = jnp.concatenate([lhs, consts], axis=0).astype(BF)
    grad = dot(lhs, grads[...])
    off_early = grad[grows : grows + 1] + grad[grows + 1 : grows + 2] + grad[grows + 2 : grows + 3]
    off_later = grad[grows + 3 : grows + 4] + grad[grows + 4 : grows + 5] + grad[grows + 5 : grows + 6]
    grad = grad[:grows] - jnp.where(has_early, off_early, 0.0) - jnp.where(has_later, off_later, 0.0)
    grad = grad / total
    biases = [None] * (NL + 1)
    first = core == 0

    def halves(value):
        lo, hi = value[:, :half], value[:, half:]
        return jnp.where(first, lo, hi), jnp.where(first, hi, lo)

    def store(left, value, p0, count, size, at):
        for part, ref in zip(halves(value), (mine, other)):
            res = dot(left, part.astype(BF), TN).astype(BF)
            for j in range(nh):
                piece_j = res[:, j * LANES : (j + 1) * LANES].reshape(count, size, LANES)
                ref[p0 : p0 + count, at + j * size : at + (j + 1) * size, :] = piece_j

    conv_size = 2 * ch // peers
    for layer in reversed(range(NL)):
        step = 2**layer
        s = sq[layer, HALO : HALO + grows, :]
        pre = jnp.where(t < length, grad * (1.0 - s * s), 0.0).astype(BF)
        own = pre[:rows].astype(F32)
        biases[layer + 1] = jnp.sum(own, axis=0, keepdims=True)
        h = hid[layer].astype(F32)
        hist = pltpu.roll(h, step, 0)[HALO : HALO + rows].astype(BF)
        at = layer * nh * conv_size
        count = ch // conv_size
        store(hid[layer, HALO : HALO + rows, :], own, 0, count, conv_size, at)
        store(hist, own, count, count, conv_size, at)
        back = dot(pre, w[layer, ch:], NT)
        grad = grad + dot(pre, w[layer, :ch], NT) + pltpu.roll(back, grows - step, 0)
    s = sq0[...]
    own = (grad[:rows] * (1.0 - s * s)).astype(BF)
    dpre[...] = own
    biases[0] = jnp.sum(own.astype(F32), axis=0, keepdims=True)
    bias = jnp.concatenate(biases, axis=0)
    for part, ref in zip(halves(bias), (mine, other)):
        hi, lo = split(part)
        tail = []
        for value in (hi.astype(F32), lo.astype(F32)):
            for j in range(nh):
                tail.append(value[:, j * LANES : (j + 1) * LANES])
        tail = jnp.concatenate(tail, axis=0).astype(BF)
        at = ref.shape[1] - tail.shape[0]
        ref[:, at:, :] = jnp.broadcast_to(tail[None], (peers,) + tail.shape)


def product_kernel(info, left, dpre, res):
    res[...] = dot(left[...], dpre[...], TN)


def pack_kernel(nbias, info, earlier, left_got, dpre_got, mine, got, packed):
    count = packed.shape[0]
    ch = dpre_got.shape[1]
    size = left_got.shape[1] // count
    res = (earlier[...] + dot(left_got[...], dpre_got[...], TN)).astype(BF)
    for j in range(ch // LANES):
        part = res[:, j * LANES : (j + 1) * LANES].reshape(count, size, LANES)
        packed[:, j * size : (j + 1) * size, :] = part
    at = size * (ch // LANES)
    body = mine.shape[1] - 2 * nbias
    value = mine[...].astype(F32) + got[...].astype(F32)
    packed[:, at : at + body, :] = value[:, :body].astype(BF)
    bias = value[0, body : body + nbias] + value[0, body + nbias :]
    hi = bias.astype(BF).astype(F32)
    tail = jnp.concatenate([hi, bias - hi], axis=0).astype(BF)
    packed[:, at + body :, :] = jnp.broadcast_to(tail[None], (count,) + tail.shape)


def sum_kernel(sizes, arrived, half_a, half_b, bias):
    in_size, conv_size, nb = sizes
    peers, wide = arrived.shape[:2]
    nh = nb // 2

    def total_of(at, count):
        def add(p, acc):
            return acc + arrived[p, at : at + count, :].astype(F32)

        return lax.fori_loop(0, peers, add, jnp.zeros((count, LANES), F32), unroll=4)

    for side, ref in enumerate((half_a, half_b)):
        count = nh * in_size
        ref[:count] = total_of(side * count, count).astype(BF)
        ch = nh // 2 * conv_size
        for layer in range(NL):
            at = nb * in_size + (layer * nh) * conv_size + side * ch
            ref[count + layer * ch : count + (layer + 1) * ch] = total_of(at, ch).astype(BF)
    nbias = bias.shape[0]
    t = total_of(wide - 2 * nbias, 2 * nbias)
    bias[...] = t[:nbias] + t[nbias:]


def unpack_kernel(sizes, nbiases, info, left, right, *refs):
    in_size, conv_size, nb, nz = sizes
    z_at = info[1]
    if nbiases:
        bias, bias_got = refs[:2]
        w_in, w_conv, b_in, b_conv = refs[-4:]
    else:
        w_in, w_conv = refs[-2:]
    nh = nb // 2
    for b, shift in enumerate(shifts(nz)):
        z = lax.rem(z_at + nz - shift, nz)
        rows = pl.ds(pl.multiple_of(z * in_size, in_size), in_size)
        conv_rows = pl.ds(pl.multiple_of(z * conv_size, conv_size), conv_size)
        for side, ref in enumerate((left, right)):
            value = ref[0, 0, 0, b].astype(F32)
            for j in range(nh):
                col = (side * nh + j) * LANES
                w_in[0, 0, rows, col : col + LANES] = value[j * in_size : (j + 1) * in_size]
            for layer in range(NL):
                for j in range(nh // 2):
                    at = nh * in_size + (layer * (nh // 2) + j) * conv_size
                    col = (side * (nh // 2) + j) * LANES
                    part = value[at : at + conv_size]
                    w_conv[layer, 0, conv_rows, col : col + LANES] = part
    if nbiases:

        @pl.when(pl.program_id(0) == 0)
        def _():
            first = info[0] == 1
            n = NL + 1
            parts = []
            for side in range(2):
                mine_side = first if side == 0 else jnp.logical_not(first)
                value = jnp.where(mine_side, bias[...], bias_got[...])
                parts += [value[j * n : (j + 1) * n] for j in range(nh)]
            full = jnp.concatenate(parts, axis=1)
            b_in[...] = full[0]
            b_conv[...] = full[1:]


def per_device(frames, w_in, b_in, w_conv, b_conv):
    frames = frames[0]
    rows, features = frames.shape
    ch = w_in.shape[1]
    core = lax.axis_index("c")
    segment = lax.axis_index("tm")
    segments = lax.axis_size("tm")
    peers = lax.axis_size("x") * segments
    length = rows * segments
    nb = ch // LANES
    nh = nb // 2
    piece = (ch // 2) * nb // peers
    dims = (rows, ch, length, peers, piece)
    info = jnp.stack([core, segment, lax.axis_index("x") * segments + segment]).astype(jnp.int32)
    ext = rows + 2 * HALO
    frames_got = swap_core(frames)

    squash0 = jnp.tanh(jnp.dot(frames, w_in, preferred_element_type=F32) + b_in)
    own = squash0.astype(BF)
    before = shift_segment(own[rows - HALO :], 1)
    after = shift_segment(own[:HALO], -1)
    hid, sq, mine, other, means = call(
        functools.partial(forward_kernel, dims),
        [
            sds((NL + 1, ext, ch), BF),
            sds((NL, ext, ch), F32),
            sds((peers, 3 * piece, LANES), F32),
            sds((peers, 3 * piece, LANES), BF),
            sds((8, ch), F32),
        ],
        info, before, own, after, w_conv, b_conv,
        scratch=[pltpu.VMEM((3, ch, ch), F32)],
        vmem=36,
    )
    got, sib, frames_got = lax.optimization_barrier(
        (swap_core(other), swap_core(means), frames_got)
    )
    (packed,) = call(
        functools.partial(pair_kernel, dims),
        [sds((peers, 3 * piece + 4 * nb, LANES), BF)],
        info, mine, got, means, sib,
        scratch=[pltpu.VMEM((ch, 8), F32)],
    )
    cov, mean_all = call(
        functools.partial(merge_kernel, dims),
        [sds((peers, 3 * piece, LANES), BF), sds((8, ch), F32)],
        info, exchange(packed),
        scratch=[
            pltpu.VMEM((peers * 2 * nb, LANES), F32),
            pltpu.VMEM((2, peers, ch), F32),
            pltpu.VMEM((3, LANES, LANES), F32),
        ],
    )
    cov = exchange(cov)
    half_features = features // 2
    in_size = half_features // peers
    conv_size = 2 * ch // peers
    nbias = (NL + 1) * nh
    conv_wide = NL * nh * conv_size + 2 * nbias
    body = nb * in_size + NL * nh * conv_size
    wide = body + 2 * nbias
    vmem = pl.BlockSpec(memory_space=pltpu.VMEM)
    smem = pl.BlockSpec(memory_space=pltpu.SMEM)
    hbm = pl.BlockSpec(memory_space=pl.ANY)
    params = pltpu.CompilerParams(vmem_limit_bytes=40 * 2**20)
    small_params = pltpu.CompilerParams(vmem_limit_bytes=16 * 2**20)
    score, mine, other, dpre = pl.pallas_call(
        functools.partial(step_kernel, dims),
        out_shape=[
            sds((8, LANES), F32),
            sds((peers, conv_wide, LANES), BF),
            sds((peers, conv_wide, LANES), BF),
            sds((rows, ch), BF),
        ],
        in_specs=[smem, vmem, vmem, vmem, hbm, hbm, hbm, hbm],
        out_specs=[vmem] * 4,
        scratch_shapes=[
            pltpu.VMEM((3, ch, ch), F32),
            pltpu.VMEM((4 * ch, ch), BF),
            pltpu.VMEM(hid.shape, BF),
            pltpu.VMEM(sq.shape, F32),
            pltpu.VMEM(squash0.shape, F32),
            pltpu.VMEM(w_conv.shape, BF),
            pltpu.SemaphoreType.DMA((4,)),
        ],
        compiler_params=params,
    )(info, cov, swap_core(cov), mean_all, hid, sq, squash0, w_conv)
    steps = 4
    group = peers // steps
    tile = group * in_size
    whole = pl.BlockSpec((rows, ch), lambda i, at: (0, 0))
    conv_spec = pl.BlockSpec((group, conv_wide, LANES), lambda i, at: (i, 0, 0))
    left_spec = pl.BlockSpec((rows, tile), lambda i, at: (0, at[0] * steps + i))
    res_spec = pl.BlockSpec((tile, ch), lambda i, at: (i, 0))
    dpre_got, got = swap_core(dpre), swap_core(other)
    earlier = pl.pallas_call(
        product_kernel,
        grid_spec=pltpu.PrefetchScalarGridSpec(
            num_scalar_prefetch=1,
            grid=(steps,),
            in_specs=[left_spec, whole],
            out_specs=res_spec,
        ),
        out_shape=sds((half_features, ch), F32),
        compiler_params=small_params,
        cost_estimate=pl.CostEstimate(
            flops=2 * rows * half_features * ch, bytes_accessed=6 * 2**20, transcendentals=0
        ),
    )(info, frames, dpre)
    packed = pl.pallas_call(
        functools.partial(pack_kernel, nbias),
        grid_spec=pltpu.PrefetchScalarGridSpec(
            num_scalar_prefetch=1,
            grid=(steps,),
            in_specs=[res_spec, left_spec, whole, conv_spec, conv_spec],
            out_specs=pl.BlockSpec((group, wide, LANES), lambda i, at: (i, 0, 0)),
        ),
        out_shape=sds((peers, wide, LANES), BF),
        compiler_params=small_params,
    )(info, earlier, frames_got, dpre_got, mine, got)
    nz = grid_side(segments)
    ny = segments // nz
    nx = peers // segments
    part = nh * in_size + NL * (nh // 2) * conv_size
    half_a, half_b, bias = pl.pallas_call(
        functools.partial(sum_kernel, (in_size, conv_size, nb)),
        in_specs=[vmem],
        out_specs=[vmem] * 3,
        out_shape=[sds((part, LANES), BF), sds((part, LANES), BF), sds((nbias, LANES), F32)],
        compiler_params=small_params,
    )(exchange(packed))
    both = along(jnp.stack([half_a, half_b]), "z", nz)
    plane_a, plane_b = lax.optimization_barrier(
        (along(both[:, 0], "y", ny), along(both[:, 1], "x", nx))
    )
    full = jnp.stack([along(plane_a, "x", nx), along(plane_b, "y", ny)])
    full, bias = lax.optimization_barrier((full, bias))
    places = nx * ny

    def slots(at, count):
        steps_back = lax.rem(at + count - jnp.arange(count), count)
        return steps_back ^ (steps_back >> 1)

    x_slots = slots(lax.axis_index("x"), nx)
    y_slots = slots(segment // nz, ny)
    tables = [jnp.repeat(x_slots, ny), jnp.tile(y_slots, nx)]

    def unpack(chunks, owner, biases, earlier):
        spare = [sds((ch,), F32), sds((NL, ch), F32)] if biases else []
        info = jnp.concatenate([jnp.stack([owner, segment % nz])] + tables).astype(jnp.int32)
        block = (1, 1, 1, nz, part, LANES)
        return pl.pallas_call(
            functools.partial(unpack_kernel, (in_size, conv_size, nb, nz), len(biases)),
            grid_spec=pltpu.PrefetchScalarGridSpec(
                num_scalar_prefetch=1,
                grid=(places,),
                in_specs=[
                    pl.BlockSpec(
                        block, lambda i, at: (0, at[2 + i], at[2 + places + i], 0, 0, 0)
                    ),
                    pl.BlockSpec(
                        block, lambda i, at: (1, at[2 + places + i], at[2 + i], 0, 0, 0)
                    ),
                ]
                + [pl.BlockSpec(b.shape, lambda i, at: (0, 0)) for b in biases]
                + [hbm] * len(earlier),
                out_specs=[
                    pl.BlockSpec((1, 1, nz * in_size, ch), lambda i, at: (at[0], i, 0, 0)),
                    pl.BlockSpec(
                        (NL, 1, nz * conv_size, ch // 2), lambda i, at: (0, i, 0, at[0])
                    ),
                ]
                + [pl.BlockSpec(b.shape, lambda i, at, n=len(b.shape): (0,) * n) for b in spare],
            ),
            out_shape=[
                sds((2, places, nz * in_size, ch), F32),
                sds((NL, places, nz * conv_size, ch), F32),
            ]
            + spare,
            input_output_aliases={3 + len(biases) + n: n for n in range(len(earlier))},
            compiler_params=small_params,
            cost_estimate=pl.CostEstimate(flops=0, bytes_accessed=12 * 2**20, transcendentals=0),
        )(info, chunks, chunks, *biases, *earlier)

    got = swap_core(full)
    bias_got = swap_core(bias)
    partial = unpack(full, core, [], [])
    got, bias_got = lax.optimization_barrier((got, bias_got))
    g_in, g_conv, g_b_in, g_b_conv = unpack(got, 1 - core, [bias, bias_got], partial)
    return (
        score[0, 0],
        g_in.reshape(features, ch),
        g_b_in,
        g_conv.reshape(NL, 2 * ch, ch),
        g_b_conv,
    )


def solution(mesh):
    devices = mesh.devices
    trajs, segments = devices.shape
    inner = Mesh(devices.reshape(trajs // 2, 2, segments), ("x", "c", "tm"))
    return jax.shard_map(
        per_device,
        mesh=inner,
        in_specs=(P(("x", "c"), "tm", None), P(), P(), P(), P()),
        out_specs=(P(), P(), P(), P(), P()),
        check_vma=False,
    )
```

```python
import functools

import jax
import jax.numpy as jnp
from jax import lax
from jax.experimental import pallas as pl
from jax.experimental.pallas import tpu as pltpu
from jax.sharding import Mesh, PartitionSpec as P

NL = 3
LAG = 16
RIDGE = 0.0001
HALO = 32
LANES = 128
BF = jnp.bfloat16
F32 = jnp.float32
PEERS = ("x", "tm")
HI = lax.Precision.HIGHEST
C0, C1, C2, C3, C4 = 2.25, -2.4375, 1.6875, -0.5625, 0.0625

NN = (((1,), (0,)), ((), ()))
NT = (((1,), (1,)), ((), ()))
TN = (((0,), (0,)), ((), ()))


def dot(a, b, dims=NN, precision=None):
    return lax.dot_general(a, b, dims, precision=precision, preferred_element_type=F32)


def split(a):
    hi = a.astype(BF)
    return hi, (a - hi.astype(F32)).astype(BF)


def dot3(a, b, dims=NN):
    return dot(a[0], b[0], dims) + (dot(a[0], b[1], dims) + dot(a[1], b[0], dims))


def swap_core(value):
    return lax.ppermute(value, "c", [(0, 1), (1, 0)])


def shift_segment(value, steps):
    count = lax.axis_size("tm")
    first, last = max(0, -steps), min(count, count - steps)
    return lax.ppermute(value, "tm", [(i, i + steps) for i in range(first, last)])


def shifts(count):
    return (0, 1, 3, 2) if count == 4 else tuple(range(count))


def spin(value, axis, steps):
    segments = lax.axis_size("tm")
    nz = grid_side(segments)
    ny = segments // nz
    if axis == "x":
        n = lax.axis_size("x")
        return lax.ppermute(value, "x", [(i, (i + steps) % n) for i in range(n)])
    pairs = []
    for i in range(segments):
        y, z = divmod(i, nz)
        y, z = ((y + steps) % ny, z) if axis == "y" else (y, (z + steps) % nz)
        pairs.append((i, y * nz + z))
    return lax.ppermute(value, "tm", pairs)


def grid_side(count):
    side = 1
    while (side * 2) * (side * 2) <= count:
        side *= 2
    return side


def along(value, axis, count):
    return jnp.stack([value] + [spin(value, axis, k) for k in shifts(count)[1:]])


def exchange(value):
    return lax.all_to_all(value, PEERS, 0, 0, tiled=True)


def call(kernel, outs, *args, scratch=(), vmem=16):
    specs = [
        pl.BlockSpec(memory_space=pltpu.SMEM if a.dtype == jnp.int32 else pltpu.VMEM) for a in args
    ]
    return pl.pallas_call(
        kernel,
        out_shape=outs,
        in_specs=specs,
        out_specs=[pl.BlockSpec(memory_space=pltpu.VMEM) for _ in outs],
        scratch_shapes=list(scratch),
        compiler_params=pltpu.CompilerParams(vmem_limit_bytes=vmem * 2**20),
    )(*args)


def sds(shape, dtype):
    return jax.ShapeDtypeStruct(shape, dtype)


def forward_kernel(dims, info, before, own, after, w, b, hid, sq, mine, other, means, mom):
    rows, ch, length, peers, piece = dims
    core, segment = info[0], info[1]
    ext = rows + 2 * HALO
    nb = ch // LANES
    t = segment * rows - HALO + lax.broadcasted_iota(jnp.int32, (ext, 1), 0)
    h = jnp.concatenate(
        [before[...].astype(F32), own[...].astype(F32), after[...].astype(F32)], axis=0
    )
    for layer in range(NL):
        hb = h.astype(BF)
        hid[layer] = hb
        hist = pltpu.roll(h, 2**layer, 0).astype(BF)
        s = jnp.tanh(dot(hb, w[layer, :ch]) + dot(hist, w[layer, ch:]) + b[layer : layer + 1])
        sq[layer] = s
        h = jnp.where(t >= 0, (h + s).astype(BF).astype(F32), 0.0)
    hid[NL] = h.astype(BF)
    tp = segment * rows + lax.broadcasted_iota(jnp.int32, (rows, 1), 0)
    pair = jnp.where(tp < length - LAG, 1.0, 0.0).astype(F32)
    last = segment == length // rows - 1
    count = jnp.where(last, rows - LAG, rows).astype(F32)
    early = h[HALO : HALO + rows] * pair
    later = h[HALO + LAG : HALO + LAG + rows] * pair
    mean_e = jnp.sum(early, axis=0, keepdims=True) / count
    mean_l = jnp.sum(later, axis=0, keepdims=True) / count
    means[...] = jnp.concatenate([mean_e, mean_l, jnp.zeros((6, ch), F32)], axis=0)
    ce = split((early - mean_e) * pair)
    cl = split((later - mean_l) * pair)
    left_e = jnp.concatenate([ce[0], ce[0], ce[1]], axis=0)
    left_l = jnp.concatenate([cl[0], cl[0], cl[1]], axis=0)
    right_e = jnp.concatenate([ce[0], ce[1], ce[0]], axis=0)
    right_l = jnp.concatenate([cl[0], cl[1], cl[0]], axis=0)
    mom[0] = dot(left_e, right_e, TN)
    mom[1] = dot(left_e, right_l, TN)
    mom[2] = dot(left_l, right_l, TN)
    half = ch // 2

    def pack(i, carry):
        at = pl.multiple_of(core * half + i * piece, piece)
        to = pl.multiple_of((1 - core) * half + i * piece, piece)
        for m in range(3):
            for j in range(nb):
                cols = slice(j * LANES, (j + 1) * LANES)
                put = slice(m * piece, (m + 1) * piece)
                mine[i * nb + j, put, :] = mom[m, pl.ds(at, piece), cols]
                other[i * nb + j, put, :] = mom[m, pl.ds(to, piece), cols].astype(BF)
        return carry

    lax.fori_loop(0, peers // nb, pack, 0)


def pair_kernel(dims, info, mine, got, means, sib, packed, turned):
    rows, ch, length, peers, piece = dims
    core, segment = info[0], info[1]
    nb = ch // LANES
    half = ch // 2
    last = segment == length // rows - 1
    weight = 0.5 * jnp.where(last, rows - LAG, rows).astype(F32)
    gap = means[...] - sib[...]
    mid = 0.5 * (means[...] + sib[...])
    turned[...] = gap.T * weight
    hi, lo = split(mid)
    tail = []
    for part in (hi.astype(F32), lo.astype(F32)):
        for k in range(2):
            for j in range(nb):
                tail.append(part[k : k + 1, j * LANES : (j + 1) * LANES])
    tail = jnp.concatenate(tail, axis=0).astype(BF)

    def pack(i, carry):
        at = pl.multiple_of(core * half + i * piece, piece)
        col = turned[pl.ds(at, piece), :]
        for j in range(nb):
            cols = slice(j * LANES, (j + 1) * LANES)
            p = i * nb + j
            for m, (a, c) in enumerate(((0, 0), (0, 1), (1, 1))):
                put = slice(m * piece, (m + 1) * piece)
                value = mine[p, put, :] + got[p, put, :].astype(F32)
                value = value + col[:, a : a + 1] * gap[c : c + 1, cols]
                packed[p, put, :] = value.astype(BF)
            packed[p, 3 * piece :, :] = tail
        return carry

    lax.fori_loop(0, peers // nb, pack, 0)


def merge_kernel(dims, info, arrived, cov, mean_all, flat, dev, square):
    rows, ch, length, peers, piece = dims
    core, peer = info[0], info[2]
    nb = ch // LANES
    segments = length // rows
    total = 2 * (peers // segments) * (length - LAG)
    body = 3 * piece

    def add(p, acc):
        z = arrived[p, body:, :].astype(F32)
        flat[pl.ds(pl.multiple_of(p * 2 * nb, 2 * nb), 2 * nb), :] = z[: 2 * nb] + z[2 * nb :]
        return acc + arrived[p, :body, :].astype(F32)

    within = lax.fori_loop(0, peers, add, jnp.zeros((body, LANES), F32))
    seg = lax.rem(lax.broadcasted_iota(jnp.int32, (peers, 1), 0), segments)
    counts = 2.0 * jnp.where(seg == segments - 1, rows - LAG, rows).astype(F32)
    mean_all[...] = jnp.zeros_like(mean_all)
    for k in range(2):
        for j in range(nb):
            cols = slice(j * LANES, (j + 1) * LANES)
            v = flat[pl.ds(k * nb + j, peers, stride=2 * nb), :]
            mean = jnp.sum(v * counts, axis=0, keepdims=True) / total
            mean_all[k : k + 1, cols] = mean
            dev[k, :, cols] = v - mean
    start = core * (ch // 2) + (peer // nb) * piece
    block = pl.multiple_of((start // LANES) * LANES, LANES)
    inside = pl.multiple_of(lax.rem(start, LANES), piece)
    here = pl.multiple_of(lax.rem(peer, nb) * LANES, LANES)
    for m, (a, c) in enumerate(((0, 0), (0, 1), (1, 1))):
        left = dev[a, :, pl.ds(block, LANES)] * counts
        square[m] = dot(left, dev[c, :, pl.ds(here, LANES)], TN, HI)
    between = jnp.concatenate([square[m, pl.ds(inside, piece), :] for m in range(3)], axis=0)
    value = ((within + between) / total).astype(BF)
    cov[...] = jnp.broadcast_to(value[None], cov.shape)


def step_kernel(
    dims, info, half_cov, other_cov, mean_all, hid_hbm, sq_hbm, sq0_hbm, w_hbm,
    score, mine, other, dpre, cov, grads, hid, sq, sq0, w, sems,
):
    rows, ch, length, peers, piece = dims
    core = info[0]
    nb = ch // LANES
    half = ch // 2
    loads = [
        pltpu.make_async_copy(src, dst, sems.at[n])
        for n, (src, dst) in enumerate(((hid_hbm, hid), (sq_hbm, sq), (sq0_hbm, sq0), (w_hbm, w)))
    ]
    for load in loads:
        load.start()

    def place(i, carry):
        at = pl.multiple_of(core * half + i * piece, piece)
        to = pl.multiple_of((1 - core) * half + i * piece, piece)
        for m in range(3):
            for j in range(nb):
                cols = slice(j * LANES, (j + 1) * LANES)
                put = slice(m * piece, (m + 1) * piece)
                cov[m, pl.ds(at, piece), cols] = half_cov[i * nb + j, put, :].astype(F32)
                cov[m, pl.ds(to, piece), cols] = other_cov[i * nb + j, put, :].astype(F32)
        return carry

    lax.fori_loop(0, peers // nb, place, 0)
    row = lax.broadcasted_iota(jnp.int32, (ch, ch), 0)
    col = lax.broadcasted_iota(jnp.int32, (ch, ch), 1)
    unit = jnp.where(row == col, 1.0, 0.0).astype(F32)

    def forward(matrix):
        shifted = matrix + RIDGE * unit
        square = jnp.sum(shifted * shifted, keepdims=True)
        inv_scale = lax.rsqrt(square)
        a = shifted * inv_scale
        ab = a.astype(BF)
        a2 = dot(ab, ab)
        a2b = a2.astype(BF)
        rest = C1 * a + C2 * a2 + dot(a2b, (C3 * a + C4 * a2).astype(BF))
        root = jnp.sqrt(inv_scale)
        return a, ab, a2b, rest, inv_scale, root, C0 * root, (rest * root).astype(BF)

    def backward(a, ab, a2b, rest, inv_scale, root, grad):
        poly = C0 * unit + rest
        dscale = -0.5 * jnp.sum(grad * poly, keepdims=True) * root * inv_scale
        g = grad * root
        gb = g.astype(BF)
        y = dot(gb, ab)
        x = dot(a2b, gb)
        xs = x + x.T
        h = C2 * g + (0.5 * C3) * (y + y.T) + C4 * xs
        z = dot(ab, h.astype(BF))
        da = C1 * g + (0.5 * C3) * xs + z + z.T
        dscale = dscale - jnp.sum(da * a, keepdims=True) * inv_scale
        return da * inv_scale + dscale * a

    fe = forward(cov[0])
    fl = forward(cov[2])
    alpha, re = fe[6:]
    beta, rl = fl[6:]
    c = cov[1]
    cb = c.astype(BF)
    u = alpha * c + dot(re, cb)
    ub = u.astype(BF)
    vb = (beta * c + dot(cb, rl)).astype(BF)
    k = beta * u + dot(ub, rl)
    score[...] = jnp.broadcast_to(1.0 + jnp.sum(k * k, keepdims=True), score.shape)
    k2 = 2.0 * k
    kb = k2.astype(BF)
    rk = alpha * k2 + dot(re, kb)
    gc = beta * rk + dot(rk.astype(BF), rl)
    grads[ch : 2 * ch] = gc.T.astype(BF)
    grads[2 * ch : 3 * ch] = gc.astype(BF)
    gre = dot(kb, vb, NT)
    grads[:ch] = backward(*fe[:6], gre + gre.T).astype(BF)
    grl = dot(ub, kb, TN)
    grads[3 * ch :] = backward(*fl[:6], grl + grl.T).astype(BF)
    for load in loads:
        load.wait()
    conv_backward(dims, info, hid, sq, sq0, w, grads, mean_all, mine, other, dpre)


def conv_backward(dims, info, hid, sq, sq0, w, grads, mean_all, mine, other, dpre):
    rows, ch, length, peers, piece = dims
    core, segment = info[0], info[1]
    segments = length // rows
    half = ch // 2
    nh = half // LANES
    total = 2 * (peers // segments) * (length - LAG)
    grows = rows + 16
    t = segment * rows + lax.broadcasted_iota(jnp.int32, (grows, 1), 0)
    has_early = t < length - LAG
    has_later = jnp.logical_and(t >= LAG, t < length)
    out = hid[NL].astype(F32)
    base = out[HALO : HALO + grows]
    mean_e, mean_l = mean_all[0:1], mean_all[1:2]
    zero = jnp.zeros((1, ch), F32)
    consts = []
    for early_on in (True, False):
        left_e, left_l = mean_e, mean_l
        for _ in range(3):
            top_e, top_l = left_e.astype(BF).astype(F32), left_l.astype(BF).astype(F32)
            parts = [top_e, top_l, zero, zero] if early_on else [zero, zero, top_e, top_l]
            consts.append(jnp.concatenate(parts, axis=1))
            left_e, left_l = left_e - top_e, left_l - top_l
    consts = jnp.concatenate(consts + [jnp.zeros((10, 4 * ch), F32)], axis=0)
    lhs = jnp.concatenate(
        [
            jnp.where(has_early, base, 0.0),
            jnp.where(has_early, out[HALO + LAG : HALO + LAG + grows], 0.0),
            jnp.where(has_later, out[HALO - LAG : HALO - LAG + grows], 0.0),
            jnp.where(has_later, base, 0.0),
        ],
        axis=1,
    )
    lhs = jnp.concatenate([lhs, consts], axis=0).astype(BF)
    grad = dot(lhs, grads[...])
    off_early = grad[grows : grows + 1] + grad[grows + 1 : grows + 2] + grad[grows + 2 : grows + 3]
    off_later = grad[grows + 3 : grows + 4] + grad[grows + 4 : grows + 5] + grad[grows + 5 : grows + 6]
    grad = grad[:grows] - jnp.where(has_early, off_early, 0.0) - jnp.where(has_later, off_later, 0.0)
    grad = grad / total
    biases = [None] * (NL + 1)
    first = core == 0

    def halves(value):
        lo, hi = value[:, :half], value[:, half:]
        return jnp.where(first, lo, hi), jnp.where(first, hi, lo)

    def store(left, value, p0, count, size, at):
        for part, ref in zip(halves(value), (mine, other)):
            res = dot(left, part.astype(BF), TN).astype(BF)
            for j in range(nh):
                piece_j = res[:, j * LANES : (j + 1) * LANES].reshape(count, size, LANES)
                ref[p0 : p0 + count, at + j * size : at + (j + 1) * size, :] = piece_j

    conv_size = 2 * ch // peers
    for layer in reversed(range(NL)):
        step = 2**layer
        s = sq[layer, HALO : HALO + grows, :]
        pre = jnp.where(t < length, grad * (1.0 - s * s), 0.0).astype(BF)
        own = pre[:rows].astype(F32)
        biases[layer + 1] = jnp.sum(own, axis=0, keepdims=True)
        h = hid[layer].astype(F32)
        hist = pltpu.roll(h, step, 0)[HALO : HALO + rows].astype(BF)
        at = layer * nh * conv_size
        count = ch // conv_size
        store(hid[layer, HALO : HALO + rows, :], own, 0, count, conv_size, at)
        store(hist, own, count, count, conv_size, at)
        back = dot(pre, w[layer, ch:], NT)
        grad = grad + dot(pre, w[layer, :ch], NT) + pltpu.roll(back, grows - step, 0)
    s = sq0[...]
    own = (grad[:rows] * (1.0 - s * s)).astype(BF)
    dpre[...] = own
    biases[0] = jnp.sum(own.astype(F32), axis=0, keepdims=True)
    bias = jnp.concatenate(biases, axis=0)
    for part, ref in zip(halves(bias), (mine, other)):
        hi, lo = split(part)
        tail = []
        for value in (hi.astype(F32), lo.astype(F32)):
            for j in range(nh):
                tail.append(value[:, j * LANES : (j + 1) * LANES])
        tail = jnp.concatenate(tail, axis=0).astype(BF)
        at = ref.shape[1] - tail.shape[0]
        ref[:, at:, :] = jnp.broadcast_to(tail[None], (peers,) + tail.shape)


def product_kernel(info, left, dpre, res):
    res[...] = dot(left[...], dpre[...], TN)


def pack_kernel(nbias, info, earlier, left_got, dpre_got, mine, got, packed):
    count = packed.shape[0]
    ch = dpre_got.shape[1]
    size = left_got.shape[1] // count
    res = (earlier[...] + dot(left_got[...], dpre_got[...], TN)).astype(BF)
    for j in range(ch // LANES):
        part = res[:, j * LANES : (j + 1) * LANES].reshape(count, size, LANES)
        packed[:, j * size : (j + 1) * size, :] = part
    at = size * (ch // LANES)
    body = mine.shape[1] - 2 * nbias
    value = mine[...].astype(F32) + got[...].astype(F32)
    packed[:, at : at + body, :] = value[:, :body].astype(BF)
    bias = value[0, body : body + nbias] + value[0, body + nbias :]
    hi = bias.astype(BF).astype(F32)
    tail = jnp.concatenate([hi, bias - hi], axis=0).astype(BF)
    packed[:, at + body :, :] = jnp.broadcast_to(tail[None], (count,) + tail.shape)


def sum_kernel(sizes, arrived, half_a, half_b, bias):
    in_size, conv_size, nb = sizes
    peers, wide = arrived.shape[:2]
    nh = nb // 2

    def total_of(at, count):
        def add(p, acc):
            return acc + arrived[p, at : at + count, :].astype(F32)

        return lax.fori_loop(0, peers, add, jnp.zeros((count, LANES), F32), unroll=4)

    for side, ref in enumerate((half_a, half_b)):
        count = nh * in_size
        ref[:count] = total_of(side * count, count).astype(BF)
        ch = nh // 2 * conv_size
        for layer in range(NL):
            at = nb * in_size + (layer * nh) * conv_size + side * ch
            ref[count + layer * ch : count + (layer + 1) * ch] = total_of(at, ch).astype(BF)
    nbias = bias.shape[0]
    t = total_of(wide - 2 * nbias, 2 * nbias)
    bias[...] = t[:nbias] + t[nbias:]


def unpack_kernel(sizes, nbiases, info, left, right, *refs):
    in_size, conv_size, nb, ny, nz = sizes
    z_at, y_at = info[1], info[2]
    if nbiases:
        bias, bias_got = refs[:2]
        w_in, w_conv, b_in, b_conv = refs[-4:]
    else:
        w_in, w_conv = refs[-2:]
    nh = nb // 2
    for a, shift_a in enumerate(shifts(ny)):
        y = lax.rem(y_at + ny - shift_a, ny)
        for b, shift_b in enumerate(shifts(nz)):
            z = lax.rem(z_at + nz - shift_b, nz)
            rows = pl.ds(pl.multiple_of(z * in_size, in_size), in_size)
            conv_rows = pl.ds(pl.multiple_of(z * conv_size, conv_size), conv_size)
            for side, value in enumerate((left[0, 0, a, b], right[0, a, 0, b])):
                value = value.astype(F32)
                for j in range(nh):
                    col = (side * nh + j) * LANES
                    w_in[0, y, rows, col : col + LANES] = value[j * in_size : (j + 1) * in_size]
                for layer in range(NL):
                    for j in range(nh // 2):
                        at = nh * in_size + (layer * (nh // 2) + j) * conv_size
                        col = (side * (nh // 2) + j) * LANES
                        part = value[at : at + conv_size]
                        w_conv[layer, y, conv_rows, col : col + LANES] = part
    if nbiases:

        @pl.when(pl.program_id(0) == 0)
        def _():
            first = info[0] == 1
            n = NL + 1
            parts = []
            for side in range(2):
                mine_side = first if side == 0 else jnp.logical_not(first)
                value = jnp.where(mine_side, bias[...], bias_got[...])
                parts += [value[j * n : (j + 1) * n] for j in range(nh)]
            full = jnp.concatenate(parts, axis=1)
            b_in[...] = full[0]
            b_conv[...] = full[1:]


def per_device(frames, w_in, b_in, w_conv, b_conv):
    frames = frames[0]
    rows, features = frames.shape
    ch = w_in.shape[1]
    core = lax.axis_index("c")
    segment = lax.axis_index("tm")
    segments = lax.axis_size("tm")
    peers = lax.axis_size("x") * segments
    length = rows * segments
    nb = ch // LANES
    nh = nb // 2
    piece = (ch // 2) * nb // peers
    dims = (rows, ch, length, peers, piece)
    info = jnp.stack([core, segment, lax.axis_index("x") * segments + segment]).astype(jnp.int32)
    ext = rows + 2 * HALO
    frames_got = swap_core(frames)

    squash0 = jnp.tanh(jnp.dot(frames, w_in, preferred_element_type=F32) + b_in)
    own = squash0.astype(BF)
    before = shift_segment(own[rows - HALO :], 1)
    after = shift_segment(own[:HALO], -1)
    hid, sq, mine, other, means = call(
        functools.partial(forward_kernel, dims),
        [
            sds((NL + 1, ext, ch), BF),
            sds((NL, ext, ch), F32),
            sds((peers, 3 * piece, LANES), F32),
            sds((peers, 3 * piece, LANES), BF),
            sds((8, ch), F32),
        ],
        info, before, own, after, w_conv, b_conv,
        scratch=[pltpu.VMEM((3, ch, ch), F32)],
        vmem=36,
    )
    got, sib, frames_got = lax.optimization_barrier(
        (swap_core(other), swap_core(means), frames_got)
    )
    (packed,) = call(
        functools.partial(pair_kernel, dims),
        [sds((peers, 3 * piece + 4 * nb, LANES), BF)],
        info, mine, got, means, sib,
        scratch=[pltpu.VMEM((ch, 8), F32)],
    )
    cov, mean_all = call(
        functools.partial(merge_kernel, dims),
        [sds((peers, 3 * piece, LANES), BF), sds((8, ch), F32)],
        info, exchange(packed),
        scratch=[
            pltpu.VMEM((peers * 2 * nb, LANES), F32),
            pltpu.VMEM((2, peers, ch), F32),
            pltpu.VMEM((3, LANES, LANES), F32),
        ],
    )
    cov = exchange(cov)
    half_features = features // 2
    in_size = half_features // peers
    conv_size = 2 * ch // peers
    nbias = (NL + 1) * nh
    conv_wide = NL * nh * conv_size + 2 * nbias
    body = nb * in_size + NL * nh * conv_size
    wide = body + 2 * nbias
    vmem = pl.BlockSpec(memory_space=pltpu.VMEM)
    smem = pl.BlockSpec(memory_space=pltpu.SMEM)
    hbm = pl.BlockSpec(memory_space=pl.ANY)
    params = pltpu.CompilerParams(vmem_limit_bytes=40 * 2**20)
    small_params = pltpu.CompilerParams(vmem_limit_bytes=16 * 2**20)
    score, mine, other, dpre = pl.pallas_call(
        functools.partial(step_kernel, dims),
        out_shape=[
            sds((8, LANES), F32),
            sds((peers, conv_wide, LANES), BF),
            sds((peers, conv_wide, LANES), BF),
            sds((rows, ch), BF),
        ],
        in_specs=[smem, vmem, vmem, vmem, hbm, hbm, hbm, hbm],
        out_specs=[vmem] * 4,
        scratch_shapes=[
            pltpu.VMEM((3, ch, ch), F32),
            pltpu.VMEM((4 * ch, ch), BF),
            pltpu.VMEM(hid.shape, BF),
            pltpu.VMEM(sq.shape, F32),
            pltpu.VMEM(squash0.shape, F32),
            pltpu.VMEM(w_conv.shape, BF),
            pltpu.SemaphoreType.DMA((4,)),
        ],
        compiler_params=params,
    )(info, cov, swap_core(cov), mean_all, hid, sq, squash0, w_conv)
    steps = 4
    group = peers // steps
    tile = group * in_size
    whole = pl.BlockSpec((rows, ch), lambda i, at: (0, 0))
    conv_spec = pl.BlockSpec((group, conv_wide, LANES), lambda i, at: (i, 0, 0))
    left_spec = pl.BlockSpec((rows, tile), lambda i, at: (0, at[0] * steps + i))
    res_spec = pl.BlockSpec((tile, ch), lambda i, at: (i, 0))
    dpre_got, got = swap_core(dpre), swap_core(other)
    earlier = pl.pallas_call(
        product_kernel,
        grid_spec=pltpu.PrefetchScalarGridSpec(
            num_scalar_prefetch=1,
            grid=(steps,),
            in_specs=[left_spec, whole],
            out_specs=res_spec,
        ),
        out_shape=sds((half_features, ch), F32),
        compiler_params=small_params,
        cost_estimate=pl.CostEstimate(
            flops=2 * rows * half_features * ch, bytes_accessed=6 * 2**20, transcendentals=0
        ),
    )(info, frames, dpre)
    packed = pl.pallas_call(
        functools.partial(pack_kernel, nbias),
        grid_spec=pltpu.PrefetchScalarGridSpec(
            num_scalar_prefetch=1,
            grid=(steps,),
            in_specs=[res_spec, left_spec, whole, conv_spec, conv_spec],
            out_specs=pl.BlockSpec((group, wide, LANES), lambda i, at: (i, 0, 0)),
        ),
        out_shape=sds((peers, wide, LANES), BF),
        compiler_params=small_params,
    )(info, earlier, frames_got, dpre_got, mine, got)
    nz = grid_side(segments)
    ny = segments // nz
    nx = peers // segments
    part = nh * in_size + NL * (nh // 2) * conv_size
    half_a, half_b, bias = pl.pallas_call(
        functools.partial(sum_kernel, (in_size, conv_size, nb)),
        in_specs=[vmem],
        out_specs=[vmem] * 3,
        out_shape=[sds((part, LANES), BF), sds((part, LANES), BF), sds((nbias, LANES), F32)],
        compiler_params=small_params,
    )(exchange(packed))
    both = along(jnp.stack([half_a, half_b]), "z", nz)
    plane_a, plane_b = lax.optimization_barrier(
        (along(both[:, 0], "y", ny), along(both[:, 1], "x", nx))
    )
    full = jnp.stack([along(plane_a, "x", nx), along(plane_b, "y", ny)])
    full, bias = lax.optimization_barrier((full, bias))
    places = nx * ny

    def slots(at, count):
        steps_back = lax.rem(at + count - jnp.arange(count), count)
        return steps_back ^ (steps_back >> 1)

    table = slots(lax.axis_index("x"), nx)

    def unpack(chunks, owner, biases, earlier):
        spare = [sds((ch,), F32), sds((NL, ch), F32)] if biases else []
        info = jnp.concatenate(
            [jnp.stack([owner, segment % nz, segment // nz]), table]
        ).astype(jnp.int32)
        return pl.pallas_call(
            functools.partial(unpack_kernel, (in_size, conv_size, nb, ny, nz), len(biases)),
            grid_spec=pltpu.PrefetchScalarGridSpec(
                num_scalar_prefetch=1,
                grid=(nx,),
                in_specs=[
                    pl.BlockSpec(
                        (1, 1, ny, nz, part, LANES), lambda i, at: (0, at[3 + i], 0, 0, 0, 0)
                    ),
                    pl.BlockSpec(
                        (1, ny, 1, nz, part, LANES), lambda i, at: (1, 0, at[3 + i], 0, 0, 0)
                    ),
                ]
                + [pl.BlockSpec(b.shape, lambda i, at: (0, 0)) for b in biases]
                + [hbm] * len(earlier),
                out_specs=[
                    pl.BlockSpec((1, ny, nz * in_size, ch), lambda i, at: (at[0], i, 0, 0)),
                    pl.BlockSpec(
                        (NL, ny, nz * conv_size, ch // 2), lambda i, at: (0, i, 0, at[0])
                    ),
                ]
                + [pl.BlockSpec(b.shape, lambda i, at, n=len(b.shape): (0,) * n) for b in spare],
            ),
            out_shape=[
                sds((2, places, nz * in_size, ch), F32),
                sds((NL, places, nz * conv_size, ch), F32),
            ]
            + spare,
            input_output_aliases={3 + len(biases) + n: n for n in range(len(earlier))},
            compiler_params=small_params,
            cost_estimate=pl.CostEstimate(flops=0, bytes_accessed=12 * 2**20, transcendentals=0),
        )(info, chunks, chunks, *biases, *earlier)

    got = swap_core(full)
    bias_got = swap_core(bias)
    partial = unpack(full, core, [], [])
    got, bias_got = lax.optimization_barrier((got, bias_got))
    g_in, g_conv, g_b_in, g_b_conv = unpack(got, 1 - core, [bias, bias_got], partial)
    return (
        score[0, 0],
        g_in.reshape(features, ch),
        g_b_in,
        g_conv.reshape(NL, 2 * ch, ch),
        g_b_conv,
    )


def solution(mesh):
    devices = mesh.devices
    trajs, segments = devices.shape
    inner = Mesh(devices.reshape(trajs // 2, 2, segments), ("x", "c", "tm"))
    return jax.shard_map(
        per_device,
        mesh=inner,
        in_specs=(P(("x", "c"), "tm", None), P(), P(), P(), P()),
        out_specs=(P(), P(), P(), P(), P()),
        check_vma=False,
    )
```
